32 devices in a mesh: groups: 1, ctx: 32 (over z, y, x, core).
Axes of the slice: x: 2, y: 2, z: 4, core: 2. Of those that a mesh axis runs over, the one named last changes fastest.
Arguments:
- queries: bfloat16 [8192, 2048], P(('groups', 'ctx')), may hold values from -6 to 6
- keys: bfloat16 [8192, 1024], P(('groups', 'ctx')), may hold values from -6 to 6
- values: bfloat16 [8192, 1024], P(('groups', 'ctx')), may hold values from -6 to 6
- out_grad: bfloat16 [8192, 2048], P(('groups', 'ctx')), may hold values from -96 to 96
- q_gain: float32 [128], replicated, may hold values from 0.25 to 1.75
- k_gain: float32 [128], replicated, may hold values from 0.25 to 1.75
- doc_ids: int32 [128], P(('groups', 'ctx')), may hold values from 0 to 7, never falling along the last dimension, each value on 1 to 48 neighbouring positions
Outputs:
- query_grad: bfloat16 [8192, 2048], P(('groups', 'ctx'))
- key_grad: bfloat16 [8192, 1024], P(('groups', 'ctx'))
- value_grad: bfloat16 [8192, 1024], P(('groups', 'ctx'))
The draws below stay inside these ranges and needn't reach their ends.
Inputs may be any that keep to these rules, and one draw needn't show every extreme that they name: `doc_ids`: document ids never fall along the sequence; each document covers 1 to 48 whole blocks, and one covers exactly 48.
All inputs are finite; a program needn't handle non-finite values.
Results may differ from the reference program's by a relative error of at most 0.0075.
Values may be sent and summed in bfloat16 or wider, within the bound.
No kernel may reach another device: no remote copies, remote signals or barrier semaphores. Data moves between devices by JAX's collectives and lax.ppermute only.
A program may use at most 128 MiB of HBM per device.

```python
import math
import jax
import jax.numpy as jnp
import numpy as np
from jax import lax

QH = 16
KVH = 8
HD = 128
WINDOW = 1024
BLK = 64
TOK_DEV = 256
SEQ = 8192
NB = 128
DOCS = 8
MOST_BLK = 48


def shard_levels(stream_key, dims, cuts, low, largest):
    def one(position, shards_of):
        draws = jax.random.uniform(jax.random.fold_in(jax.random.fold_in(stream_key, 6), position), (shards_of,), jnp.float32, low / len(cuts), largest / len(cuts))
        return jnp.repeat(jnp.exp(draws), dims[position] // shards_of).reshape((-1,) + (1,) * (len(dims) - position - 1))

    loudness = one(*cuts[0])
    for cut in cuts[1:]:
        loudness = loudness * one(*cut)
    return loudness


def length_profile(count, total, most, lean):
    weights = [(1 << 20) // math.isqrt(rank ** lean) + 1 for rank in range(2, count + 1)]
    rest, counts = total - most - (count - 1), [1] * (count - 1)
    while rest > 0:
        candidates = [i for i in range(count - 1) if counts[i] < most]
        pool, remaining = sum([weights[i] for i in candidates]), rest
        for i in candidates:
            extra = min(most - counts[i], max(1, remaining * weights[i] // pool), rest)
            counts[i] = counts[i] + extra
            rest = rest - extra
    return np.array([most] + counts)


def ragged_sizes(key, number_of, total, most, lean):
    if number_of == 2:
        one = jax.random.randint(key, (), max(1, total - most), min(most, total - 1) + 1)
        return jnp.stack([one, total - one])
    lengths = jnp.asarray(length_profile(number_of, total, most, lean), jnp.int32)
    twos = (number_of - 1) // 2
    giver, sink = lengths[1:1 + 2 * twos:2], lengths[2:2 + 2 * twos:2]
    room = jnp.minimum(giver - 1, most - sink)
    passed = jax.random.randint(jax.random.fold_in(key, 1), (twos,), 0, 1 << 20) % (room + 1)
    lengths = lengths.at[1:1 + 2 * twos:2].set(giver - passed).at[2:2 + 2 * twos:2].set(sink + passed)
    return lengths[jax.random.permutation(jax.random.fold_in(key, 2), number_of)]


def bell_draw(stream_key, shape, scale, most, shards=(), held_as=jnp.bfloat16):
    values = jax.random.normal(stream_key, shape, jnp.float32) * scale
    if len(shards) > 0:
        values = shard_levels(stream_key, shape, shards, -0.22, 0.18) * values
    return jnp.clip(values, min=-most, max=most).astype(held_as)


def setup_inputs(seed: int = 0, part: int = 0) -> dict:
    arg_keys = jax.random.split(jax.random.key(seed), 8)
    own_keys = jax.random.split(jax.random.fold_in(arg_keys[7], part), 8)
    queries = bell_draw(own_keys[0], (SEQ, QH * HD), 1.0, 6.0, ((0, 32),))
    keys = bell_draw(own_keys[1], (SEQ, KVH * HD), 1.0, 6.0, ((0, 32),))
    values = bell_draw(own_keys[2], (SEQ, KVH * HD), 1.0, 6.0, ((0, 32),))
    out_grad = bell_draw(own_keys[3], (SEQ, QH * HD), 16.0, 96.0, ((0, 32),))
    q_gain = jnp.clip(1.0 + 0.15 * jax.random.normal(arg_keys[4], (HD,), jnp.float32), 0.25, 1.75)
    k_gain = jnp.clip(1.0 + 0.15 * jax.random.normal(arg_keys[5], (HD,), jnp.float32), 0.25, 1.75)
    doc_ids = jnp.searchsorted(jnp.cumsum(ragged_sizes(own_keys[6], DOCS, NB, MOST_BLK, 2)), jnp.arange(NB), side="right").astype(jnp.int32)
    return dict(queries=queries, keys=keys, values=values, out_grad=out_grad, q_gain=q_gain, k_gain=k_gain, doc_ids=doc_ids)


qk_scale = 168.0 ** (-0.5)
norm_epsilon = 1e-06

def rms_norm(values_in, gain):
    inverse_rms = lax.rsqrt(lax.optimization_barrier(jnp.mean(values_in * values_in, axis=-1, keepdims=True)) + norm_epsilon)
    return (values_in * inverse_rms * gain, inverse_rms)

def rms_norm_back(values_in, inverse_rms, gain, incoming):
    scaled = incoming * gain
    cubed = inverse_rms * inverse_rms * inverse_rms
    return inverse_rms * scaled - values_in * cubed * lax.optimization_barrier(jnp.mean(values_in * scaled, axis=-1, keepdims=True))

def tile_mask(offset_rows, query_docs, key_docs, usable):
    count_rows = query_docs.shape[0]
    spacing = offset_rows + jnp.arange(count_rows, dtype=jnp.int32)[:, None] - jnp.arange(count_rows, dtype=jnp.int32)[None, :]
    return (spacing >= 0) & (spacing < WINDOW) & (query_docs[:, None] == key_docs[None, :]) & usable

def halfway_round(values_in):
    return lax.optimization_barrier(values_in.astype(jnp.bfloat16)).astype(jnp.float32)

def forward_tile(query_tile_rows, key_tile_rows, value_tile_rows, key_mask):
    score_matrix = jnp.einsum('jefo,heo->efjh', query_tile_rows.astype(jnp.float32), key_tile_rows.astype(jnp.float32))
    attention_weight = jnp.where(key_mask, jnp.exp(score_matrix), 0.0)
    totals = lax.optimization_barrier(jnp.sum(attention_weight, axis=-1))
    reduced_total = jnp.einsum('jleq,qjn->ejln', halfway_round(attention_weight), value_tile_rows.astype(jnp.float32))
    return (totals, reduced_total)

def backward_tile(query_tile_rows, key_tile_rows, value_tile_rows, gradient_tile_rows, key_mask, totals, deltas):
    score_matrix = jnp.einsum('jefo,heo->efjh', query_tile_rows.astype(jnp.float32), key_tile_rows.astype(jnp.float32))
    attention_weight = jnp.where(key_mask, jnp.exp(score_matrix), 0.0)
    probability_rows = attention_weight / totals[..., None]
    value_section = jnp.einsum('xqpt,pxqh->txh', halfway_round(probability_rows), gradient_tile_rows.astype(jnp.float32))
    probability_gradient = jnp.einsum('jefo,heo->efjh', gradient_tile_rows.astype(jnp.float32), value_tile_rows.astype(jnp.float32))
    score_gradient = halfway_round(probability_rows * (probability_gradient - deltas[..., None]))
    query_section = jnp.einsum('jleq,qjn->ejln', score_gradient, key_tile_rows.astype(jnp.float32))
    key_section = jnp.einsum('xqpt,pxqh->txh', score_gradient, query_tile_rows.astype(jnp.float32))
    return (query_section, key_section, value_section)

def reference(queries, keys, values, out_grad, q_gain, k_gain, doc_ids):
    block_rows = TOK_DEV
    reach = WINDOW // block_rows
    total_rows = queries.shape[0]
    block_count = total_rows // block_rows
    kv_heads = keys.shape[1] // HD
    group_size = queries.shape[1] // keys.shape[1]
    q_raw = queries.astype(jnp.float32).reshape(total_rows, kv_heads, group_size, HD)
    q_normed, q_inverse = rms_norm(q_raw, q_gain * qk_scale)
    q_half = q_normed.astype(jnp.bfloat16)
    k_raw = keys.astype(jnp.float32).reshape(total_rows, kv_heads, HD)
    k_normed, k_inverse = rms_norm(k_raw, k_gain)
    k_half = k_normed.astype(jnp.bfloat16)
    v_half = values.reshape(total_rows, kv_heads, HD)
    grad_half = out_grad.reshape(total_rows, kv_heads, group_size, HD)
    token_docs = jnp.repeat(doc_ids, BLK)
    padding = reach * block_rows
    k_padded = jnp.concatenate([jnp.zeros((padding, kv_heads, HD), jnp.bfloat16), k_half], axis=0)
    v_padded = jnp.concatenate([jnp.zeros((padding, kv_heads, HD), jnp.bfloat16), v_half], axis=0)
    docs_padded = jnp.concatenate([jnp.full((padding,), -1, jnp.int32), token_docs.astype(jnp.int32)], axis=0)

    def one_block(carry, block_index):
        key_acc, value_acc = carry
        start = block_index * block_rows
        query_tile_rows = lax.dynamic_slice_in_dim(q_half, start, block_rows, 0)
        gradient_tile_rows = lax.dynamic_slice_in_dim(grad_half, start, block_rows, 0)
        query_docs = lax.dynamic_slice_in_dim(token_docs, start, block_rows, 0)
        pieces = []
        for distance in range(reach + 1):
            key_start = start + (reach - distance) * block_rows
            key_tile_rows = lax.dynamic_slice_in_dim(k_padded, key_start, block_rows, 0)
            value_tile_rows = lax.dynamic_slice_in_dim(v_padded, key_start, block_rows, 0)
            key_docs = lax.dynamic_slice_in_dim(docs_padded, key_start, block_rows, 0)
            key_mask = tile_mask(distance * block_rows, query_docs, key_docs, True)
            pieces.append((key_start, key_tile_rows, value_tile_rows, key_mask))
        totals = jnp.zeros((kv_heads, group_size, block_rows), jnp.float32)
        reduced_total = jnp.zeros((block_rows, kv_heads, group_size, HD), jnp.float32)
        for key_start, key_tile_rows, value_tile_rows, key_mask in pieces:
            tile_totals, tile_summed = forward_tile(query_tile_rows, key_tile_rows, value_tile_rows, key_mask)
            totals = totals + tile_totals
            reduced_total = reduced_total + tile_summed
        outputs = reduced_total / jnp.transpose(totals, (2, 0, 1))[..., None]
        deltas = jnp.transpose(lax.optimization_barrier(jnp.sum(gradient_tile_rows.astype(jnp.float32) * outputs, axis=-1)), (1, 2, 0))
        query_acc = jnp.zeros((block_rows, kv_heads, group_size, HD), jnp.float32)
        for key_start, key_tile_rows, value_tile_rows, key_mask in pieces:
            query_section, key_section, value_section = backward_tile(query_tile_rows, key_tile_rows, value_tile_rows, gradient_tile_rows, key_mask, totals, deltas)
            query_acc = query_acc + query_section
            key_now = lax.dynamic_slice_in_dim(key_acc, key_start, block_rows, 0)
            key_acc = lax.dynamic_update_slice_in_dim(key_acc, key_now + key_section, key_start, 0)
            value_now = lax.dynamic_slice_in_dim(value_acc, key_start, block_rows, 0)
            value_acc = lax.dynamic_update_slice_in_dim(value_acc, value_now + value_section, key_start, 0)
        q_raw_block = lax.dynamic_slice_in_dim(q_raw, start, block_rows, 0)
        q_inverse_block = lax.dynamic_slice_in_dim(q_inverse, start, block_rows, 0)
        query_out = rms_norm_back(q_raw_block, q_inverse_block, q_gain * qk_scale, query_acc).astype(jnp.bfloat16)
        return ((key_acc, value_acc), query_out)
    empty = jnp.zeros((padding + total_rows, kv_heads, HD), jnp.float32)
    (key_acc, value_acc), query_blocks = lax.scan(one_block, (empty, empty), jnp.arange(block_count, dtype=jnp.int32))
    query_grad = query_blocks.reshape(total_rows, kv_heads * group_size * HD)
    key_grad = rms_norm_back(k_raw, k_inverse, k_gain, key_acc[padding:]).astype(jnp.bfloat16).reshape(total_rows, kv_heads * HD)
    value_grad = value_acc[padding:].astype(jnp.bfloat16).reshape(total_rows, kv_heads * HD)
    return (query_grad, key_grad, value_grad)
```

```python
import functools

import jax
import jax.numpy as jnp
from jax import lax
from jax.experimental import pallas as pl
from jax.experimental.pallas import tpu as pltpu
from jax.sharding import PartitionSpec as P

HD = 128
WINDOW = 1024
BLK = 64
PIECES = 2

qk_scale = 168.0 ** (-0.5)
norm_epsilon = 1e-06


def attention_kernel(
    rows, heads_block, meta, docs, q_m, g_m, q_t, g_t, kv0, kv1, kv2, q_gain, k_gain,
    dq_m, dq_t, h1, h2, own,
    k_s, kt_s, v_s, vt_s, dk_s, dv_s, qraw_s, qn_s, r_s, g_s, dq_s, e_s,
):
    f32, b16 = jnp.float32, jnp.bfloat16
    core, chip = meta[0], meta[1]
    key_tiles = WINDOW // rows + 1
    span = key_tiles * rows
    group = q_m.shape[1] // HD
    place = (core, 1 - core)

    for source, base in ((kv2, 0), (kv1, 2 * rows), (kv0, 4 * rows)):
        for part in range(2):
            off = pl.multiple_of(base + place[part] * rows, rows)
            k = source[part, 0].astype(f32)
            r = lax.rsqrt(jnp.mean(k * k, axis=-1, keepdims=True) + norm_epsilon)
            kn = k * r * k_gain[...]
            k_s[pl.ds(off, rows), :] = kn.astype(b16)
            kt_s[:, pl.ds(off, rows)] = kn.T.astype(b16)
            v = source[part, 1]
            v_s[pl.ds(off, rows), :] = v
            vt_s[:, pl.ds(off, rows)] = v.astype(f32).T.astype(b16)

    gain = q_gain[...] * qk_scale
    for part, (q_ref, g_ref) in enumerate(((q_m, g_m), (q_t, g_t))):
        slot = place[part]
        for head in range(group):
            lanes = slice(head * rows, (head + 1) * rows)
            columns = slice(head * HD, (head + 1) * HD)
            q = q_ref[..., columns].reshape(rows, HD).astype(f32).T
            r = lax.rsqrt(jnp.mean(q * q, axis=0, keepdims=True) + norm_epsilon)
            qraw_s[slot, :, lanes] = q
            r_s[slot, :, lanes] = r
            qn_s[slot, :, lanes] = (q * r * gain).astype(b16)
            g_s[slot, :, lanes] = g_ref[..., columns].reshape(rows, HD).astype(f32).T

    dk_s[...] = jnp.zeros_like(dk_s)
    dv_s[...] = jnp.zeros_like(dv_s)

    wide = group * rows
    blocks = rows // BLK
    token = lax.rem(lax.broadcasted_iota(jnp.int32, (1, wide), 1), rows)
    tile_row = lax.broadcasted_iota(jnp.int32, (rows, wide), 0)
    nt = (((1,), (1,)), ((), ()))
    for slot in range(2):
        first = jnp.zeros((1, wide), jnp.int32)
        for b in range(blocks):
            here = chip * (2 * blocks) + slot * blocks + b
            doc = docs[here]
            same = jnp.int32(0)
            for back in range(1, WINDOW // BLK + 1):
                at = here - back
                seen = (at >= 0) & (docs[jnp.maximum(at, 0)] == doc)
                same = same + seen.astype(jnp.int32)
            start = (b - same) * BLK + WINDOW
            first = jnp.where(token >= b * BLK, start, first)
        first = jnp.maximum(first, token + 1)
        qn = qn_s[slot]
        g = g_s[slot]
        total = jnp.zeros((1, wide), f32)
        out = jnp.zeros((HD, wide), f32)
        for tile in range(key_tiles):
            keys = slice((slot + tile) * rows, (slot + tile + 1) * rows)
            s = jnp.dot(k_s[keys, :], qn, preferred_element_type=f32)
            seen = tile_row >= first - tile * rows
            if tile == key_tiles - 1:
                seen = seen & (tile_row <= token)
            e = jnp.where(seen, jnp.exp(s), 0.0)
            total = total + jnp.sum(e, axis=0, keepdims=True)
            e = e.astype(b16)
            e_s[tile] = e
            out = out + jnp.dot(vt_s[:, keys], e, preferred_element_type=f32)
        inverse = 1.0 / total
        g_l = (g * inverse).astype(b16)
        delta = jnp.sum(g_l.astype(f32) * (out * inverse), axis=0, keepdims=True)
        dq = jnp.zeros((HD, wide), f32)
        for tile in range(key_tiles):
            keys = slice((slot + tile) * rows, (slot + tile + 1) * rows)
            e = e_s[tile]
            dp = jnp.dot(v_s[keys, :], g_l, preferred_element_type=f32)
            ds = (e.astype(f32) * (dp - delta)).astype(b16)
            dv_s[keys, :] += lax.dot_general(e, g_l, nt, preferred_element_type=f32)
            dk_s[keys, :] += lax.dot_general(ds, qn, nt, preferred_element_type=f32)
            dq = dq + jnp.dot(kt_s[:, keys], ds, preferred_element_type=f32)
        q = qraw_s[slot]
        r = r_s[slot]
        scaled = dq * gain
        dq = r * scaled - q * (r * r * r * jnp.mean(q * scaled, axis=0, keepdims=True))
        for head in range(group):
            lanes = slice(head * rows, (head + 1) * rows)
            columns = slice(head * HD, (head + 1) * HD)
            dq_s[slot, :, columns] = dq[:, lanes].T.astype(b16)

    dq_m[...] = dq_s[core]
    dq_t[...] = dq_s[1 - core]
    for target, base in ((h2, 0), (h1, 2 * rows), (own, 4 * rows)):
        for part in range(2):
            off = pl.multiple_of(base + place[part] * rows, rows)
            target[part, 0] = dk_s[pl.ds(off, rows), :].astype(target.dtype)
            target[part, 1] = dv_s[pl.ds(off, rows), :].astype(target.dtype)


def attention(piece, per_piece, half_heads, meta, docs, queries, out_grad, qg_t, kv0, kv1, kv2, q_gain, k_gain):
    rows = queries.shape[0]
    group_cols = queries.shape[1] // (2 * half_heads)
    group = group_cols // HD
    wide = group * rows
    key_rows = 2 * rows + WINDOW
    key_tiles = WINDOW // rows + 1
    f32, b16 = jnp.float32, jnp.bfloat16
    mine = lambda h, meta, docs: (0, meta[0] * half_heads + piece * per_piece + h)
    kv_spec = pl.BlockSpec((2, 2, rows, HD), lambda h, meta, docs: (0, 0, 0, h))
    side = lambda which: pl.BlockSpec(
        (None, rows, group_cols), lambda h, meta, docs: (which, 0, piece * per_piece + h)
    )
    whole = lambda shape: pl.BlockSpec(shape, lambda h, meta, docs: (0, 0))
    dq_spec = pl.BlockSpec((rows, group_cols), lambda h, meta, docs: (0, h))
    dq_shape = jax.ShapeDtypeStruct((rows, per_piece * group_cols), b16)
    kv_shape = (2, 2, rows, per_piece * HD)
    pairs = half_heads * group * rows * 2 * (WINDOW + rows) // (half_heads // per_piece)
    return pl.pallas_call(
        functools.partial(attention_kernel, rows, per_piece),
        grid_spec=pltpu.PrefetchScalarGridSpec(
            num_scalar_prefetch=2,
            grid=(per_piece,),
            in_specs=[
                pl.BlockSpec((rows, group_cols), mine),
                pl.BlockSpec((rows, group_cols), mine),
                side(0),
                side(1),
                kv_spec,
                kv_spec,
                kv_spec,
                whole((HD, 1)),
                whole((1, HD)),
            ],
            out_specs=[dq_spec, dq_spec, kv_spec, kv_spec, kv_spec],
            scratch_shapes=[
                pltpu.VMEM((key_rows, HD), b16),
                pltpu.VMEM((HD, key_rows), b16),
                pltpu.VMEM((key_rows, HD), b16),
                pltpu.VMEM((HD, key_rows), b16),
                pltpu.VMEM((key_rows, HD), f32),
                pltpu.VMEM((key_rows, HD), f32),
                pltpu.VMEM((2, HD, wide), f32),
                pltpu.VMEM((2, HD, wide), b16),
                pltpu.VMEM((2, 1, wide), f32),
                pltpu.VMEM((2, HD, wide), f32),
                pltpu.VMEM((2, rows, group_cols), b16),
                pltpu.VMEM((key_tiles, rows, wide), b16),
            ],
        ),
        out_shape=[
            dq_shape,
            dq_shape,
            jax.ShapeDtypeStruct(kv_shape, b16),
            jax.ShapeDtypeStruct(kv_shape, b16),
            jax.ShapeDtypeStruct(kv_shape, f32),
        ],
        compiler_params=pltpu.CompilerParams(vmem_limit_bytes=40 * 1024 * 1024),
        cost_estimate=pl.CostEstimate(
            flops=12 * pairs * HD, bytes_accessed=8 * 1024 * 1024, transcendentals=pairs
        ),
        name=f"attention_{piece}",
    )(meta, docs, queries, out_grad, qg_t, qg_t, kv0, kv1, kv2, q_gain, k_gain)


def rms_norm_back(values_in, gain, incoming):
    r = lax.rsqrt(jnp.mean(values_in * values_in, axis=-1, keepdims=True) + norm_epsilon)
    scaled = incoming * gain
    return r * scaled - values_in * (r * r * r) * jnp.mean(values_in * scaled, axis=-1, keepdims=True)


def on_device(queries, keys, values, out_grad, q_gain, k_gain, doc_ids):
    rows = queries.shape[0]
    kv_heads = keys.shape[1] // HD
    half_heads = kv_heads // 2
    per_piece = half_heads // PIECES
    count = lax.axis_size("ctx")
    if WINDOW != 4 * rows or count % 4 != 0:
        raise ValueError("unsupported split")
    rank = lax.axis_index("ctx")
    core = lax.rem(rank, 2)
    chip = lax.div(rank, 2)
    odd = lax.rem(chip, 2) == 1
    even_f = jnp.where(odd, 0.0, 1.0)
    odd_f = 1.0 - even_f

    core_swap = [(i, i ^ 1) for i in range(count)]
    x_swap = [(i, i ^ 2) for i in range(count)]
    ahead = [(i, i + 4) for i in range(count - 4)]
    back = [(i + 4, i) for i in range(count - 4)]

    docs = lax.all_gather(doc_ids, "ctx", tiled=True)
    meta = jnp.stack([core, chip]).astype(jnp.int32)

    half = half_heads * HD
    piece_cols = per_piece * HD

    def columns(array, who, width):
        return lax.dynamic_slice(array, (0, who * width), (rows, width))

    def pack(who):
        return jnp.stack([columns(keys, who, half), columns(values, who, half)])

    kv_m = pack(core)
    kv_t = lax.ppermute(pack(1 - core), "ctx", core_swap)
    q_half = queries.shape[1] // 2
    qg_t = lax.ppermute(
        jnp.stack([columns(queries, 1 - core, q_half), columns(out_grad, 1 - core, q_half)]),
        "ctx",
        core_swap,
    )
    kv0, kv1, kv2 = [], [], []
    for piece in range(PIECES):
        cols = slice(piece * piece_cols, (piece + 1) * piece_cols)
        kv0.append(jnp.stack([kv_m[:, :, cols], kv_t[:, :, cols]]))
    for piece in range(PIECES):
        kv2.append(lax.ppermute(kv0[piece], "ctx", ahead))
    for piece in range(PIECES):
        kv1.append(lax.ppermute(jnp.where(odd, kv2[piece], kv0[piece]), "ctx", x_swap))

    q_gain_col = q_gain.reshape(HD, 1)
    k_gain_row = k_gain.reshape(1, HD)
    results = []
    for piece in range(PIECES):
        results.append(
            attention(
                piece, per_piece, half_heads, meta, docs, queries, out_grad, qg_t,
                kv0[piece], kv1[piece], kv2[piece], q_gain_col, k_gain_row,
            )
        )
    swapped = [lax.ppermute(results[piece][2], "ctx", x_swap) for piece in range(PIECES)]
    returned = []
    for piece in range(PIECES):
        joined = results[piece][3].astype(jnp.float32) + odd_f * swapped[piece].astype(jnp.float32)
        returned.append(lax.ppermute(joined.astype(jnp.bfloat16), "ctx", back))

    finals = []
    for piece in range(PIECES):
        total = (
            results[piece][4]
            + even_f * swapped[piece].astype(jnp.float32)
            + returned[piece].astype(jnp.float32)
        )
        raw = kv0[piece][:, 0].astype(jnp.float32).reshape(2, rows, per_piece, HD)
        dk = rms_norm_back(raw, k_gain, total[:, 0].reshape(2, rows, per_piece, HD))
        dk = dk.reshape(2, rows, piece_cols)
        finals.append(jnp.stack([dk, total[:, 1]], axis=1).astype(jnp.bfloat16))
    final = jnp.concatenate(finals, axis=-1)

    def join(mine, theirs):
        return jnp.where(
            core == 0,
            jnp.concatenate([mine, theirs], axis=-1),
            jnp.concatenate([theirs, mine], axis=-1),
        )

    dq_m = jnp.concatenate([r[0] for r in results], axis=-1)
    dq_t = lax.ppermute(jnp.concatenate([r[1] for r in results], axis=-1), "ctx", core_swap)
    query_grad = join(dq_m, dq_t)
    kv_back = lax.ppermute(final[1], "ctx", core_swap)
    key_grad = join(final[0, 0], kv_back[0])
    value_grad = join(final[0, 1], kv_back[1])
    return (query_grad, key_grad, value_grad)


def solution(mesh):
    split = P(("groups", "ctx"), None)
    in_specs = (split, split, split, split, P(), P(), P(("groups", "ctx")))
    return jax.shard_map(
        on_device, mesh=mesh, in_specs=in_specs, out_specs=(split, split, split), check_vma=False
    )
```

```python
import functools

import jax
import jax.numpy as jnp
from jax import lax
from jax.experimental import pallas as pl
from jax.experimental.pallas import tpu as pltpu
from jax.sharding import PartitionSpec as P

HD = 128
WINDOW = 1024
BLK = 64
PIECES = 4
VMEM_LIMIT = 56 * 1024 * 1024

qk_scale = 168.0 ** (-0.5)
norm_epsilon = 1e-06


def attention_kernel(
    rows, meta, q_m, g_m, q_t, g_t, kv0, kv1, kv2, q_gain, k_gain,
    dq_m, dq_t, h1, h2, own,
    k_s, kt_s, v_s, vt_s, dk_s, dv_s, qraw_s, qn_s, r_s, g_s, dq_s, e_s,
):
    f32, b16 = jnp.float32, jnp.bfloat16
    core = meta[0]
    key_tiles = WINDOW // rows + 1
    group = q_m.shape[1] // HD
    wide = group * rows
    blocks = rows // BLK
    place = (core, 1 - core)

    for source, base in ((kv2, 0), (kv1, 2 * rows), (kv0, 4 * rows)):
        for part in range(2):
            off = pl.multiple_of(base + place[part] * rows, rows)
            k = source[part, :rows].astype(f32)
            r = lax.rsqrt(jnp.mean(k * k, axis=-1, keepdims=True) + norm_epsilon)
            kn = k * r * k_gain[...]
            k_s[pl.ds(off, rows), :] = kn.astype(b16)
            kt_s[:, pl.ds(off, rows)] = kn.T.astype(b16)
            v = source[part, rows : 2 * rows]
            v_s[pl.ds(off, rows), :] = v
            vt_s[:, pl.ds(off, rows)] = v.astype(f32).T.astype(b16)

    gain = q_gain[...] * qk_scale
    for part, (q_ref, g_ref) in enumerate(((q_m, g_m), (q_t, g_t))):
        slot = place[part]
        for head in range(group):
            lanes = slice(head * rows, (head + 1) * rows)
            columns = slice(head * HD, (head + 1) * HD)
            q = q_ref[:, columns].astype(f32).T
            r = lax.rsqrt(jnp.mean(q * q, axis=0, keepdims=True) + norm_epsilon)
            qraw_s[slot, :, lanes] = q
            r_s[slot, :, lanes] = r
            qn_s[slot, :, lanes] = (q * r * gain).astype(b16)
            g_s[slot, :, lanes] = g_ref[:, columns].astype(f32).T

    dk_s[...] = jnp.zeros_like(dk_s)
    dv_s[...] = jnp.zeros_like(dv_s)

    token = lax.rem(lax.broadcasted_iota(jnp.int32, (1, wide), 1), rows)
    tile_row = lax.broadcasted_iota(jnp.int32, (rows, wide), 0)
    nt = (((1,), (1,)), ((), ()))
    ids = [
        [source[part, 2 * rows :, :1].astype(f32)[b : b + 1] for b in range(blocks)]
        for source in (kv2, kv1, kv0)
        for part in range(2)
    ]
    for slot in range(2):
        doc = jnp.zeros((1, wide), f32)
        for b in range(blocks):
            here = jnp.where(core == slot, ids[4][b], ids[5][b])
            doc = jnp.where(token >= b * BLK, here, doc)
        earlier = jnp.zeros((1, wide), f32)
        for tokens in ids:
            for one in tokens:
                earlier = earlier + (one < doc).astype(f32)
        first = earlier.astype(jnp.int32) * BLK - slot * rows
        first = jnp.maximum(first, token + 1)
        qn = qn_s[slot]
        g = g_s[slot]
        total = jnp.zeros((1, wide), f32)
        out = jnp.zeros((HD, wide), f32)
        for tile in range(key_tiles):
            keys = slice((slot + tile) * rows, (slot + tile + 1) * rows)
            s = jnp.dot(k_s[keys, :], qn, preferred_element_type=f32)
            seen = tile_row >= first - tile * rows
            if tile == key_tiles - 1:
                seen = seen & (tile_row <= token)
            e = jnp.where(seen, jnp.exp(s), 0.0)
            total = total + jnp.sum(e, axis=0, keepdims=True)
            e = e.astype(b16)
            e_s[tile] = e
            out = out + jnp.dot(vt_s[:, keys], e, preferred_element_type=f32)
        inverse = 1.0 / total
        g_l = (g * inverse).astype(b16)
        delta = jnp.sum(g_l.astype(f32) * (out * inverse), axis=0, keepdims=True)
        dq = jnp.zeros((HD, wide), f32)
        for tile in range(key_tiles):
            keys = slice((slot + tile) * rows, (slot + tile + 1) * rows)
            e = e_s[tile]
            dp = jnp.dot(v_s[keys, :], g_l, preferred_element_type=f32)
            ds = (e.astype(f32) * (dp - delta)).astype(b16)
            dv_s[keys, :] += lax.dot_general(e, g_l, nt, preferred_element_type=f32)
            dk_s[keys, :] += lax.dot_general(ds, qn, nt, preferred_element_type=f32)
            dq = dq + jnp.dot(kt_s[:, keys], ds, preferred_element_type=f32)
        q = qraw_s[slot]
        r = r_s[slot]
        scaled = dq * gain
        dq = r * scaled - q * (r * r * r * jnp.mean(q * scaled, axis=0, keepdims=True))
        for head in range(group):
            lanes = slice(head * rows, (head + 1) * rows)
            columns = slice(head * HD, (head + 1) * HD)
            dq_s[slot, :, columns] = dq[:, lanes].T.astype(b16)

    dq_m[...] = dq_s[core]
    dq_t[...] = dq_s[1 - core]
    for target, base in ((h2, 0), (h1, 2 * rows), (own, 4 * rows)):
        for part in range(2):
            off = pl.multiple_of(base + place[part] * rows, rows)
            target[part, :rows] = dk_s[pl.ds(off, rows), :].astype(target.dtype)
            target[part, rows:] = dv_s[pl.ds(off, rows), :].astype(target.dtype)


def attention(piece, half_heads, meta, queries, out_grad, qg_t, kv0, kv1, kv2, q_gain, k_gain):
    rows = queries.shape[0]
    group_cols = queries.shape[1] // (2 * half_heads)
    group = group_cols // HD
    per_piece = kv0.shape[2] // HD
    wide = group * rows
    key_rows = 2 * rows + WINDOW
    key_tiles = WINDOW // rows + 1
    f32, b16 = jnp.float32, jnp.bfloat16
    mine = pl.BlockSpec(
        (rows, group_cols), lambda h, meta: (0, meta[0] * half_heads + piece * per_piece + h)
    )
    kv_in = pl.BlockSpec((2, kv0.shape[1], HD), lambda h, meta: (0, 0, h))
    kv_out = pl.BlockSpec((2, 2 * rows, HD), lambda h, meta: (0, 0, h))
    side = lambda which: pl.BlockSpec(
        (None, rows, group_cols), lambda h, meta: (which, 0, piece * per_piece + h)
    )
    whole = lambda shape: pl.BlockSpec(shape, lambda h, meta: (0, 0))
    dq_spec = pl.BlockSpec((rows, group_cols), lambda h, meta: (0, h))
    dq_shape = jax.ShapeDtypeStruct((rows, per_piece * group_cols), b16)
    kv_shape = (2, 2 * rows, per_piece * HD)
    pairs = per_piece * group * 2 * rows * (WINDOW + rows)
    return pl.pallas_call(
        functools.partial(attention_kernel, rows),
        grid_spec=pltpu.PrefetchScalarGridSpec(
            num_scalar_prefetch=1,
            grid=(per_piece,),
            in_specs=[
                mine, mine, side(0), side(1), kv_in, kv_in, kv_in, whole((HD, 1)), whole((1, HD)),
            ],
            out_specs=[dq_spec, dq_spec, kv_out, kv_out, kv_out],
            scratch_shapes=[
                pltpu.VMEM((key_rows, HD), b16),
                pltpu.VMEM((HD, key_rows), b16),
                pltpu.VMEM((key_rows, HD), b16),
                pltpu.VMEM((HD, key_rows), b16),
                pltpu.VMEM((key_rows, HD), f32),
                pltpu.VMEM((key_rows, HD), f32),
                pltpu.VMEM((2, HD, wide), f32),
                pltpu.VMEM((2, HD, wide), b16),
                pltpu.VMEM((2, 1, wide), f32),
                pltpu.VMEM((2, HD, wide), f32),
                pltpu.VMEM((2, rows, group_cols), b16),
                pltpu.VMEM((key_tiles, rows, wide), b16),
            ],
        ),
        out_shape=[
            dq_shape,
            dq_shape,
            jax.ShapeDtypeStruct(kv_shape, b16),
            jax.ShapeDtypeStruct(kv_shape, b16),
            jax.ShapeDtypeStruct(kv_shape, f32),
        ],
        compiler_params=pltpu.CompilerParams(vmem_limit_bytes=VMEM_LIMIT),
        cost_estimate=pl.CostEstimate(
            flops=12 * pairs * HD, bytes_accessed=4 * 1024 * 1024, transcendentals=pairs
        ),
        name=f"attention_{piece}",
    )(meta, queries, out_grad, qg_t, qg_t, kv0, kv1, kv2, q_gain, k_gain)


def finish_kernel(rows, meta, own, swapped, returned, kv0, k_gain, out):
    f32 = jnp.float32
    even = meta[1] == 0
    for part in range(2):
        for which in range(2):
            at = slice(which * rows, (which + 1) * rows)
            total = own[part, at] + returned[part, at].astype(f32)
            total = total + jnp.where(even, swapped[part, at].astype(f32), 0.0)
            if which == 0:
                for head in range(total.shape[1] // HD):
                    cols = slice(head * HD, (head + 1) * HD)
                    k = kv0[part, :rows, cols].astype(f32)
                    r = lax.rsqrt(jnp.mean(k * k, axis=-1, keepdims=True) + norm_epsilon)
                    scaled = total[:, cols] * k_gain[...]
                    grad = r * scaled - k * (r * r * r * jnp.mean(k * scaled, axis=-1, keepdims=True))
                    out[part, at, cols] = grad.astype(out.dtype)
            else:
                out[part, at] = total.astype(out.dtype)


def finish(piece, meta, own, swapped, returned, kv0, k_gain):
    rows = own.shape[1] // 2
    vmem = pl.BlockSpec(memory_space=pltpu.VMEM)
    return pl.pallas_call(
        functools.partial(finish_kernel, rows),
        in_specs=[pl.BlockSpec(memory_space=pltpu.SMEM)] + [vmem] * 5,
        out_specs=vmem,
        out_shape=jax.ShapeDtypeStruct(own.shape, jnp.bfloat16),
        cost_estimate=pl.CostEstimate(
            flops=16 * own.size, bytes_accessed=12 * own.size, transcendentals=0
        ),
        name=f"finish_{piece}",
    )(meta, own, swapped, returned, kv0, k_gain)


def on_device(queries, keys, values, out_grad, q_gain, k_gain, doc_ids):
    f32, b16 = jnp.float32, jnp.bfloat16
    rows = queries.shape[0]
    kv_heads = keys.shape[1] // HD
    half_heads = kv_heads // 2
    per_piece = half_heads // PIECES
    count = lax.axis_size("ctx")
    if WINDOW != 4 * rows or count % 4 != 0:
        raise ValueError("unsupported split")
    rank = lax.axis_index("ctx")
    core = lax.rem(rank, 2)
    parity = lax.rem(lax.div(rank, 2), 2)
    odd = parity == 1
    meta = jnp.stack([core, parity]).astype(jnp.int32)

    core_swap = [(i, i ^ 1) for i in range(count)]
    x_swap = [(i, i ^ 2) for i in range(count)]
    ahead = [(i, i + 4) for i in range(count - 4)]
    back = [(i + 4, i) for i in range(count - 4)]

    half = half_heads * HD
    piece_cols = per_piece * HD
    id_rows = jnp.pad((doc_ids + 1).astype(b16), (0, 16 - doc_ids.shape[0]))
    id_rows = jnp.broadcast_to(id_rows[:, None], (16, half))

    def columns(array, who, width):
        return lax.dynamic_slice(array, (0, who * width), (rows, width))

    def pack(who):
        return jnp.concatenate([columns(keys, who, half), columns(values, who, half), id_rows])

    kv_m = pack(core)
    kv_t = lax.ppermute(pack(1 - core), "ctx", core_swap)
    q_half = queries.shape[1] // 2
    qg_t = lax.ppermute(
        jnp.stack([columns(queries, 1 - core, q_half), columns(out_grad, 1 - core, q_half)]),
        "ctx",
        core_swap,
    )
    kv0, kv1, kv2 = [], [], []
    for piece in range(PIECES):
        cols = slice(piece * piece_cols, (piece + 1) * piece_cols)
        kv0.append(jnp.stack([kv_m[:, cols], kv_t[:, cols]]))
    for piece in range(PIECES):
        kv2.append(lax.ppermute(kv0[piece], "ctx", ahead))
    for piece in range(PIECES):
        kv1.append(lax.ppermute(jnp.where(odd, kv2[piece], kv0[piece]), "ctx", x_swap))

    q_gain_col = q_gain.reshape(HD, 1)
    k_gain_row = k_gain.reshape(1, HD)
    dq_m, dq_t, final = [], [], []
    for piece in range(PIECES):
        mine, theirs, h1, h2, own = attention(
            piece, half_heads, meta, queries, out_grad, qg_t,
            kv0[piece], kv1[piece], kv2[piece], q_gain_col, k_gain_row,
        )
        dq_m.append(mine)
        dq_t.append(theirs)
        swapped = lax.ppermute(h1, "ctx", x_swap)
        joined = h2.astype(f32) + jnp.where(odd, swapped.astype(f32), 0.0)
        returned = lax.ppermute(joined.astype(b16), "ctx", back)
        final.append(finish(piece, meta, own, swapped, returned, kv0[piece], k_gain_row))

    def join(mine, theirs):
        return jnp.where(
            core == 0,
            jnp.concatenate(mine + theirs, axis=-1),
            jnp.concatenate(theirs + mine, axis=-1),
        )

    dq_back = lax.ppermute(jnp.concatenate(dq_t, axis=-1), "ctx", core_swap)
    query_grad = join(dq_m, [dq_back])
    kv_back = [lax.ppermute(one[1], "ctx", core_swap) for one in final]
    key_grad = join([one[0, :rows] for one in final], [one[:rows] for one in kv_back])
    value_grad = join([one[0, rows:] for one in final], [one[rows:] for one in kv_back])
    return (query_grad, key_grad, value_grad)


def solution(mesh):
    split = P(("groups", "ctx"), None)
    in_specs = (split, split, split, split, P(), P(), P(("groups", "ctx")))
    return jax.shard_map(
        on_device, mesh=mesh, in_specs=in_specs, out_specs=(split, split, split), check_vma=False
    )
```

```python
import functools

import jax
import jax.numpy as jnp
from jax import lax
from jax.experimental import pallas as pl
from jax.experimental.pallas import tpu as pltpu
from jax.sharding import PartitionSpec as P

HD = 128
WINDOW = 1024
BLK = 64
ID_ROWS = 16
VMEM_LIMIT = 32 * 1024 * 1024

qk_scale = 168.0 ** (-0.5)
norm_epsilon = 1e-06


def inverse_rms(values_in, axis):
    return lax.rsqrt(jnp.mean(values_in * values_in, axis=axis, keepdims=True) + norm_epsilon)


def pack_kernel(rows, meta, ids, k_m, v_m, k_o, v_o, mine, other):
    spread = lax.broadcasted_iota(jnp.int32, (ID_ROWS, mine.shape[1]), 0)
    id_rows = jnp.zeros(spread.shape, jnp.float32)
    for b in range(rows // BLK):
        id_rows = jnp.where(spread == b, (ids[b] + 1).astype(jnp.float32), id_rows)
    for target, k, v in ((mine, k_m, v_m), (other, k_o, v_o)):
        target[:rows] = k[...]
        target[rows : 2 * rows] = v[...]
        target[2 * rows :] = id_rows.astype(target.dtype)


def pack(meta, ids, keys, values):
    rows, columns = keys.shape
    half = columns // 2
    mine = pl.BlockSpec((rows, half), lambda i, meta, ids: (0, meta[0]))
    other = pl.BlockSpec((rows, half), lambda i, meta, ids: (0, 1 - meta[0]))
    out = jax.ShapeDtypeStruct((2 * rows + ID_ROWS, half), keys.dtype)
    out_spec = pl.BlockSpec(out.shape, lambda i, meta, ids: (0, 0))

    def body(meta, ids, *refs):
        pack_kernel(rows, meta, ids, *refs)

    return pl.pallas_call(
        body,
        grid_spec=pltpu.PrefetchScalarGridSpec(
            num_scalar_prefetch=2,
            grid=(1,),
            in_specs=[mine, mine, other, other],
            out_specs=[out_spec, out_spec],
        ),
        out_shape=[out, out],
        name="pack",
    )(meta, ids, keys, values, keys, values)


def ready_kernel(rows, meta, q_m, g_m, q_t, g_t, kv0, k_gain, qt, gt, k_own, kt_own, vt_own):
    f32, b16 = jnp.float32, jnp.bfloat16
    core = meta[0]
    place = (core, 1 - core)
    for part, (q_ref, g_ref) in enumerate(((q_m, g_m), (q_t, g_t))):
        slot = place[part]
        for head in range(q_m.shape[1] // HD):
            lanes = slice(head * rows, (head + 1) * rows)
            columns = slice(head * HD, (head + 1) * HD)
            qt[slot, :, lanes] = q_ref[:, columns].T
            gt[slot, :, lanes] = g_ref[:, columns].T
    for part in range(2):
        k = kv0[part, :rows].astype(f32)
        kn = (k * inverse_rms(k, -1) * k_gain[...]).astype(b16)
        k_own[place[part]] = kn
        kt_own[place[part]] = kn.T
        vt_own[place[part]] = kv0[part, rows : 2 * rows].T


def ready(meta, queries, out_grad, qg_t, kv0, k_gain):
    rows = queries.shape[0]
    heads = kv0.shape[2] // HD
    group_cols = queries.shape[1] // (2 * heads)
    wide = group_cols // HD * rows
    mine = pl.BlockSpec((rows, group_cols), lambda h, meta: (0, meta[0] * heads + h))
    side = lambda which: pl.BlockSpec((None, rows, group_cols), lambda h, meta: (which, 0, h))
    out = lambda *shape: (
        pl.BlockSpec((None,) + shape, lambda h, meta: (h,) + (0,) * len(shape)),
        jax.ShapeDtypeStruct((heads,) + shape, queries.dtype),
    )
    outs = [
        out(2, HD, wide), out(2, HD, wide), out(2, rows, HD), out(2, HD, rows), out(2, HD, rows),
    ]
    return pl.pallas_call(
        functools.partial(ready_kernel, rows),
        grid_spec=pltpu.PrefetchScalarGridSpec(
            num_scalar_prefetch=1,
            grid=(heads,),
            in_specs=[
                mine, mine, side(0), side(1),
                pl.BlockSpec((2, kv0.shape[1], HD), lambda h, meta: (0, 0, h)),
                pl.BlockSpec((1, HD), lambda h, meta: (0, 0)),
            ],
            out_specs=[one[0] for one in outs],
        ),
        out_shape=[one[1] for one in outs],
        compiler_params=pltpu.CompilerParams(vmem_limit_bytes=VMEM_LIMIT),
        cost_estimate=pl.CostEstimate(
            flops=2**30, bytes_accessed=8 * 1024 * 1024, transcendentals=0
        ),
        name="ready",
    )(meta, queries, out_grad, qg_t, qg_t, kv0, k_gain)


def attention_kernel(
    piece, rows, meta, qt, gt, k_own, kt_own, vt_own, kv0, kv1, kv2, q_gain, k_gain,
    dq_m, dq_t, h1, h2, own,
    k_s, kt_s, v_s, vt_s, dk_s, dv_s, dq_s, e_s,
):
    f32, b16 = jnp.float32, jnp.bfloat16
    core = meta[0]
    key_tiles = WINDOW // rows + 1
    wide = qt.shape[-1]
    group = wide // rows
    blocks = rows // BLK
    place = (core, 1 - core)

    for source, base in ((kv2, 0), (kv1, 2)):
        for part in range(2):
            at = base + place[part]
            k = source[part, :rows].astype(f32)
            kn = (k * inverse_rms(k, -1) * k_gain[...]).astype(b16)
            k_s[at] = kn
            kt_s[at] = kn.T
            v = source[part, rows : 2 * rows]
            v_s[at] = v
            vt_s[at] = v.T
    for part in range(2):
        v_s[4 + place[part]] = kv0[part, rows : 2 * rows]

    def key_tile(at):
        if at < 4:
            return k_s[at], kt_s[at], vt_s[at]
        return k_own[piece, at - 4], kt_own[piece, at - 4], vt_own[piece, at - 4]

    dk_s[...] = jnp.zeros_like(dk_s)
    dv_s[...] = jnp.zeros_like(dv_s)

    gain = jnp.broadcast_to(q_gain[...], (HD, HD)).T * qk_scale
    gain = jnp.concatenate([gain] * (wide // HD), axis=1)
    token = lax.rem(lax.broadcasted_iota(jnp.int32, (1, wide), 1), rows)
    tile_row = lax.broadcasted_iota(jnp.int32, (rows, wide), 0)
    nt = (((1,), (1,)), ((), ()))
    ids = [
        [source[part, 2 * rows :, :1].astype(f32)[b : b + 1] for b in range(blocks)]
        for source in (kv2, kv1, kv0)
        for part in range(2)
    ]
    for slot in range(2):
        doc = jnp.zeros((1, wide), f32)
        for b in range(blocks):
            here = jnp.where(core == slot, ids[4][b], ids[5][b])
            doc = jnp.where(token >= b * BLK, here, doc)
        earlier = jnp.zeros((1, wide), f32)
        for tokens in ids:
            for one in tokens:
                earlier = earlier + (one < doc).astype(f32)
        first = earlier.astype(jnp.int32) * BLK - slot * rows
        first = jnp.maximum(first, token + 1)
        q = qt[piece, slot].astype(f32)
        r = inverse_rms(q, 0)
        qn = (q * r * gain).astype(b16)
        total = jnp.zeros((1, wide), f32)
        out = jnp.zeros((HD, wide), f32)
        for tile in range(key_tiles):
            k, kt, vt = key_tile(slot + tile)
            s = jnp.dot(k, qn, preferred_element_type=f32)
            seen = tile_row >= first - tile * rows
            if tile == key_tiles - 1:
                seen = seen & (tile_row <= token)
            e = jnp.where(seen, jnp.exp(s), 0.0)
            total = total + jnp.sum(e, axis=0, keepdims=True)
            e = e.astype(b16)
            e_s[tile] = e
            out = out + jnp.dot(vt, e, preferred_element_type=f32)
        inverse = 1.0 / total
        g_l = (gt[piece, slot].astype(f32) * inverse).astype(b16)
        delta = jnp.sum(g_l.astype(f32) * (out * inverse), axis=0, keepdims=True)
        dq = jnp.zeros((HD, wide), f32)
        for tile in range(key_tiles):
            k, kt, vt = key_tile(slot + tile)
            e = e_s[tile]
            dp = jnp.dot(v_s[slot + tile], g_l, preferred_element_type=f32)
            ds = (e.astype(f32) * (dp - delta)).astype(b16)
            dv_s[slot + tile] += lax.dot_general(e, g_l, nt, preferred_element_type=f32)
            dk_s[slot + tile] += lax.dot_general(ds, qn, nt, preferred_element_type=f32)
            dq = dq + jnp.dot(kt, ds, preferred_element_type=f32)
        scaled = dq * gain
        dq = r * scaled - q * (r * r * r * jnp.mean(q * scaled, axis=0, keepdims=True))
        for head in range(group):
            lanes = slice(head * rows, (head + 1) * rows)
            columns = slice(head * HD, (head + 1) * HD)
            dq_s[slot, :, columns] = dq[:, lanes].T.astype(b16)

    dq_m[...] = dq_s[core]
    dq_t[...] = dq_s[1 - core]
    for target, base in ((h2, 0), (h1, 2), (own, 4)):
        for part in range(2):
            target[part, :rows] = dk_s[base + place[part]].astype(target.dtype)
            target[part, rows:] = dv_s[base + place[part]].astype(target.dtype)


def attention(piece, meta, prepared, kv0, kv1, kv2, q_gain, k_gain):
    rows = prepared[2].shape[2]
    wide = prepared[0].shape[-1]
    group_cols = wide // rows * HD
    key_blocks = WINDOW // rows + 2
    key_tiles = key_blocks - 1
    f32, b16 = jnp.float32, jnp.bfloat16
    vmem = pl.BlockSpec(memory_space=pltpu.VMEM)
    pairs = 2 * wide * (WINDOW + rows)
    kv_shape = (2, 2 * rows, HD)
    return pl.pallas_call(
        functools.partial(attention_kernel, piece, rows),
        in_specs=[pl.BlockSpec(memory_space=pltpu.SMEM)] + [vmem] * 10,
        out_specs=[vmem] * 5,
        scratch_shapes=[
            pltpu.VMEM((key_blocks - 2, rows, HD), b16),
            pltpu.VMEM((key_blocks - 2, HD, rows), b16),
            pltpu.VMEM((key_blocks, rows, HD), b16),
            pltpu.VMEM((key_blocks - 2, HD, rows), b16),
            pltpu.VMEM((key_blocks, rows, HD), f32),
            pltpu.VMEM((key_blocks, rows, HD), f32),
            pltpu.VMEM((2, rows, group_cols), b16),
            pltpu.VMEM((key_tiles, rows, wide), b16),
        ],
        out_shape=[
            jax.ShapeDtypeStruct((rows, group_cols), b16),
            jax.ShapeDtypeStruct((rows, group_cols), b16),
            jax.ShapeDtypeStruct(kv_shape, b16),
            jax.ShapeDtypeStruct(kv_shape, b16),
            jax.ShapeDtypeStruct(kv_shape, f32),
        ],
        compiler_params=pltpu.CompilerParams(vmem_limit_bytes=VMEM_LIMIT),
        cost_estimate=pl.CostEstimate(
            flops=48 * pairs * HD, bytes_accessed=4 * 1024 * 1024, transcendentals=pairs
        ),
        name=f"attention_{piece}",
    )(meta, *prepared, kv0, kv1, kv2, q_gain, k_gain)


def finish_kernel(rows, count, meta, k_gain, *refs):
    f32 = jnp.float32
    even = meta[1] == 0
    outs = refs[4 * count :]
    for piece in range(count):
        own, swapped, returned, kv0 = refs[4 * piece : 4 * piece + 4]
        columns = slice(piece * HD, (piece + 1) * HD)
        for part in range(2):
            total = own[part] + returned[part].astype(f32)
            total = total + jnp.where(even, swapped[part].astype(f32), 0.0)
            k = kv0[part, :rows].astype(f32)
            r = inverse_rms(k, -1)
            scaled = total[:rows] * k_gain[...]
            grad = r * scaled - k * (r * r * r * jnp.mean(k * scaled, axis=-1, keepdims=True))
            outs[part][:rows, columns] = grad.astype(outs[part].dtype)
            outs[part][rows:, columns] = total[rows:].astype(outs[part].dtype)


def finish(name, meta, k_gain, pieces):
    rows = pieces[0][0].shape[1] // 2
    vmem = pl.BlockSpec(memory_space=pltpu.VMEM)
    shape = jax.ShapeDtypeStruct((2 * rows, len(pieces) * HD), jnp.bfloat16)
    flat = [one for piece in pieces for one in piece]
    return pl.pallas_call(
        functools.partial(finish_kernel, rows, len(pieces)),
        in_specs=[pl.BlockSpec(memory_space=pltpu.SMEM)] + [vmem] * (1 + len(flat)),
        out_specs=[vmem, vmem],
        out_shape=[shape, shape],
        compiler_params=pltpu.CompilerParams(vmem_limit_bytes=VMEM_LIMIT),
        cost_estimate=pl.CostEstimate(
            flops=2**28 * len(pieces), bytes_accessed=2**21 * len(pieces), transcendentals=0
        ),
        name=name,
    )(meta, k_gain, *flat)


def after(value, *others):
    return lax.optimization_barrier((value,) + others)[0]


def on_device(queries, keys, values, out_grad, q_gain, k_gain, doc_ids):
    f32, b16 = jnp.float32, jnp.bfloat16
    rows = queries.shape[0]
    half = keys.shape[1] // 2
    pieces = half // HD
    count = lax.axis_size("ctx")
    if WINDOW != 4 * rows or count % 4 != 0:
        raise ValueError("unsupported split")
    rank = lax.axis_index("ctx")
    core = lax.rem(rank, 2)
    parity = lax.rem(lax.div(rank, 2), 2)
    odd = parity == 1
    meta = jnp.stack([core, parity]).astype(jnp.int32)

    core_swap = [(i, i ^ 1) for i in range(count)]
    x_swap = [(i, i ^ 2) for i in range(count)]
    ahead = [(i, i + 4) for i in range(count - 4)]
    back = [(i + 4, i) for i in range(count - 4)]

    kv_m, kv_o = pack(meta, doc_ids, keys, values)
    kv_t = lax.ppermute(kv_o, "ctx", core_swap)
    q_half = queries.shape[1] // 2
    other_half = lambda array: lax.dynamic_slice(array, (0, (1 - core) * q_half), (rows, q_half))
    qg_t = lax.ppermute(
        jnp.stack([other_half(queries), other_half(out_grad)]), "ctx", core_swap
    )
    kv0, kv1, kv2 = [], [], []
    for piece in range(pieces):
        cols = slice(piece * HD, (piece + 1) * HD)
        kv0.append(jnp.stack([kv_m[:, cols], kv_t[:, cols]]))
        kv2.append(lax.ppermute(kv0[piece], "ctx", ahead))
    for piece in range(pieces):
        kv1.append(lax.ppermute(jnp.where(odd, kv2[piece], kv0[piece]), "ctx", x_swap))

    q_gain_row = q_gain.reshape(1, HD)
    k_gain_row = k_gain.reshape(1, HD)
    prepared = ready(meta, queries, out_grad, qg_t, jnp.stack([kv_m, kv_t]), k_gain_row)
    dq_m, dq_t, sums, joined = [], [], [], []
    order = meta
    for piece in range(pieces):
        if piece >= 2:
            order = after(order, joined[piece - 2])
        mine, theirs, h1, h2, own = attention(
            piece, order, prepared, kv0[piece], kv1[piece], kv2[piece], q_gain_row, k_gain_row
        )
        dq_m.append(mine)
        dq_t.append(theirs)
        swapped = lax.ppermute(h1, "ctx", x_swap)
        order = after(order, own)
        join_sum = h2.astype(f32) + jnp.where(odd, swapped.astype(f32), 0.0)
        joined.append(join_sum.astype(b16))
        returned = lax.ppermute(joined[piece], "ctx", back)
        sums.append((own, swapped, returned, kv0[piece]))

    def join(mine, theirs):
        return jnp.where(
            core == 0,
            jnp.concatenate(mine + theirs, axis=-1),
            jnp.concatenate(theirs + mine, axis=-1),
        )

    dq_back = lax.ppermute(jnp.concatenate(dq_t, axis=-1), "ctx", core_swap)
    query_grad = join(dq_m, [dq_back])
    final_m, final_t = [], []
    for name, group in (("finish_first", sums[:-1]), ("finish_last", sums[-1:])):
        mine, theirs = finish(name, meta, k_gain_row, group)
        final_m.append(mine)
        final_t.append(lax.ppermute(theirs, "ctx", core_swap))
    key_grad = join([one[:rows] for one in final_m], [one[:rows] for one in final_t])
    value_grad = join([one[rows:] for one in final_m], [one[rows:] for one in final_t])
    return (query_grad, key_grad, value_grad)


def solution(mesh):
    split = P(("groups", "ctx"), None)
    in_specs = (split, split, split, split, P(), P(), P(("groups", "ctx")))
    return jax.shard_map(
        on_device, mesh=mesh, in_specs=in_specs, out_specs=(split, split, split), check_vma=False
    )
```

```python
import functools

import jax
import jax.numpy as jnp
from jax import lax
from jax.experimental import pallas as pl
from jax.experimental.pallas import tpu as pltpu
from jax.sharding import PartitionSpec as P

HD = 128
WINDOW = 1024
BLK = 64
ID_ROWS = 16
VMEM_LIMIT = 32 * 1024 * 1024
SMALL = pl.CostEstimate(flops=2**20, bytes_accessed=2**16, transcendentals=0)

qk_scale = 168.0 ** (-0.5)
norm_epsilon = 1e-06


def inverse_rms(values_in, axis):
    return lax.rsqrt(jnp.mean(values_in * values_in, axis=axis, keepdims=True) + norm_epsilon)


def pack_kernel(rows, half, ids, keys, values, queries, out_grad, mine, other, qg_other, sem):
    core = lax.rem(lax.axis_index("ctx"), 2)
    copies = []
    for target, who in ((mine, core), (other, 1 - core)):
        for head in range(half // HD):
            columns = pl.ds(pl.multiple_of(who * half + head * HD, HD), HD)
            for at, source in enumerate((keys, values)):
                copies.append(
                    pltpu.make_async_copy(
                        source.at[:, columns],
                        target.at[head, pl.ds(at * rows, rows)],
                        sem.at[len(copies)],
                    )
                )
    q_half = qg_other.shape[-1]
    columns = pl.ds(pl.multiple_of((1 - core) * q_half, q_half), q_half)
    for at, source in enumerate((queries, out_grad)):
        copies.append(
            pltpu.make_async_copy(source.at[:, columns], qg_other.at[at], sem.at[len(copies)])
        )
    for copy in copies:
        copy.start()
    spread = lax.broadcasted_iota(jnp.int32, (ID_ROWS, HD), 0)
    id_rows = jnp.zeros(spread.shape, jnp.float32)
    for b in range(rows // BLK):
        id_rows = jnp.where(spread == b, (ids[b] + 1).astype(jnp.float32), id_rows)
    for target in (mine, other):
        for head in range(half // HD):
            target[head, 2 * rows :] = id_rows.astype(target.dtype)
    for copy in copies:
        copy.wait()


def pack(ids, keys, values, queries, out_grad):
    rows, columns = keys.shape
    half = columns // 2
    out = jax.ShapeDtypeStruct((half // HD, 2 * rows + ID_ROWS, HD), keys.dtype)
    vmem = pl.BlockSpec(memory_space=pltpu.VMEM)
    hbm = pl.BlockSpec(memory_space=pltpu.HBM)
    return pl.pallas_call(
        functools.partial(pack_kernel, rows, half),
        in_specs=[pl.BlockSpec(memory_space=pltpu.SMEM), hbm, hbm, hbm, hbm],
        out_specs=[vmem, vmem, vmem],
        out_shape=[
            out, out, jax.ShapeDtypeStruct((2, rows, queries.shape[1] // 2), queries.dtype),
        ],
        scratch_shapes=[pltpu.SemaphoreType.DMA((4 * (half // HD) + 2,))],
        name="pack",
    )(ids, keys, values, queries, out_grad)


def local_kernel(
    rows, meta, q_m, g_m, q_t, g_t, kv_m, kv_t, q_gain, k_gain,
    qt, qn, gt, k_own, kt_own, v_own, e_own, total_own, out_own, doc_own,
):
    f32, b16 = jnp.float32, jnp.bfloat16
    core = meta[0]
    place = (core, 1 - core)
    wide = qt.shape[-1]
    blocks = rows // BLK
    gain = jnp.broadcast_to(q_gain[...], (HD, HD)).T * qk_scale
    gain = jnp.concatenate([gain] * (wide // HD), axis=1)
    for part, (q_ref, g_ref, kv) in enumerate(((q_m, g_m, kv_m), (q_t, g_t, kv_t))):
        slot = place[part]
        for head in range(q_m.shape[1] // HD):
            lanes = slice(head * rows, (head + 1) * rows)
            columns = slice(head * HD, (head + 1) * HD)
            qt[slot, :, lanes] = q_ref[:, columns].T
            gt[slot, :, lanes] = g_ref[:, columns].T
        k = kv[:rows].astype(f32)
        kn = (k * inverse_rms(k, -1) * k_gain[...]).astype(b16)
        k_own[slot] = kn
        kt_own[slot] = kn.T
        v_own[slot] = kv[rows : 2 * rows]
    token = lax.rem(lax.broadcasted_iota(jnp.int32, (1, wide), 1), rows)
    tile_row = lax.broadcasted_iota(jnp.int32, (rows, wide), 0)
    ids = [[kv[2 * rows :, :1].astype(f32)[b : b + 1] for b in range(blocks)] for kv in (kv_m, kv_t)]
    for slot in range(2):
        doc = jnp.zeros((1, wide), f32)
        for b in range(blocks):
            here = jnp.where(core == slot, ids[0][b], ids[1][b])
            doc = jnp.where(token >= b * BLK, here, doc)
        doc_own[slot] = doc
        earlier = jnp.zeros((1, wide), f32)
        for one in ids[0] + ids[1]:
            earlier = earlier + (one < doc).astype(f32)
        first = earlier.astype(jnp.int32) * BLK
        q = qt[slot].astype(f32)
        qn_slot = (q * inverse_rms(q, 0) * gain).astype(b16)
        qn[slot] = qn_slot
        total = jnp.zeros((1, wide), f32)
        out = jnp.zeros((HD, wide), f32)
        for tile in range(slot + 1):
            s = jnp.dot(k_own[tile], qn_slot, preferred_element_type=f32)
            seen = tile_row >= first - tile * rows
            if tile == slot:
                seen = seen & (tile_row <= token)
            e = jnp.where(seen, jnp.exp(s), 0.0)
            total = total + jnp.sum(e, axis=0, keepdims=True)
            e = e.astype(b16)
            e_own[slot + tile] = e
            out = out + jnp.dot(v_own[tile].T, e, preferred_element_type=f32)
        total_own[slot] = total
        out_own[slot] = out


def local(meta, queries, out_grad, qg_t, kv_m, kv_t, q_gain, k_gain):
    f32, b16 = jnp.float32, jnp.bfloat16
    rows = queries.shape[0]
    heads = kv_m.shape[0]
    group_cols = queries.shape[1] // (2 * heads)
    wide = group_cols // HD * rows
    mine = pl.BlockSpec((rows, group_cols), lambda h, meta: (0, meta[0] * heads + h))
    side = lambda which: pl.BlockSpec((None, rows, group_cols), lambda h, meta: (which, 0, h))
    own_kv = pl.BlockSpec((None,) + kv_m.shape[1:], lambda h, meta: (h, 0, 0))
    row = pl.BlockSpec((1, HD), lambda h, meta: (0, 0))
    out = lambda dtype, *shape: (
        pl.BlockSpec((None,) + shape, lambda h, meta: (h,) + (0,) * len(shape)),
        jax.ShapeDtypeStruct((heads,) + shape, dtype),
    )
    outs = [
        out(b16, 2, HD, wide), out(b16, 2, HD, wide), out(b16, 2, HD, wide),
        out(b16, 2, rows, HD), out(b16, 2, HD, rows), out(b16, 2, rows, HD),
        out(b16, 3, rows, wide), out(f32, 2, 1, wide), out(f32, 2, HD, wide),
        out(f32, 2, 1, wide),
    ]
    return pl.pallas_call(
        functools.partial(local_kernel, rows),
        grid_spec=pltpu.PrefetchScalarGridSpec(
            num_scalar_prefetch=1,
            grid=(heads,),
            in_specs=[mine, mine, side(0), side(1), own_kv, own_kv, row, row],
            out_specs=[one[0] for one in outs],
        ),
        out_shape=[one[1] for one in outs],
        compiler_params=pltpu.CompilerParams(vmem_limit_bytes=VMEM_LIMIT),
        cost_estimate=SMALL,
        name="local",
    )(meta, queries, out_grad, qg_t, qg_t, kv_m, kv_t, q_gain, k_gain)


def halo_kernel(
    piece, rows, meta, qn, gt, total_own, out_own, doc_own, kv1, kv2, k_gain,
    h1, h2, g_out, delta_out, dq_out,
    k_s, kt_s, v_s, vt_s, dk_s, dv_s, e_s,
):
    f32, b16 = jnp.float32, jnp.bfloat16
    core = meta[0]
    tiles = WINDOW // rows
    wide = qn.shape[-1]
    blocks = rows // BLK
    place = (core, 1 - core)

    for source, base in ((kv2, 0), (kv1, 2)):
        for part in range(2):
            at = base + place[part]
            k = source[part, :rows].astype(f32)
            kn = (k * inverse_rms(k, -1) * k_gain[...]).astype(b16)
            k_s[at] = kn
            kt_s[at] = kn.T
            v = source[part, rows : 2 * rows]
            v_s[at] = v
            vt_s[at] = v.T

    token = lax.rem(lax.broadcasted_iota(jnp.int32, (1, wide), 1), rows)
    tile_row = lax.broadcasted_iota(jnp.int32, (rows, wide), 0)
    nt = (((1,), (1,)), ((), ()))
    ids = [
        source[part, 2 * rows :, :1].astype(f32)[b : b + 1]
        for source in (kv2, kv1)
        for part in range(2)
        for b in range(blocks)
    ]
    for slot in range(2):
        doc = doc_own[piece, slot]
        earlier = jnp.zeros((1, wide), f32)
        for one in ids:
            earlier = earlier + (one < doc).astype(f32)
        first = jnp.maximum(earlier.astype(jnp.int32) * BLK, token + (slot * rows + 1))
        qn_slot = qn[piece, slot]
        total = total_own[piece, slot]
        out = out_own[piece, slot]
        for tile in range(slot, tiles):
            s = jnp.dot(k_s[tile], qn_slot, preferred_element_type=f32)
            e = jnp.where(tile_row >= first - tile * rows, jnp.exp(s), 0.0)
            total = total + jnp.sum(e, axis=0, keepdims=True)
            e = e.astype(b16)
            e_s[tile] = e
            out = out + jnp.dot(vt_s[tile], e, preferred_element_type=f32)
        inverse = 1.0 / total
        g_l = (gt[piece, slot].astype(f32) * inverse).astype(b16)
        delta = jnp.sum(g_l.astype(f32) * (out * inverse), axis=0, keepdims=True)
        g_out[slot] = g_l
        delta_out[slot] = delta
        dq = jnp.zeros((HD, wide), f32)
        for tile in range(slot, tiles):
            e = e_s[tile]
            dp = jnp.dot(v_s[tile], g_l, preferred_element_type=f32)
            ds = (e.astype(f32) * (dp - delta)).astype(b16)
            dv = lax.dot_general(e, g_l, nt, preferred_element_type=f32)
            dk = lax.dot_general(ds, qn_slot, nt, preferred_element_type=f32)
            dv_s[tile] = dv if slot == 0 else dv_s[tile] + dv
            dk_s[tile] = dk if slot == 0 else dk_s[tile] + dk
            dq = dq + jnp.dot(kt_s[tile], ds, preferred_element_type=f32)
        dq_out[slot] = dq

    for target, base in ((h2, 0), (h1, 2)):
        for part in range(2):
            target[part, :rows] = dk_s[base + place[part]].astype(b16)
            target[part, rows:] = dv_s[base + place[part]].astype(b16)


def halo(piece, meta, qn, gt, total_own, out_own, doc_own, kv1, kv2, k_gain):
    rows = (kv1.shape[1] - ID_ROWS) // 2
    wide = qn.shape[-1]
    tiles = WINDOW // rows
    f32, b16 = jnp.float32, jnp.bfloat16
    vmem = pl.BlockSpec(memory_space=pltpu.VMEM)
    pairs = 2 * wide * WINDOW
    return pl.pallas_call(
        functools.partial(halo_kernel, piece, rows),
        in_specs=[pl.BlockSpec(memory_space=pltpu.SMEM)] + [vmem] * 8,
        out_specs=[vmem] * 5,
        scratch_shapes=[
            pltpu.VMEM((tiles, rows, HD), b16),
            pltpu.VMEM((tiles, HD, rows), b16),
            pltpu.VMEM((tiles, rows, HD), b16),
            pltpu.VMEM((tiles, HD, rows), b16),
            pltpu.VMEM((tiles, rows, HD), f32),
            pltpu.VMEM((tiles, rows, HD), f32),
            pltpu.VMEM((tiles, rows, wide), b16),
        ],
        out_shape=[
            jax.ShapeDtypeStruct((2, 2 * rows, HD), b16),
            jax.ShapeDtypeStruct((2, 2 * rows, HD), b16),
            jax.ShapeDtypeStruct((2, HD, wide), b16),
            jax.ShapeDtypeStruct((2, 1, wide), f32),
            jax.ShapeDtypeStruct((2, HD, wide), f32),
        ],
        compiler_params=pltpu.CompilerParams(vmem_limit_bytes=VMEM_LIMIT),
        cost_estimate=SMALL,
        name=f"halo_{piece}",
    )(meta, qn, gt, total_own, out_own, doc_own, kv1, kv2, k_gain)


def own_kernel(pieces, rows, meta, q_gain, qt, qn, k_own, kt_own, v_own, e_own, *refs):
    f32, b16 = jnp.float32, jnp.bfloat16
    core = meta[0]
    count = len(pieces)
    inputs, (dq_m, dq_t), owns, (dq_s,) = (
        refs[: 3 * count], refs[3 * count : 3 * count + 2],
        refs[3 * count + 2 : 4 * count + 2], refs[4 * count + 2 :],
    )
    wide = qt.shape[-1]
    group = wide // rows
    nt = (((1,), (1,)), ((), ()))
    gain = jnp.broadcast_to(q_gain[...], (HD, HD)).T * qk_scale
    gain = jnp.concatenate([gain] * (wide // HD), axis=1)
    for at, piece in enumerate(pieces):
        g_l, delta, dq_in = inputs[3 * at : 3 * at + 3]
        dk, dv = [0.0, 0.0], [0.0, 0.0]
        for slot in range(2):
            dq = dq_in[slot]
            for tile in range(slot + 1):
                e = e_own[piece, slot + tile]
                dp = jnp.dot(v_own[piece, tile], g_l[slot], preferred_element_type=f32)
                ds = (e.astype(f32) * (dp - delta[slot])).astype(b16)
                dv[tile] += lax.dot_general(e, g_l[slot], nt, preferred_element_type=f32)
                dk[tile] += lax.dot_general(ds, qn[piece, slot], nt, preferred_element_type=f32)
                dq = dq + jnp.dot(kt_own[piece, tile], ds, preferred_element_type=f32)
            q = qt[piece, slot].astype(f32)
            r = inverse_rms(q, 0)
            scaled = dq * gain
            dq = r * scaled - q * (r * r * r * jnp.mean(q * scaled, axis=0, keepdims=True))
            for head in range(group):
                lanes = slice(head * rows, (head + 1) * rows)
                columns = slice((at * group + head) * HD, (at * group + head + 1) * HD)
                dq_s[slot, :, columns] = dq[:, lanes].T.astype(b16)
        for tile in range(2):
            part = lax.rem(tile + core, 2)
            owns[at][part, :rows] = dk[tile]
            owns[at][part, rows:] = dv[tile]
    dq_m[...] = dq_s[core]
    dq_t[...] = dq_s[1 - core]


def own_keys(pieces, meta, q_gain, qt, qn, k_own, kt_own, v_own, e_own, results):
    rows = k_own.shape[2]
    wide = qt.shape[-1]
    columns = len(pieces) * (wide // rows) * HD
    vmem = pl.BlockSpec(memory_space=pltpu.VMEM)
    dq = jax.ShapeDtypeStruct((rows, columns), jnp.bfloat16)
    own = jax.ShapeDtypeStruct((2, 2 * rows, HD), jnp.float32)
    flat = [one for piece in pieces for one in results[piece]]
    out = pl.pallas_call(
        functools.partial(own_kernel, tuple(pieces), rows),
        in_specs=[pl.BlockSpec(memory_space=pltpu.SMEM)] + [vmem] * (7 + len(flat)),
        out_specs=[vmem] * (2 + len(pieces)),
        scratch_shapes=[pltpu.VMEM((2, rows, columns), jnp.bfloat16)],
        out_shape=[dq, dq] + [own] * len(pieces),
        compiler_params=pltpu.CompilerParams(vmem_limit_bytes=VMEM_LIMIT),
        cost_estimate=SMALL,
        name=f"own_{pieces[0]}",
    )(meta, q_gain, qt, qn, k_own, kt_own, v_own, e_own, *flat)
    return out[0], out[1], out[2:]


def finish_kernel(rows, count, meta, k_gain, *refs):
    f32 = jnp.float32
    even = meta[1] == 0
    outs = refs[4 * count :]
    for piece in range(count):
        own, swapped, returned, kv0 = refs[4 * piece : 4 * piece + 4]
        columns = slice(piece * HD, (piece + 1) * HD)
        for part in range(2):
            total = own[part] + returned[part].astype(f32)
            total = total + jnp.where(even, swapped[part].astype(f32), 0.0)
            k = kv0[part, :rows].astype(f32)
            r = inverse_rms(k, -1)
            scaled = total[:rows] * k_gain[...]
            grad = r * scaled - k * (r * r * r * jnp.mean(k * scaled, axis=-1, keepdims=True))
            outs[part][:rows, columns] = grad.astype(outs[part].dtype)
            outs[part][rows:, columns] = total[rows:].astype(outs[part].dtype)


def finish(name, meta, k_gain, pieces):
    rows = pieces[0][0].shape[1] // 2
    vmem = pl.BlockSpec(memory_space=pltpu.VMEM)
    shape = jax.ShapeDtypeStruct((2 * rows, len(pieces) * HD), jnp.bfloat16)
    flat = [one for piece in pieces for one in piece]
    return pl.pallas_call(
        functools.partial(finish_kernel, rows, len(pieces)),
        in_specs=[pl.BlockSpec(memory_space=pltpu.SMEM)] + [vmem] * (1 + len(flat)),
        out_specs=[vmem, vmem],
        out_shape=[shape, shape],
        compiler_params=pltpu.CompilerParams(vmem_limit_bytes=VMEM_LIMIT),
        cost_estimate=SMALL,
        name=name,
    )(meta, k_gain, *flat)


def after(value, *others):
    return lax.optimization_barrier((value,) + others)[0]


def on_device(queries, keys, values, out_grad, q_gain, k_gain, doc_ids):
    f32, b16 = jnp.float32, jnp.bfloat16
    rows = queries.shape[0]
    half = keys.shape[1] // 2
    pieces = half // HD
    count = lax.axis_size("ctx")
    if WINDOW != 4 * rows or count % 4 != 0:
        raise ValueError("unsupported split")
    rank = lax.axis_index("ctx")
    core = lax.rem(rank, 2)
    parity = lax.rem(lax.div(rank, 2), 2)
    odd = parity == 1
    meta = jnp.stack([core, parity]).astype(jnp.int32)

    core_swap = [(i, i ^ 1) for i in range(count)]
    x_swap = [(i, i ^ 2) for i in range(count)]
    ahead = [(i, i + 4) for i in range(count - 4)]
    back = [(i + 4, i) for i in range(count - 4)]

    kv_m, kv_o, qg_o = pack(doc_ids, keys, values, queries, out_grad)
    kv_t = lax.ppermute(kv_o, "ctx", core_swap)
    qg_t = lax.ppermute(qg_o, "ctx", core_swap)
    kv0, kv1, kv2 = [], [], []
    for piece in range(pieces):
        kv0.append(jnp.stack([kv_m[piece], kv_t[piece]]))
        kv2.append(lax.ppermute(kv0[piece], "ctx", ahead))
    q_gain_row = q_gain.reshape(1, HD)
    k_gain_row = k_gain.reshape(1, HD)
    qt, qn, gt, k_own, kt_own, v_own, e_own, total_own, out_own, doc_own = local(
        meta, queries, out_grad, qg_t, kv_m, kv_t, q_gain_row, k_gain_row
    )
    swapped, joined, returned, results, sums_h2 = [], [], [], [], []
    order = meta

    def x_hop(piece, turn):
        operand = jnp.where(turn, kv2[piece], kv0[piece])
        kv1.append(lax.ppermute(operand, "ctx", x_swap))
        return operand

    def send_back(piece, turn):
        arrived = jnp.where(turn, swapped[piece].astype(f32), 0.0)
        joined.append((sums_h2[piece].astype(f32) + arrived).astype(b16))
        returned.append(lax.ppermute(joined[piece], "ctx", back))

    order = after(order, x_hop(1, after(odd, x_hop(0, odd))))
    for piece in range(pieces):
        if piece >= 2:
            order = after(order, joined[piece - 2])
        if piece >= 3:
            order = after(order, returned[piece - 3])
        h1, h2, *result = halo(
            piece, order, qn, gt, total_own, out_own, doc_own, kv1[piece], kv2[piece], k_gain_row
        )
        results.append(result)
        order = after(order, result[1])
        if piece + 2 < pieces:
            order = after(order, x_hop(piece + 2, after(odd, result[1])))
        swapped.append(lax.ppermute(h1, "ctx", x_swap))
        sums_h2.append(h2)
        if piece >= 1:
            send_back(piece - 1, after(odd, result[1]))

    def own_part(group, order):
        return own_keys(
            list(group), order, q_gain_row, qt, qn, k_own, kt_own, v_own, e_own, results
        )

    order = after(order, joined[-1], returned[-2])
    dq_m_first, dq_t_first, own_first = own_part(range(pieces // 2), order)
    send_back(pieces - 1, after(odd, dq_m_first))
    order = after(order, joined[-1], returned[-2])
    dq_m_last, dq_t_last, own_last = own_part(range(pieces // 2, pieces), order)
    dq_m, dq_t, own = [dq_m_first, dq_m_last], [dq_t_first, dq_t_last], [*own_first, *own_last]
    sums = [(own[i], swapped[i], returned[i], kv0[i]) for i in range(pieces)]

    def join(mine, theirs, first):
        return jnp.where(
            first == 0,
            jnp.concatenate(mine + theirs, axis=-1),
            jnp.concatenate(theirs + mine, axis=-1),
        )

    dq_back = [lax.ppermute(one, "ctx", core_swap) for one in dq_t]
    final_m, final_t = [], []
    for name, group in (("finish_first", sums[:-1]), ("finish_last", sums[-1:])):
        mine, theirs = finish(name, order, k_gain_row, group)
        order = after(order, mine)
        final_m.append(mine)
        final_t.append(lax.ppermute(theirs, "ctx", core_swap))
    query_grad = join(dq_m, dq_back, after(core, final_m[-1]))
    key_grad = join([one[:rows] for one in final_m], [one[:rows] for one in final_t], core)
    value_grad = join([one[rows:] for one in final_m], [one[rows:] for one in final_t], core)
    return (query_grad, key_grad, value_grad)


def solution(mesh):
    split = P(("groups", "ctx"), None)
    in_specs = (split, split, split, split, P(), P(), P(("groups", "ctx")))
    return jax.shard_map(
        on_device, mesh=mesh, in_specs=in_specs, out_specs=(split, split, split), check_vma=False
    )
```

```python
import functools

import jax
import jax.numpy as jnp
from jax import lax
from jax.experimental import pallas as pl
from jax.experimental.pallas import tpu as pltpu
from jax.sharding import PartitionSpec as P

HD = 128
WINDOW = 1024
BLK = 64
ID_ROWS = 16
VMEM_LIMIT = 16 * 1024 * 1024
HIDDEN = -1e30
SMALL = pl.CostEstimate(flops=2**20, bytes_accessed=2**16, transcendentals=0)

qk_scale = 168.0 ** (-0.5)
norm_epsilon = 1e-06


def inverse_rms(values_in, axis):
    return lax.rsqrt(jnp.mean(values_in * values_in, axis=axis, keepdims=True) + norm_epsilon)


def pack_kernel(rows, half, ids, keys, values, queries, out_grad, mine, other, qg_other, sem):
    core = lax.rem(lax.axis_index("ctx"), 2)
    copies = []
    for target, who in ((mine, core), (other, 1 - core)):
        for head in range(half // HD):
            columns = pl.ds(pl.multiple_of(who * half + head * HD, HD), HD)
            for at, source in enumerate((keys, values)):
                copies.append(
                    pltpu.make_async_copy(
                        source.at[:, columns],
                        target.at[head, pl.ds(at * rows, rows)],
                        sem.at[len(copies)],
                    )
                )
    q_half = qg_other.shape[-1]
    columns = pl.ds(pl.multiple_of((1 - core) * q_half, q_half), q_half)
    for at, source in enumerate((queries, out_grad)):
        copies.append(
            pltpu.make_async_copy(source.at[:, columns], qg_other.at[at], sem.at[len(copies)])
        )
    for copy in copies:
        copy.start()
    spread = lax.broadcasted_iota(jnp.int32, (ID_ROWS, HD), 0)
    id_rows = jnp.zeros(spread.shape, jnp.float32)
    for b in range(rows // BLK):
        id_rows = jnp.where(spread == b, (ids[b] + 1).astype(jnp.float32), id_rows)
    for target in (mine, other):
        for head in range(half // HD):
            target[head, 2 * rows :] = id_rows.astype(target.dtype)
    for copy in copies:
        copy.wait()


def pack(ids, keys, values, queries, out_grad):
    rows, columns = keys.shape
    half = columns // 2
    out = jax.ShapeDtypeStruct((half // HD, 2 * rows + ID_ROWS, HD), keys.dtype)
    vmem = pl.BlockSpec(memory_space=pltpu.VMEM)
    hbm = pl.BlockSpec(memory_space=pltpu.HBM)
    return pl.pallas_call(
        functools.partial(pack_kernel, rows, half),
        in_specs=[pl.BlockSpec(memory_space=pltpu.SMEM), hbm, hbm, hbm, hbm],
        out_specs=[vmem, vmem, vmem],
        out_shape=[
            out, out, jax.ShapeDtypeStruct((2, rows, queries.shape[1] // 2), queries.dtype),
        ],
        scratch_shapes=[pltpu.SemaphoreType.DMA((4 * (half // HD) + 2,))],
        compiler_params=pltpu.CompilerParams(vmem_limit_bytes=VMEM_LIMIT),
        name="pack",
    )(ids, keys, values, queries, out_grad)


def weights(scores, first, diagonal, token, e_ref, base):
    total = jnp.zeros((8, scores.shape[1]), jnp.float32)
    key = lax.broadcasted_iota(jnp.int32, (BLK, scores.shape[1]), 0)
    for at in range(0, scores.shape[0], BLK):
        block = scores[at : at + BLK] + jnp.where(first <= at, 0.0, HIDDEN)
        if diagonal == "window" and at < HD:
            block = jnp.where(key + at > token, block, HIDDEN)
        if diagonal == "causal" and at >= scores.shape[0] - HD:
            block = jnp.where(key + (at - scores.shape[0] + HD) <= token, block, HIDDEN)
        e = jnp.exp(block)
        total = total + jnp.sum(e.reshape(BLK // 8, 8, scores.shape[1]), axis=0)
        e_ref[base + at : base + at + BLK, :] = e.astype(e_ref.dtype)
    return jnp.sum(total, axis=0, keepdims=True)


def local_kernel(
    rows, meta, q_m, g_m, q_t, g_t, kv_m, kv_t, q_gain, k_gain,
    qt, qn, gt, k_own, kt_own, v_own, e_own, total_own, out_own, doc_own,
):
    f32, b16 = jnp.float32, jnp.bfloat16
    core = meta[0]
    wide = qt.shape[-1]
    blocks = rows // BLK
    runs = rows // HD
    gain = jnp.broadcast_to(q_gain[...], (HD, HD)).T * qk_scale
    gain = jnp.concatenate([gain] * (wide // HD), axis=1)
    for part, (q_ref, g_ref, kv) in enumerate(((q_m, g_m, kv_m), (q_t, g_t, kv_t))):
        slot = core if part == 0 else 1 - core
        for head in range(q_m.shape[1] // HD):
            columns = slice(head * HD, (head + 1) * HD)
            q, g = q_ref[:, columns].T, g_ref[:, columns].T
            for run in range(runs):
                tokens = slice(run * HD, (run + 1) * HD)
                qt[slot * runs + run, :, columns] = q[:, tokens]
                gt[slot * runs + run, :, columns] = g[:, tokens]
        off = pl.multiple_of(slot * rows, rows)
        k = kv[:rows].astype(f32)
        kn = (k * inverse_rms(k, -1) * k_gain[...]).astype(b16)
        k_own[pl.ds(off, rows), :] = kn
        kt_own[:, pl.ds(off, rows)] = kn.T
        v_own[pl.ds(off, rows), :] = kv[rows : 2 * rows]
    token = lax.rem(lax.broadcasted_iota(jnp.int32, (1, wide), 1), HD)
    ids = [[kv[2 * rows :, :1].astype(f32)[b : b + 1] for b in range(blocks)] for kv in (kv_m, kv_t)]
    base = 0
    for run in range(2 * runs):
        slot, inside = divmod(run * HD, rows)
        doc = jnp.zeros((1, wide), f32)
        for b in range(HD // BLK):
            at = inside // BLK + b
            here = jnp.where(core == slot, ids[0][at], ids[1][at])
            doc = jnp.where(token >= b * BLK, here, doc)
        doc_own[run] = doc
        earlier = jnp.zeros((1, wide), f32)
        for one in ids[0] + ids[1]:
            earlier = earlier + (one < doc).astype(f32)
        first = earlier.astype(jnp.int32) * BLK
        q = qt[run].astype(f32)
        qn_run = (q * inverse_rms(q, 0) * gain).astype(b16)
        qn[run] = qn_run
        count = (run + 1) * HD
        s = jnp.dot(k_own[:count, :], qn_run, preferred_element_type=f32)
        total_own[run] = weights(s, first, "causal", token, e_own, base)
        vt = v_own[:count, :].T
        out_own[run] = jnp.dot(vt, e_own[base : base + count, :], preferred_element_type=f32)
        base += count


def local(meta, queries, out_grad, qg_t, kv_m, kv_t, q_gain, k_gain):
    f32, b16 = jnp.float32, jnp.bfloat16
    rows = queries.shape[0]
    heads = kv_m.shape[0]
    group_cols = queries.shape[1] // (2 * heads)
    runs = 2 * rows // HD
    pairs = HD * runs * (runs + 1) // 2
    mine = pl.BlockSpec((rows, group_cols), lambda h, meta: (0, meta[0] * heads + h))
    side = lambda which: pl.BlockSpec((None, rows, group_cols), lambda h, meta: (which, 0, h))
    own_kv = pl.BlockSpec((None,) + kv_m.shape[1:], lambda h, meta: (h, 0, 0))
    row = pl.BlockSpec((1, HD), lambda h, meta: (0, 0))
    out = lambda dtype, *shape: (
        pl.BlockSpec((None,) + shape, lambda h, meta: (h,) + (0,) * len(shape)),
        jax.ShapeDtypeStruct((heads,) + shape, dtype),
    )
    outs = [
        out(b16, runs, HD, group_cols), out(b16, runs, HD, group_cols),
        out(b16, runs, HD, group_cols), out(b16, 2 * rows, HD), out(b16, HD, 2 * rows),
        out(b16, 2 * rows, HD), out(b16, pairs, group_cols), out(f32, runs, 1, group_cols),
        out(f32, runs, HD, group_cols), out(f32, runs, 1, group_cols),
    ]
    return pl.pallas_call(
        functools.partial(local_kernel, rows),
        grid_spec=pltpu.PrefetchScalarGridSpec(
            num_scalar_prefetch=1,
            grid=(heads,),
            in_specs=[mine, mine, side(0), side(1), own_kv, own_kv, row, row],
            out_specs=[one[0] for one in outs],
        ),
        out_shape=[one[1] for one in outs],
        compiler_params=pltpu.CompilerParams(vmem_limit_bytes=VMEM_LIMIT),
        cost_estimate=SMALL,
        name="local",
    )(meta, queries, out_grad, qg_t, qg_t, kv_m, kv_t, q_gain, k_gain)


def halo_kernel(
    piece, at, rows, meta, qn, gt, total_own, out_own, doc_own, kv1, kv2, k_gain,
    h1, h2, g_out, delta_out, dq_out,
    k_s, kt_s, v_s, vt_s, dk_s, dv_s, e_s,
):
    f32, b16 = jnp.float32, jnp.bfloat16
    core = meta[0]
    wide = qn.shape[-1]
    blocks = rows // BLK
    sources = ((kv2.at[at], 0), (kv1, 2 * rows))

    for source, base in sources:
        for part in range(2):
            off = pl.multiple_of(base + (core if part == 0 else 1 - core) * rows, rows)
            k = source[part, :rows].astype(f32)
            kn = (k * inverse_rms(k, -1) * k_gain[...]).astype(b16)
            k_s[pl.ds(off, rows), :] = kn
            kt_s[:, pl.ds(off, rows)] = kn.T
            v = source[part, rows : 2 * rows]
            v_s[pl.ds(off, rows), :] = v
            vt_s[:, pl.ds(off, rows)] = v.T

    token = lax.rem(lax.broadcasted_iota(jnp.int32, (1, wide), 1), HD)
    nt = (((1,), (1,)), ((), ()))
    ids = [
        source[part, 2 * rows :, :1].astype(f32)[b : b + 1]
        for source, base in sources
        for part in range(2)
        for b in range(blocks)
    ]
    for run in range(2 * rows // HD):
        low = run * HD
        doc = doc_own[piece, run]
        earlier = jnp.zeros((1, wide), f32)
        for one in ids:
            earlier = earlier + (one < doc).astype(f32)
        first = earlier.astype(jnp.int32) * BLK - low
        qn_run = qn[piece, run]
        s = jnp.dot(k_s[low:, :], qn_run, preferred_element_type=f32)
        total = total_own[piece, run] + weights(s, first, "window", token, e_s, low)
        e = e_s[low:, :]
        out = out_own[piece, run] + jnp.dot(vt_s[:, low:], e, preferred_element_type=f32)
        inverse = 1.0 / total
        g_l = (gt[piece, run].astype(f32) * inverse).astype(b16)
        delta = jnp.sum(g_l.astype(f32) * (out * inverse), axis=0, keepdims=True)
        g_out[run] = g_l
        delta_out[run] = delta
        dp = jnp.dot(v_s[low:, :], g_l, preferred_element_type=f32)
        ds = (e.astype(f32) * (dp - delta)).astype(b16)
        dv = lax.dot_general(e, g_l, nt, preferred_element_type=f32)
        dk = lax.dot_general(ds, qn_run, nt, preferred_element_type=f32)
        dv_s[low:, :] = dv if run == 0 else dv_s[low:, :] + dv
        dk_s[low:, :] = dk if run == 0 else dk_s[low:, :] + dk
        dq_out[run] = jnp.dot(kt_s[:, low:], ds, preferred_element_type=f32)

    for target, base in ((h2, 0), (h1, 2 * rows)):
        for part in range(2):
            off = pl.multiple_of(base + (core if part == 0 else 1 - core) * rows, rows)
            target[part, :rows] = dk_s[pl.ds(off, rows), :].astype(b16)
            target[part, rows:] = dv_s[pl.ds(off, rows), :].astype(b16)


def halo(piece, meta, qn, gt, total_own, out_own, doc_own, kv1, kv2, k_gain):
    array, at = kv2
    rows = (array.shape[2] - ID_ROWS) // 2
    runs, wide = qn.shape[1], qn.shape[-1]
    f32, b16 = jnp.float32, jnp.bfloat16
    vmem = pl.BlockSpec(memory_space=pltpu.VMEM)
    return pl.pallas_call(
        functools.partial(halo_kernel, piece, at, rows),
        in_specs=[pl.BlockSpec(memory_space=pltpu.SMEM)] + [vmem] * 8,
        out_specs=[vmem] * 5,
        scratch_shapes=[
            pltpu.VMEM((WINDOW, HD), b16),
            pltpu.VMEM((HD, WINDOW), b16),
            pltpu.VMEM((WINDOW, HD), b16),
            pltpu.VMEM((HD, WINDOW), b16),
            pltpu.VMEM((WINDOW, HD), f32),
            pltpu.VMEM((WINDOW, HD), f32),
            pltpu.VMEM((WINDOW, wide), b16),
        ],
        out_shape=[
            jax.ShapeDtypeStruct((2, 2 * rows, HD), b16),
            jax.ShapeDtypeStruct((2, 2 * rows, HD), b16),
            jax.ShapeDtypeStruct((runs, HD, wide), b16),
            jax.ShapeDtypeStruct((runs, 1, wide), f32),
            jax.ShapeDtypeStruct((runs, HD, wide), f32),
        ],
        compiler_params=pltpu.CompilerParams(vmem_limit_bytes=VMEM_LIMIT),
        cost_estimate=SMALL,
        name=f"halo_{piece}",
    )(meta, qn, gt, total_own, out_own, doc_own, kv1, array, k_gain)


def own_kernel(pieces, rows, meta, q_gain, qt, qn, k_own, kt_own, v_own, e_own, *refs):
    f32, b16 = jnp.float32, jnp.bfloat16
    core = meta[0]
    count = len(pieces)
    inputs, (dq_m, dq_t), owns, (dq_s, dk_s, dv_s) = (
        refs[: 3 * count], refs[3 * count : 3 * count + 2],
        refs[3 * count + 2 : 4 * count + 2], refs[4 * count + 2 :],
    )
    runs, wide = qt.shape[1], qt.shape[-1]
    nt = (((1,), (1,)), ((), ()))
    gain = jnp.broadcast_to(q_gain[...], (HD, HD)).T * qk_scale
    gain = jnp.concatenate([gain] * (wide // HD), axis=1)
    for at, piece in enumerate(pieces):
        g_in, delta_in, dq_in = inputs[3 * at : 3 * at + 3]
        base = runs * (runs + 1) // 2 * HD
        for run in reversed(range(runs)):
            keys = (run + 1) * HD
            base -= keys
            g_l, qn_run = g_in[run], qn[piece, run]
            e = e_own[piece, base : base + keys, :]
            dp = jnp.dot(v_own[piece, :keys, :], g_l, preferred_element_type=f32)
            ds = (e.astype(f32) * (dp - delta_in[run])).astype(b16)
            dv = lax.dot_general(e, g_l, nt, preferred_element_type=f32)
            dk = lax.dot_general(ds, qn_run, nt, preferred_element_type=f32)
            dv_s[:keys, :] = dv if run == runs - 1 else dv_s[:keys, :] + dv
            dk_s[:keys, :] = dk if run == runs - 1 else dk_s[:keys, :] + dk
            dq = dq_in[run] + jnp.dot(kt_own[piece, :, :keys], ds, preferred_element_type=f32)
            q = qt[piece, run].astype(f32)
            r = inverse_rms(q, 0)
            scaled = dq * gain
            dq = r * scaled - q * (r * r * r * jnp.mean(q * scaled, axis=0, keepdims=True))
            slot, inside = divmod(run * HD, rows)
            for head in range(wide // HD):
                lanes = slice(head * HD, (head + 1) * HD)
                columns = slice(at * wide + head * HD, at * wide + (head + 1) * HD)
                dq_s[slot, inside : inside + HD, columns] = dq[:, lanes].T.astype(b16)
        for slot in range(2):
            part = lax.rem(slot + core, 2)
            owns[at][part, :rows] = dk_s[slot * rows : (slot + 1) * rows, :]
            owns[at][part, rows:] = dv_s[slot * rows : (slot + 1) * rows, :]
    dq_m[...] = dq_s[core]
    dq_t[...] = dq_s[1 - core]


def own_keys(pieces, meta, q_gain, qt, qn, k_own, kt_own, v_own, e_own, results):
    rows = k_own.shape[1] // 2
    columns = len(pieces) * qt.shape[-1]
    f32, b16 = jnp.float32, jnp.bfloat16
    vmem = pl.BlockSpec(memory_space=pltpu.VMEM)
    dq = jax.ShapeDtypeStruct((rows, columns), b16)
    own = jax.ShapeDtypeStruct((2, 2 * rows, HD), f32)
    flat = [one for piece in pieces for one in results[piece]]
    out = pl.pallas_call(
        functools.partial(own_kernel, tuple(pieces), rows),
        in_specs=[pl.BlockSpec(memory_space=pltpu.SMEM)] + [vmem] * (7 + len(flat)),
        out_specs=[vmem] * (2 + len(pieces)),
        scratch_shapes=[
            pltpu.VMEM((2, rows, columns), b16),
            pltpu.VMEM((2 * rows, HD), f32),
            pltpu.VMEM((2 * rows, HD), f32),
        ],
        out_shape=[dq, dq] + [own] * len(pieces),
        compiler_params=pltpu.CompilerParams(vmem_limit_bytes=VMEM_LIMIT),
        cost_estimate=SMALL,
        name=f"own_{pieces[0]}",
    )(meta, q_gain, qt, qn, k_own, kt_own, v_own, e_own, *flat)
    return out[0], out[1], out[2:]


def finish_kernel(rows, places, meta, k_gain, *refs):
    f32 = jnp.float32
    even = meta[1] == 0
    outs = refs[4 * len(places) :]
    for piece, (at_returned, at_kv0) in enumerate(places):
        own, swapped, returned, kv0 = refs[4 * piece : 4 * piece + 4]
        columns = slice(piece * HD, (piece + 1) * HD)
        for part in range(2):
            total = own[part] + returned[at_returned, part].astype(f32)
            total = total + jnp.where(even, swapped[part].astype(f32), 0.0)
            k = kv0[at_kv0, part, :rows].astype(f32)
            r = inverse_rms(k, -1)
            scaled = total[:rows] * k_gain[...]
            grad = r * scaled - k * (r * r * r * jnp.mean(k * scaled, axis=-1, keepdims=True))
            outs[part][:rows, columns] = grad.astype(outs[part].dtype)
            outs[part][rows:, columns] = total[rows:].astype(outs[part].dtype)


def finish(name, meta, k_gain, pieces):
    rows = pieces[0][0].shape[1] // 2
    vmem = pl.BlockSpec(memory_space=pltpu.VMEM)
    shape = jax.ShapeDtypeStruct((2 * rows, len(pieces) * HD), jnp.bfloat16)
    flat = [one for own, swapped, back, kv0 in pieces for one in (own, swapped, back[0], kv0[0])]
    places = tuple((back[1], kv0[1]) for own, swapped, back, kv0 in pieces)
    return pl.pallas_call(
        functools.partial(finish_kernel, rows, places),
        in_specs=[pl.BlockSpec(memory_space=pltpu.SMEM)] + [vmem] * (1 + len(flat)),
        out_specs=[vmem, vmem],
        out_shape=[shape, shape],
        compiler_params=pltpu.CompilerParams(vmem_limit_bytes=VMEM_LIMIT),
        cost_estimate=SMALL,
        name=name,
    )(meta, k_gain, *flat)


def after(value, *others):
    return lax.optimization_barrier((value,) + others)[0]


def on_device(queries, keys, values, out_grad, q_gain, k_gain, doc_ids):
    f32, b16 = jnp.float32, jnp.bfloat16
    rows = queries.shape[0]
    half = keys.shape[1] // 2
    pieces = half // HD
    count = lax.axis_size("ctx")
    if WINDOW != 4 * rows or count % 4 != 0:
        raise ValueError("unsupported split")
    rank = lax.axis_index("ctx")
    core = lax.rem(rank, 2)
    parity = lax.rem(lax.div(rank, 2), 2)
    odd = parity == 1
    meta = jnp.stack([core, parity]).astype(jnp.int32)

    core_swap = [(i, i ^ 1) for i in range(count)]
    x_swap = [(i, i ^ 2) for i in range(count)]
    ahead = [(i, i + 4) for i in range(count - 4)]
    back = [(i + 4, i) for i in range(count - 4)]

    kv_m, kv_o, qg_o = pack(doc_ids, keys, values, queries, out_grad)
    kv_t = lax.ppermute(kv_o, "ctx", core_swap)
    qg_t = lax.ppermute(qg_o, "ctx", core_swap)
    kv0, kv1, kv2 = [], [], []
    for group in ((0,), (1,), tuple(range(2, pieces))):
        block = jnp.stack([jnp.stack([kv_m[piece], kv_t[piece]]) for piece in group])
        moved = lax.ppermute(block, "ctx", ahead)
        kv0.extend((block, at) for at in range(len(group)))
        kv2.extend((moved, at) for at in range(len(group)))
    q_gain_row = q_gain.reshape(1, HD)
    k_gain_row = k_gain.reshape(1, HD)

    swapped, joined, returned, results, sums_h2 = [], [], [], [], []

    def x_hop(piece, turn):
        operand = jnp.where(turn, kv2[piece][0][kv2[piece][1]], kv0[piece][0][kv0[piece][1]])
        kv1.append(lax.ppermute(operand, "ctx", x_swap))
        return operand

    def send_back(group, turn):
        block = []
        for piece in group:
            arrived = jnp.where(turn, swapped[piece].astype(f32), 0.0)
            block.append((sums_h2[piece].astype(f32) + arrived).astype(b16))
        joined.append(jnp.stack(block))
        moved = lax.ppermute(joined[-1], "ctx", back)
        returned.extend((moved, at) for at in range(len(group)))

    hop_0 = x_hop(0, odd)
    qt, qn, gt, k_own, kt_own, v_own, e_own, total_own, out_own, doc_own = local(
        after(meta, hop_0), queries, out_grad, qg_t, kv_m, kv_t, q_gain_row, k_gain_row
    )
    order = after(meta, x_hop(1, after(odd, total_own)))
    for piece in range(pieces):
        h1, h2, *result = halo(
            piece, order, qn, gt, total_own, out_own, doc_own, kv1[piece], kv2[piece], k_gain_row
        )
        results.append(result)
        order = after(order, result[1])
        if piece + 2 < pieces:
            order = after(order, x_hop(piece + 2, after(odd, result[1])))
        swapped.append(lax.ppermute(h1, "ctx", x_swap))
        sums_h2.append(h2)
        if piece == 2:
            send_back((0, 1), after(odd, result[1]))
            order = after(order, joined[-1])
        elif piece > 2:
            send_back((piece - 1,), after(odd, result[1]))

    def own_part(group, order):
        return own_keys(
            list(group), order, q_gain_row, qt, qn, k_own, kt_own, v_own, e_own, results
        )

    order = after(order, joined[-1], returned[0][0])
    dq_m_first, dq_t_first, own_first = own_part(range(pieces // 2), order)
    send_back((pieces - 1,), after(odd, dq_m_first))
    order = after(order, joined[-1], returned[2][0])
    dq_m_last, dq_t_last, own_last = own_part(range(pieces // 2, pieces), order)
    dq_m, dq_t, own = [dq_m_first, dq_m_last], [dq_t_first, dq_t_last], [*own_first, *own_last]
    sums = [(own[i], swapped[i], returned[i], kv0[i]) for i in range(pieces)]

    def join(mine, theirs, first):
        return jnp.where(
            first == 0,
            jnp.concatenate(mine + theirs, axis=-1),
            jnp.concatenate(theirs + mine, axis=-1),
        )

    dq_back = [lax.ppermute(one, "ctx", core_swap) for one in dq_t]
    final_m, final_t = [], []
    for name, group in (("finish_first", sums[:-1]), ("finish_last", sums[-1:])):
        mine, theirs = finish(name, order, k_gain_row, group)
        order = after(order, mine)
        final_m.append(mine)
        final_t.append(lax.ppermute(theirs, "ctx", core_swap))
    query_grad = join(dq_m, dq_back, after(core, final_m[-1]))
    key_grad = join([one[:rows] for one in final_m], [one[:rows] for one in final_t], core)
    value_grad = join([one[rows:] for one in final_m], [one[rows:] for one in final_t], core)
    return (query_grad, key_grad, value_grad)


def solution(mesh):
    split = P(("groups", "ctx"), None)
    in_specs = (split, split, split, split, P(), P(), P(("groups", "ctx")))
    return jax.shard_map(
        on_device, mesh=mesh, in_specs=in_specs, out_specs=(split, split, split), check_vma=False
    )
```

```python
import functools

import jax
import jax.numpy as jnp
from jax import lax
from jax.experimental import pallas as pl
from jax.experimental.pallas import tpu as pltpu
from jax.sharding import PartitionSpec as P

HD = 128
WINDOW = 1024
BLK = 64
ID_ROWS = 16
VMEM_LIMIT = 12 * 1024 * 1024
HIDDEN = -1e30
SMALL = pl.CostEstimate(flops=2**20, bytes_accessed=2**16, transcendentals=0)

qk_scale = 168.0 ** (-0.5)
norm_epsilon = 1e-06


def inverse_rms(values_in, axis):
    return lax.rsqrt(jnp.mean(values_in * values_in, axis=axis, keepdims=True) + norm_epsilon)


def weights(scores, first, diagonal, token, e_ref, base):
    total = jnp.zeros((8, scores.shape[1]), jnp.float32)
    key = lax.broadcasted_iota(jnp.int32, (BLK, scores.shape[1]), 0)
    for at in range(0, scores.shape[0], BLK):
        block = scores[at : at + BLK] + jnp.where(first <= at, 0.0, HIDDEN)
        if diagonal == "window" and at < HD:
            block = jnp.where(key + at > token, block, HIDDEN)
        if diagonal == "causal" and at >= scores.shape[0] - HD:
            block = jnp.where(key + (at - scores.shape[0] + HD) <= token, block, HIDDEN)
        e = jnp.exp(block)
        total = total + jnp.sum(e.reshape(BLK // 8, 8, scores.shape[1]), axis=0)
        e_ref[base + at : base + at + BLK, :] = e.astype(e_ref.dtype)
    return jnp.sum(total, axis=0, keepdims=True)


def local_kernel(
    rows, meta, ids_m, ids_t, q_m, g_m, q_t, g_t, kv_m, kv_t, q_gain, k_gain,
    qt, qn, gt, k_own, kt_own, v_own, e_own, total_own, out_own, doc_own,
):
    f32, b16 = jnp.float32, jnp.bfloat16
    core = meta[0]
    wide = qt.shape[-1]
    blocks = rows // BLK
    runs = rows // HD
    gain = jnp.broadcast_to(q_gain[...], (HD, HD)).T * qk_scale
    gain = jnp.concatenate([gain] * (wide // HD), axis=1)
    for part, (q_ref, g_ref, kv) in enumerate(((q_m, g_m, kv_m), (q_t, g_t, kv_t))):
        slot = core if part == 0 else 1 - core
        for head in range(q_m.shape[1] // HD):
            columns = slice(head * HD, (head + 1) * HD)
            q, g = q_ref[:, columns].T, g_ref[:, columns].T
            for run in range(runs):
                tokens = slice(run * HD, (run + 1) * HD)
                qt[slot * runs + run, :, columns] = q[:, tokens]
                gt[slot * runs + run, :, columns] = g[:, tokens]
        off = pl.multiple_of(slot * rows, rows)
        k = kv[0].astype(f32)
        kn = (k * inverse_rms(k, -1) * k_gain[...]).astype(b16)
        k_own[pl.ds(off, rows), :] = kn
        kt_own[:, pl.ds(off, rows)] = kn.T
        v_own[pl.ds(off, rows), :] = kv[1]
    token = lax.rem(lax.broadcasted_iota(jnp.int32, (1, wide), 1), HD)
    ids = [[one[b] + 1 for b in range(blocks)] for one in (ids_m, ids_t)]
    base = 0
    for run in range(2 * runs):
        slot, inside = divmod(run * HD, rows)
        doc = jnp.zeros((1, wide), jnp.int32)
        for b in range(HD // BLK):
            at = inside // BLK + b
            here = jnp.where(core == slot, ids[0][at], ids[1][at])
            doc = jnp.where(token >= b * BLK, here, doc)
        doc_own[run] = doc.astype(f32)
        earlier = jnp.zeros((1, wide), jnp.int32)
        for one in ids[0] + ids[1]:
            earlier = earlier + (one < doc).astype(jnp.int32)
        first = earlier * BLK
        q = qt[run].astype(f32)
        qn_run = (q * inverse_rms(q, 0) * gain).astype(b16)
        qn[run] = qn_run
        count = (run + 1) * HD
        s = jnp.dot(k_own[:count, :], qn_run, preferred_element_type=f32)
        total_own[run] = weights(s, first, "causal", token, e_own, base)
        vt = v_own[:count, :].T
        out_own[run] = jnp.dot(vt, e_own[base : base + count, :], preferred_element_type=f32)
        base += count


def local(meta, ids_m, ids_t, queries, out_grad, qg_t, kv_m, kv_t, q_gain, k_gain):
    f32, b16 = jnp.float32, jnp.bfloat16
    rows = queries.shape[0]
    heads = kv_m.shape[2] // HD
    group_cols = queries.shape[1] // (2 * heads)
    runs = 2 * rows // HD
    pairs = HD * runs * (runs + 1) // 2
    mine = pl.BlockSpec((rows, group_cols), lambda h, *scalars: (0, scalars[0][0] * heads + h))
    side = lambda which: pl.BlockSpec((None, rows, group_cols), lambda h, *scalars: (which, 0, h))
    own_kv = pl.BlockSpec((2, rows, HD), lambda h, *scalars: (0, 0, h))
    row = pl.BlockSpec((1, HD), lambda h, *scalars: (0, 0))
    out = lambda dtype, *shape: (
        pl.BlockSpec((None,) + shape, lambda h, *scalars: (h,) + (0,) * len(shape)),
        jax.ShapeDtypeStruct((heads,) + shape, dtype),
    )
    outs = [
        out(b16, runs, HD, group_cols), out(b16, runs, HD, group_cols),
        out(b16, runs, HD, group_cols), out(b16, 2 * rows, HD), out(b16, HD, 2 * rows),
        out(b16, 2 * rows, HD), out(b16, pairs, group_cols), out(f32, runs, 1, group_cols),
        out(f32, runs, HD, group_cols), out(f32, runs, 1, group_cols),
    ]
    return pl.pallas_call(
        functools.partial(local_kernel, rows),
        grid_spec=pltpu.PrefetchScalarGridSpec(
            num_scalar_prefetch=3,
            grid=(heads,),
            in_specs=[mine, mine, side(0), side(1), own_kv, own_kv, row, row],
            out_specs=[one[0] for one in outs],
        ),
        out_shape=[one[1] for one in outs],
        compiler_params=pltpu.CompilerParams(vmem_limit_bytes=VMEM_LIMIT),
        cost_estimate=SMALL,
        name="local",
    )(meta, ids_m, ids_t, queries, out_grad, qg_t, qg_t, kv_m, kv_t, q_gain, k_gain)


def halo_kernel(
    piece, at, rows, meta, qn, gt, total_own, out_own, doc_own, kv1, kv2, k_gain,
    h1, h2, g_out, delta_out, dq_out,
    k_s, kt_s, v_s, vt_s, dk_s, dv_s, e_s,
):
    f32, b16 = jnp.float32, jnp.bfloat16
    core = meta[0]
    wide = qn.shape[-1]
    blocks = rows // BLK
    sources = ((kv2.at[at], 0), (kv1, 2 * rows))

    for source, base in sources:
        for part in range(2):
            off = pl.multiple_of(base + (core if part == 0 else 1 - core) * rows, rows)
            k = source[part, :rows].astype(f32)
            kn = (k * inverse_rms(k, -1) * k_gain[...]).astype(b16)
            k_s[pl.ds(off, rows), :] = kn
            kt_s[:, pl.ds(off, rows)] = kn.T
            v = source[part, rows : 2 * rows]
            v_s[pl.ds(off, rows), :] = v
            vt_s[:, pl.ds(off, rows)] = v.T

    token = lax.rem(lax.broadcasted_iota(jnp.int32, (1, wide), 1), HD)
    nt = (((1,), (1,)), ((), ()))
    ids = [
        source[part, 2 * rows :, :1].astype(f32)[b : b + 1]
        for source, base in sources
        for part in range(2)
        for b in range(blocks)
    ]
    for run in range(2 * rows // HD):
        low = run * HD
        doc = doc_own[piece, run]
        earlier = jnp.zeros((1, wide), f32)
        for one in ids:
            earlier = earlier + (one < doc).astype(f32)
        first = earlier.astype(jnp.int32) * BLK - low
        qn_run = qn[piece, run]
        s = jnp.dot(k_s[low:, :], qn_run, preferred_element_type=f32)
        total = total_own[piece, run] + weights(s, first, "window", token, e_s, low)
        e = e_s[low:, :]
        out = out_own[piece, run] + jnp.dot(vt_s[:, low:], e, preferred_element_type=f32)
        inverse = 1.0 / total
        g_l = (gt[piece, run].astype(f32) * inverse).astype(b16)
        delta = jnp.sum(g_l.astype(f32) * (out * inverse), axis=0, keepdims=True)
        g_out[run] = g_l
        delta_out[run] = delta
        dp = jnp.dot(v_s[low:, :], g_l, preferred_element_type=f32)
        ds = (e.astype(f32) * (dp - delta)).astype(b16)
        dv = lax.dot_general(e, g_l, nt, preferred_element_type=f32)
        dk = lax.dot_general(ds, qn_run, nt, preferred_element_type=f32)
        dv_s[low:, :] = dv if run == 0 else dv_s[low:, :] + dv
        dk_s[low:, :] = dk if run == 0 else dk_s[low:, :] + dk
        dq_out[run] = jnp.dot(kt_s[:, low:], ds, preferred_element_type=f32)

    for target, base in ((h2, 0), (h1, 2 * rows)):
        for part in range(2):
            off = pl.multiple_of(base + (core if part == 0 else 1 - core) * rows, rows)
            target[part, :rows] = dk_s[pl.ds(off, rows), :].astype(b16)
            target[part, rows:] = dv_s[pl.ds(off, rows), :].astype(b16)


def halo(piece, meta, qn, gt, total_own, out_own, doc_own, kv1, kv2, k_gain):
    array, at = kv2
    rows = (array.shape[2] - ID_ROWS) // 2
    runs, wide = qn.shape[1], qn.shape[-1]
    f32, b16 = jnp.float32, jnp.bfloat16
    vmem = pl.BlockSpec(memory_space=pltpu.VMEM)
    return pl.pallas_call(
        functools.partial(halo_kernel, piece, at, rows),
        in_specs=[pl.BlockSpec(memory_space=pltpu.SMEM)] + [vmem] * 8,
        out_specs=[vmem] * 5,
        scratch_shapes=[
            pltpu.VMEM((WINDOW, HD), b16),
            pltpu.VMEM((HD, WINDOW), b16),
            pltpu.VMEM((WINDOW, HD), b16),
            pltpu.VMEM((HD, WINDOW), b16),
            pltpu.VMEM((WINDOW, HD), f32),
            pltpu.VMEM((WINDOW, HD), f32),
            pltpu.VMEM((WINDOW, wide), b16),
        ],
        out_shape=[
            jax.ShapeDtypeStruct((2, 2 * rows, HD), b16),
            jax.ShapeDtypeStruct((2, 2 * rows, HD), b16),
            jax.ShapeDtypeStruct((runs, HD, wide), b16),
            jax.ShapeDtypeStruct((runs, 1, wide), f32),
            jax.ShapeDtypeStruct((runs, HD, wide), f32),
        ],
        compiler_params=pltpu.CompilerParams(vmem_limit_bytes=VMEM_LIMIT),
        cost_estimate=SMALL,
        name=f"halo_{piece}",
    )(meta, qn, gt, total_own, out_own, doc_own, kv1, array, k_gain)


def key_finish(rows, even, k_gain, own_k, own_v, swapped, returned, kv0, out, columns):
    f32 = jnp.float32
    arrived = returned.astype(f32) + jnp.where(even, swapped.astype(f32), 0.0)
    k = kv0[:rows].astype(f32)
    r = inverse_rms(k, -1)
    scaled = (own_k + arrived[:rows]) * k_gain
    grad = r * scaled - k * (r * r * r * jnp.mean(k * scaled, axis=-1, keepdims=True))
    out[:rows, columns] = grad.astype(out.dtype)
    out[rows:, columns] = (own_v + arrived[rows:]).astype(out.dtype)


def own_kernel(
    pieces, places, rows, meta, q_gain, k_gain, qt, qn, k_own, kt_own, v_own, e_own, *refs
):
    f32, b16 = jnp.float32, jnp.bfloat16
    core, even = meta[0], meta[1] == 0
    count = len(pieces)
    inputs, refs = refs[: 3 * count], refs[3 * count :]
    ends, refs = refs[: 3 * len(places)], refs[3 * len(places) :]
    (dq_m, dq_t), outs, (dq_s, dk_s, dv_s) = refs[:2], refs[2:-3], refs[-3:]
    runs, wide = qt.shape[1], qt.shape[-1]
    nt = (((1,), (1,)), ((), ()))
    gain = jnp.broadcast_to(q_gain[...], (HD, HD)).T * qk_scale
    gain = jnp.concatenate([gain] * (wide // HD), axis=1)
    for at, piece in enumerate(pieces):
        g_in, delta_in, dq_in = inputs[3 * at : 3 * at + 3]
        base = runs * (runs + 1) // 2 * HD
        for run in reversed(range(runs)):
            keys = (run + 1) * HD
            base -= keys
            g_l, qn_run = g_in[run], qn[piece, run]
            e = e_own[piece, base : base + keys, :]
            dp = jnp.dot(v_own[piece, :keys, :], g_l, preferred_element_type=f32)
            ds = (e.astype(f32) * (dp - delta_in[run])).astype(b16)
            dv = lax.dot_general(e, g_l, nt, preferred_element_type=f32)
            dk = lax.dot_general(ds, qn_run, nt, preferred_element_type=f32)
            dv_s[:keys, :] = dv if run == runs - 1 else dv_s[:keys, :] + dv
            dk_s[:keys, :] = dk if run == runs - 1 else dk_s[:keys, :] + dk
            dq = dq_in[run] + jnp.dot(kt_own[piece, :, :keys], ds, preferred_element_type=f32)
            q = qt[piece, run].astype(f32)
            r = inverse_rms(q, 0)
            scaled = dq * gain
            dq = r * scaled - q * (r * r * r * jnp.mean(q * scaled, axis=0, keepdims=True))
            slot, inside = divmod(run * HD, rows)
            for head in range(wide // HD):
                lanes = slice(head * HD, (head + 1) * HD)
                columns = slice(at * wide + head * HD, at * wide + (head + 1) * HD)
                dq_s[slot, inside : inside + HD, columns] = dq[:, lanes].T.astype(b16)
        for part in range(2):
            tokens = pl.ds(pl.multiple_of((core if part == 0 else 1 - core) * rows, rows), rows)
            if places:
                swapped, returned, kv0 = ends[3 * at : 3 * at + 3]
                at_returned, at_kv0 = places[at]
                key_finish(
                    rows, even, k_gain[...], dk_s[tokens, :], dv_s[tokens, :], swapped[part],
                    returned[at_returned, part], kv0[at_kv0, part],
                    outs[part], slice(at * HD, (at + 1) * HD),
                )
            else:
                outs[at][part, :rows] = dk_s[tokens, :]
                outs[at][part, rows:] = dv_s[tokens, :]
    dq_m[...] = dq_s[core]
    dq_t[...] = dq_s[1 - core]


def own_keys(pieces, meta, q_gain, k_gain, prepared, results, ends):
    qt, qn, k_own, kt_own, v_own, e_own = prepared
    rows = k_own.shape[1] // 2
    columns = len(pieces) * qt.shape[-1]
    f32, b16 = jnp.float32, jnp.bfloat16
    vmem = pl.BlockSpec(memory_space=pltpu.VMEM)
    dq = jax.ShapeDtypeStruct((rows, columns), b16)
    own = jax.ShapeDtypeStruct((2, 2 * rows, HD), f32)
    final = jax.ShapeDtypeStruct((2 * rows, len(pieces) * HD), b16)
    flat = [one for piece in pieces for one in results[piece]]
    flat += [one for swapped, back, kv0 in ends for one in (swapped, back[0], kv0[0])]
    places = tuple((back[1], kv0[1]) for swapped, back, kv0 in ends)
    outs = [dq, dq] + ([final] * 2 if ends else [own] * len(pieces))
    return pl.pallas_call(
        functools.partial(own_kernel, tuple(pieces), places, rows),
        in_specs=[pl.BlockSpec(memory_space=pltpu.SMEM)] + [vmem] * (8 + len(flat)),
        out_specs=[vmem] * len(outs),
        scratch_shapes=[
            pltpu.VMEM((2, rows, columns), b16),
            pltpu.VMEM((2 * rows, HD), f32),
            pltpu.VMEM((2 * rows, HD), f32),
        ],
        out_shape=outs,
        compiler_params=pltpu.CompilerParams(vmem_limit_bytes=VMEM_LIMIT),
        cost_estimate=pl.CostEstimate(flops=2**32, bytes_accessed=2**22, transcendentals=0),
        name=f"own_{pieces[0]}",
    )(meta, q_gain, k_gain, *prepared, *flat)


def finish_kernel(rows, places, meta, k_gain, *refs):
    outs = refs[4 * len(places) :]
    for at, (at_returned, at_kv0) in enumerate(places):
        own, swapped, returned, kv0 = refs[4 * at : 4 * at + 4]
        for part in range(2):
            key_finish(
                rows, meta[1] == 0, k_gain[...], own[part, :rows], own[part, rows:], swapped[part],
                returned[at_returned, part], kv0[at_kv0, part],
                outs[part], slice(at * HD, (at + 1) * HD),
            )


def finish(meta, k_gain, owns, ends):
    rows = owns[0].shape[1] // 2
    vmem = pl.BlockSpec(memory_space=pltpu.VMEM)
    shape = jax.ShapeDtypeStruct((2 * rows, len(owns) * HD), jnp.bfloat16)
    flat = []
    for own, (swapped, back, kv0) in zip(owns, ends):
        flat += [own, swapped, back[0], kv0[0]]
    places = tuple((back[1], kv0[1]) for swapped, back, kv0 in ends)
    return pl.pallas_call(
        functools.partial(finish_kernel, rows, places),
        in_specs=[pl.BlockSpec(memory_space=pltpu.SMEM)] + [vmem] * (1 + len(flat)),
        out_specs=[vmem, vmem],
        out_shape=[shape, shape],
        compiler_params=pltpu.CompilerParams(vmem_limit_bytes=VMEM_LIMIT),
        cost_estimate=SMALL,
        name="finish",
    )(meta, k_gain, *flat)


def join_kernel(count, stacked, *refs):
    core = lax.rem(lax.axis_index("ctx"), 2)
    mine, theirs, refs = refs[:count], refs[count : 2 * count], refs[2 * count :]
    outs, sem = refs[:stacked], refs[-1]
    rows, width = outs[0].shape
    copies = []
    for parts, who in ((mine, core), (theirs, 1 - core)):
        at = 0
        for part in parts:
            columns = pl.ds(pl.multiple_of(who * (width // 2) + at, HD), part.shape[1])
            at += part.shape[1]
            for index, out in enumerate(outs):
                copies.append(
                    pltpu.make_async_copy(
                        part.at[pl.ds(index * rows, rows)], out.at[:, columns], sem.at[len(copies)]
                    )
                )
    for copy in copies:
        copy.start()
    for copy in copies:
        copy.wait()


def join(name, stacked, mine, theirs):
    rows = mine[0].shape[0] // stacked
    width = 2 * sum(part.shape[1] for part in mine)
    out = jax.ShapeDtypeStruct((rows, width), mine[0].dtype)
    vmem = pl.BlockSpec(memory_space=pltpu.VMEM)
    return pl.pallas_call(
        functools.partial(join_kernel, len(mine), stacked),
        in_specs=[vmem] * (2 * len(mine)),
        out_specs=[pl.BlockSpec(memory_space=pltpu.HBM)] * stacked,
        out_shape=[out] * stacked,
        scratch_shapes=[pltpu.SemaphoreType.DMA((2 * stacked * len(mine),))],
        compiler_params=pltpu.CompilerParams(vmem_limit_bytes=VMEM_LIMIT),
        cost_estimate=SMALL,
        name=name,
    )(*mine, *theirs)


def lay_kernel(rows, ids_m, ids_t, kv_m, kv_t, *outs):
    place = [(out, at) for out in outs for at in range(out.shape[0])]
    spread = lax.broadcasted_iota(jnp.int32, (ID_ROWS, HD), 0)
    for part, (ids, kv) in enumerate(((ids_m, kv_m), (ids_t, kv_t))):
        id_rows = jnp.zeros(spread.shape, jnp.float32)
        for b in range(rows // BLK):
            id_rows = jnp.where(spread == b, (ids[b] + 1).astype(jnp.float32), id_rows)
        for head, (out, at) in enumerate(place):
            columns = slice(head * HD, (head + 1) * HD)
            out[at, part, :rows] = kv[0, :, columns]
            out[at, part, rows : 2 * rows] = kv[1, :, columns]
            out[at, part, 2 * rows :] = id_rows.astype(out.dtype)


def lay(ids_m, ids_t, kv_m, kv_t):
    rows = kv_m.shape[1]
    shape = lambda count: jax.ShapeDtypeStruct((count, 2, 2 * rows + ID_ROWS, HD), kv_m.dtype)
    vmem = pl.BlockSpec(memory_space=pltpu.VMEM)
    smem = pl.BlockSpec(memory_space=pltpu.SMEM)
    return pl.pallas_call(
        functools.partial(lay_kernel, rows),
        in_specs=[smem, smem, vmem, vmem],
        out_specs=[vmem] * 3,
        out_shape=[shape(1), shape(1), shape(kv_m.shape[2] // HD - 2)],
        compiler_params=pltpu.CompilerParams(vmem_limit_bytes=VMEM_LIMIT),
        cost_estimate=SMALL,
        name="lay",
    )(ids_m, ids_t, kv_m, kv_t)


def after(value, *others):
    return lax.optimization_barrier((value,) + others)[0]


def on_device(queries, keys, values, out_grad, q_gain, k_gain, doc_ids):
    f32, b16 = jnp.float32, jnp.bfloat16
    rows = queries.shape[0]
    half = keys.shape[1] // 2
    pieces = half // HD
    count = lax.axis_size("ctx")
    if WINDOW != 4 * rows or count % 4 != 0:
        raise ValueError("unsupported split")
    rank = lax.axis_index("ctx")
    core = lax.rem(rank, 2)
    parity = lax.rem(lax.div(rank, 2), 2)
    odd = parity == 1
    meta = jnp.stack([core, parity]).astype(jnp.int32)

    core_swap = [(i, i ^ 1) for i in range(count)]
    x_swap = [(i, i ^ 2) for i in range(count)]
    ahead = [(i, i + 4) for i in range(count - 4)]
    back = [(i + 4, i) for i in range(count - 4)]

    def half_of(array, who):
        width = array.shape[1] // 2
        return lax.dynamic_slice(array, (0, who * width), (rows, width))

    def both(one, two, who):
        return jnp.stack([half_of(one, who), half_of(two, who)])

    kv_o = both(keys, values, 1 - core)
    kv_t = lax.ppermute(kv_o, "ctx", core_swap)
    kv_m = both(keys, values, core)
    ids_t = lax.ppermute(doc_ids, "ctx", core_swap)

    blocks = lay(doc_ids, ids_t, kv_m, kv_t)
    kv0, kv1, kv2 = [], [], []
    for block in blocks:
        moved = lax.ppermute(block, "ctx", ahead)
        kv0.extend((block, at) for at in range(block.shape[0]))
        kv2.extend((moved, at) for at in range(block.shape[0]))
    other = after(1 - core, kv_o)
    qg_t = lax.ppermute(both(queries, out_grad, other), "ctx", core_swap)

    q_gain_row = q_gain.reshape(1, HD)
    k_gain_row = k_gain.reshape(1, HD)
    swapped, joined, returned, results, sums_h2 = [], [], [], [], []

    def x_hop(piece, turn):
        operand = jnp.where(turn, kv2[piece][0][kv2[piece][1]], kv0[piece][0][kv0[piece][1]])
        kv1.append(lax.ppermute(operand, "ctx", x_swap))
        return operand

    def send_back(group, turn):
        block = []
        for piece in group:
            arrived = jnp.where(turn, swapped[piece].astype(f32), 0.0)
            block.append((sums_h2[piece].astype(f32) + arrived).astype(b16))
        joined.append(jnp.stack(block))
        moved = lax.ppermute(joined[-1], "ctx", back)
        returned.extend((moved, at) for at in range(len(group)))

    hop_0 = x_hop(0, odd)
    qt, qn, gt, k_own, kt_own, v_own, e_own, total_own, out_own, doc_own = local(
        after(meta, hop_0), doc_ids, ids_t, queries, out_grad, qg_t, kv_m, kv_t, q_gain_row, k_gain_row
    )
    order = after(meta, x_hop(1, after(odd, total_own)))
    for piece in range(pieces):
        h1, h2, *result = halo(
            piece, order, qn, gt, total_own, out_own, doc_own, kv1[piece], kv2[piece], k_gain_row
        )
        results.append(result)
        order = after(order, result[1])
        if piece + 2 < pieces:
            order = after(order, x_hop(piece + 2, after(odd, result[1])))
        swapped.append(lax.ppermute(h1, "ctx", x_swap))
        sums_h2.append(h2)
        if piece == 2:
            send_back((0, 1), after(odd, result[1]))
            order = after(order, joined[-1])
        elif piece > 2:
            send_back((piece - 1,), after(odd, result[1]))

    prepared = (qt, qn, k_own, kt_own, v_own, e_own)
    ends = lambda group: [(swapped[i], returned[i], kv0[i]) for i in group]
    middle = pieces // 2
    late, soon = list(range(middle, pieces)), list(range(middle))
    order = after(order, joined[-1])
    dq_m_late, dq_t_late, *own_late = own_keys(
        late, order, q_gain_row, k_gain_row, prepared, results, []
    )
    send_back((pieces - 1,), after(odd, dq_m_late))
    order = after(order, joined[-1], returned[0][0], returned[2][0])
    dq_m_soon, dq_t_soon, kv_m_soon, kv_t_soon = own_keys(
        soon, order, q_gain_row, k_gain_row, prepared, results, ends(soon)
    )
    swap = lambda array: lax.ppermute(array, "ctx", core_swap)
    (query_grad,) = join(
        "join_query", 1, [dq_m_soon, dq_m_late], [swap(dq_t_soon), swap(dq_t_late)]
    )
    kv_m_late, kv_t_late = finish(order, k_gain_row, own_late, ends(late))
    key_grad, value_grad = join(
        "join_key", 2, [kv_m_soon, kv_m_late], [swap(kv_t_soon), swap(kv_t_late)]
    )
    return (query_grad, key_grad, value_grad)


def solution(mesh):
    split = P(("groups", "ctx"), None)
    in_specs = (split, split, split, split, P(), P(), P(("groups", "ctx")))
    return jax.shard_map(
        on_device, mesh=mesh, in_specs=in_specs, out_specs=(split, split, split), check_vma=False
    )
```

```python
import functools

import jax
import jax.numpy as jnp
from jax import lax
from jax.experimental import pallas as pl
from jax.experimental.pallas import tpu as pltpu
from jax.sharding import PartitionSpec as P

HD = 128
WINDOW = 1024
BLK = 64
ID_ROWS = 16
VMEM_LIMIT = 12 * 1024 * 1024
HIDDEN = -1e30
SMALL = pl.CostEstimate(flops=2**20, bytes_accessed=2**16, transcendentals=0)

qk_scale = 168.0 ** (-0.5)
norm_epsilon = 1e-06


def inverse_rms(values_in, axis):
    return lax.rsqrt(jnp.mean(values_in * values_in, axis=axis, keepdims=True) + norm_epsilon)


def weights(scores, first, diagonal, token, e_ref, base):
    total = jnp.zeros((8, scores.shape[1]), jnp.float32)
    key = lax.broadcasted_iota(jnp.int32, (BLK, scores.shape[1]), 0)
    for at in range(0, scores.shape[0], BLK):
        block = scores[at : at + BLK] + jnp.where(first <= at, 0.0, HIDDEN)
        if diagonal == "window" and at < HD:
            block = jnp.where(key + at > token, block, HIDDEN)
        if diagonal == "causal" and at >= scores.shape[0] - HD:
            block = jnp.where(key + (at - scores.shape[0] + HD) <= token, block, HIDDEN)
        e = jnp.exp(block)
        total = total + jnp.sum(e.reshape(BLK // 8, 8, scores.shape[1]), axis=0)
        e_ref[base + at : base + at + BLK, :] = e.astype(e_ref.dtype)
    return jnp.sum(total, axis=0, keepdims=True)


def local_kernel(
    rows, meta, qg_m, qg_t, kv_m, kv_t, q_gain, k_gain,
    qt, qn, gt, k_own, kt_own, v_own, e_own, total_own, out_own, doc_own,
):
    f32, b16 = jnp.float32, jnp.bfloat16
    core = meta[0]
    wide = qt.shape[-1]
    blocks = rows // BLK
    runs = rows // HD
    gain = jnp.broadcast_to(q_gain[...], (HD, HD)).T * qk_scale
    gain = jnp.concatenate([gain] * (wide // HD), axis=1)
    for part, (qg, kv) in enumerate(((qg_m, kv_m), (qg_t, kv_t))):
        slot = core if part == 0 else 1 - core
        for head in range(wide // HD):
            columns = slice(head * HD, (head + 1) * HD)
            q, g = qg[0, :, columns].T, qg[1, :, columns].T
            for run in range(runs):
                tokens = slice(run * HD, (run + 1) * HD)
                qt[slot * runs + run, :, columns] = q[:, tokens]
                gt[slot * runs + run, :, columns] = g[:, tokens]
        off = pl.multiple_of(slot * rows, rows)
        k = kv[:rows].astype(f32)
        kn = (k * inverse_rms(k, -1) * k_gain[...]).astype(b16)
        k_own[pl.ds(off, rows), :] = kn
        kt_own[:, pl.ds(off, rows)] = kn.T
        v_own[pl.ds(off, rows), :] = kv[rows : 2 * rows]
    token = lax.rem(lax.broadcasted_iota(jnp.int32, (1, wide), 1), HD)
    ids = [[kv[2 * rows :, :1].astype(f32)[b : b + 1] for b in range(blocks)] for kv in (kv_m, kv_t)]
    base = 0
    for run in range(2 * runs):
        slot, inside = divmod(run * HD, rows)
        doc = jnp.zeros((1, wide), f32)
        for b in range(HD // BLK):
            at = inside // BLK + b
            here = jnp.where(core == slot, ids[0][at], ids[1][at])
            doc = jnp.where(token >= b * BLK, here, doc)
        doc_own[run] = doc
        earlier = jnp.zeros((1, wide), f32)
        for one in ids[0] + ids[1]:
            earlier = earlier + (one < doc).astype(f32)
        first = earlier.astype(jnp.int32) * BLK
        q = qt[run].astype(f32)
        qn_run = (q * inverse_rms(q, 0) * gain).astype(b16)
        qn[run] = qn_run
        count = (run + 1) * HD
        s = jnp.dot(k_own[:count, :], qn_run, preferred_element_type=f32)
        total_own[run] = weights(s, first, "causal", token, e_own, base)
        vt = v_own[:count, :].T
        out_own[run] = jnp.dot(vt, e_own[base : base + count, :], preferred_element_type=f32)
        base += count


def local(begin, heads, meta, qg_m, qg_t, kv_m, kv_t, q_gain, k_gain):
    f32, b16 = jnp.float32, jnp.bfloat16
    rows = qg_m.shape[1]
    group_cols = qg_m.shape[2] // (kv_m.shape[1] // HD)
    runs = 2 * rows // HD
    pairs = HD * runs * (runs + 1) // 2
    qg = pl.BlockSpec((2, rows, group_cols), lambda h, meta: (0, 0, begin + h))
    kv = pl.BlockSpec((kv_m.shape[0], HD), lambda h, meta: (0, begin + h))
    row = pl.BlockSpec((1, HD), lambda h, meta: (0, 0))
    out = lambda dtype, *shape: (
        pl.BlockSpec((None,) + shape, lambda h, meta: (h,) + (0,) * len(shape)),
        jax.ShapeDtypeStruct((heads,) + shape, dtype),
    )
    outs = [
        out(b16, runs, HD, group_cols), out(b16, runs, HD, group_cols),
        out(b16, runs, HD, group_cols), out(b16, 2 * rows, HD), out(b16, HD, 2 * rows),
        out(b16, 2 * rows, HD), out(b16, pairs, group_cols), out(f32, runs, 1, group_cols),
        out(f32, runs, HD, group_cols), out(f32, runs, 1, group_cols),
    ]
    return pl.pallas_call(
        functools.partial(local_kernel, rows),
        grid_spec=pltpu.PrefetchScalarGridSpec(
            num_scalar_prefetch=1,
            grid=(heads,),
            in_specs=[qg, qg, kv, kv, row, row],
            out_specs=[one[0] for one in outs],
        ),
        out_shape=[one[1] for one in outs],
        compiler_params=pltpu.CompilerParams(vmem_limit_bytes=VMEM_LIMIT),
        cost_estimate=SMALL,
        name=f"local_{begin}",
    )(meta, qg_m, qg_t, kv_m, kv_t, q_gain, k_gain)


def halo_kernel(
    piece, at, rows, meta, qn, gt, total_own, out_own, doc_own, kv1, kv2, k_gain,
    h1, h2, g_out, delta_out, dq_out,
    k_s, kt_s, v_s, vt_s, dk_s, dv_s, e_s,
):
    f32, b16 = jnp.float32, jnp.bfloat16
    core = meta[0]
    wide = qn.shape[-1]
    blocks = rows // BLK
    sources = ((kv2.at[at], 0), (kv1, 2 * rows))

    for source, base in sources:
        for part in range(2):
            off = pl.multiple_of(base + (core if part == 0 else 1 - core) * rows, rows)
            k = source[part, :rows].astype(f32)
            kn = (k * inverse_rms(k, -1) * k_gain[...]).astype(b16)
            k_s[pl.ds(off, rows), :] = kn
            kt_s[:, pl.ds(off, rows)] = kn.T
            v = source[part, rows : 2 * rows]
            v_s[pl.ds(off, rows), :] = v
            vt_s[:, pl.ds(off, rows)] = v.T

    token = lax.rem(lax.broadcasted_iota(jnp.int32, (1, wide), 1), HD)
    nt = (((1,), (1,)), ((), ()))
    ids = [
        source[part, 2 * rows :, :1].astype(f32)[b : b + 1]
        for source, base in sources
        for part in range(2)
        for b in range(blocks)
    ]
    for run in range(2 * rows // HD):
        low = run * HD
        doc = doc_own[piece, run]
        earlier = jnp.zeros((1, wide), f32)
        for one in ids:
            earlier = earlier + (one < doc).astype(f32)
        first = earlier.astype(jnp.int32) * BLK - low
        qn_run = qn[piece, run]
        s = jnp.dot(k_s[low:, :], qn_run, preferred_element_type=f32)
        total = total_own[piece, run] + weights(s, first, "window", token, e_s, low)
        e = e_s[low:, :]
        out = out_own[piece, run] + jnp.dot(vt_s[:, low:], e, preferred_element_type=f32)
        inverse = 1.0 / total
        g_l = (gt[piece, run].astype(f32) * inverse).astype(b16)
        delta = jnp.sum(g_l.astype(f32) * (out * inverse), axis=0, keepdims=True)
        g_out[run] = g_l
        delta_out[run] = delta
        dp = jnp.dot(v_s[low:, :], g_l, preferred_element_type=f32)
        ds = (e.astype(f32) * (dp - delta)).astype(b16)
        dv = lax.dot_general(e, g_l, nt, preferred_element_type=f32)
        dk = lax.dot_general(ds, qn_run, nt, preferred_element_type=f32)
        dv_s[low:, :] = dv if run == 0 else dv_s[low:, :] + dv
        dk_s[low:, :] = dk if run == 0 else dk_s[low:, :] + dk
        dq_out[run] = jnp.dot(kt_s[:, low:], ds, preferred_element_type=f32)

    for target, base in ((h2, 0), (h1, 2 * rows)):
        for part in range(2):
            off = pl.multiple_of(base + (core if part == 0 else 1 - core) * rows, rows)
            target[part, :rows] = dk_s[pl.ds(off, rows), :].astype(b16)
            target[part, rows:] = dv_s[pl.ds(off, rows), :].astype(b16)


def halo(piece, meta, qn, gt, total_own, out_own, doc_own, kv1, kv2, k_gain):
    array, at = kv2
    rows = (array.shape[2] - ID_ROWS) // 2
    runs, wide = qn.shape[1], qn.shape[-1]
    f32, b16 = jnp.float32, jnp.bfloat16
    vmem = pl.BlockSpec(memory_space=pltpu.VMEM)
    return pl.pallas_call(
        functools.partial(halo_kernel, piece, at, rows),
        in_specs=[pl.BlockSpec(memory_space=pltpu.SMEM)] + [vmem] * 8,
        out_specs=[vmem] * 5,
        scratch_shapes=[
            pltpu.VMEM((WINDOW, HD), b16),
            pltpu.VMEM((HD, WINDOW), b16),
            pltpu.VMEM((WINDOW, HD), b16),
            pltpu.VMEM((HD, WINDOW), b16),
            pltpu.VMEM((WINDOW, HD), f32),
            pltpu.VMEM((WINDOW, HD), f32),
            pltpu.VMEM((WINDOW, wide), b16),
        ],
        out_shape=[
            jax.ShapeDtypeStruct((2, 2 * rows, HD), b16),
            jax.ShapeDtypeStruct((2, 2 * rows, HD), b16),
            jax.ShapeDtypeStruct((runs, HD, wide), b16),
            jax.ShapeDtypeStruct((runs, 1, wide), f32),
            jax.ShapeDtypeStruct((runs, HD, wide), f32),
        ],
        compiler_params=pltpu.CompilerParams(vmem_limit_bytes=VMEM_LIMIT),
        cost_estimate=SMALL,
        name=f"halo_{piece}",
    )(meta, qn, gt, total_own, out_own, doc_own, kv1, array, k_gain)


def key_sum(even, own, swapped, returned):
    f32 = jnp.float32
    return own + returned.astype(f32) + jnp.where(even, swapped.astype(f32), 0.0)


def own_kernel(
    pieces, places, rows, meta, q_gain, qt, qn, k_own, kt_own, v_own, e_own, *refs
):
    f32, b16 = jnp.float32, jnp.bfloat16
    core, even = meta[0], meta[1] == 0
    count = len(pieces)
    inputs, refs = refs[: 3 * count], refs[3 * count :]
    ends, refs = refs[: 2 * len(places)], refs[2 * len(places) :]
    (dq_m, dq_t), outs, (dq_s, dk_s, dv_s) = refs[:2], refs[2:-3], refs[-3:]
    runs, wide = qt.shape[1], qt.shape[-1]
    nt = (((1,), (1,)), ((), ()))
    gain = jnp.broadcast_to(q_gain[...], (HD, HD)).T * qk_scale
    gain = jnp.concatenate([gain] * (wide // HD), axis=1)
    for at, piece in enumerate(pieces):
        g_in, delta_in, dq_in = inputs[3 * at : 3 * at + 3]
        base = runs * (runs + 1) // 2 * HD
        for run in reversed(range(runs)):
            keys = (run + 1) * HD
            base -= keys
            g_l, qn_run = g_in[run], qn[piece, run]
            e = e_own[piece, base : base + keys, :]
            dp = jnp.dot(v_own[piece, :keys, :], g_l, preferred_element_type=f32)
            ds = (e.astype(f32) * (dp - delta_in[run])).astype(b16)
            dv = lax.dot_general(e, g_l, nt, preferred_element_type=f32)
            dk = lax.dot_general(ds, qn_run, nt, preferred_element_type=f32)
            dv_s[:keys, :] = dv if run == runs - 1 else dv_s[:keys, :] + dv
            dk_s[:keys, :] = dk if run == runs - 1 else dk_s[:keys, :] + dk
            dq = dq_in[run] + jnp.dot(kt_own[piece, :, :keys], ds, preferred_element_type=f32)
            q = qt[piece, run].astype(f32)
            r = inverse_rms(q, 0)
            scaled = dq * gain
            dq = r * scaled - q * (r * r * r * jnp.mean(q * scaled, axis=0, keepdims=True))
            slot, inside = divmod(run * HD, rows)
            for head in range(wide // HD):
                lanes = slice(head * HD, (head + 1) * HD)
                columns = slice(at * wide + head * HD, at * wide + (head + 1) * HD)
                dq_s[slot, inside : inside + HD, columns] = dq[:, lanes].T.astype(b16)
        for part in range(2):
            tokens = pl.ds(pl.multiple_of((core if part == 0 else 1 - core) * rows, rows), rows)
            if places:
                swapped, returned = ends[2 * at : 2 * at + 2]
                columns = slice(at * HD, (at + 1) * HD)
                for which, sums in enumerate((dk_s, dv_s)):
                    span = slice(which * rows, (which + 1) * rows)
                    total = key_sum(
                        even, sums[tokens, :], swapped[part, span], returned[places[at], part, span]
                    )
                    outs[part][span, columns] = total.astype(b16)
            else:
                outs[at][part, :rows] = dk_s[tokens, :]
                outs[at][part, rows:] = dv_s[tokens, :]
    dq_m[...] = dq_s[core]
    dq_t[...] = dq_s[1 - core]


def own_keys(pieces, meta, q_gain, prepared, results, ends):
    qt, qn, k_own, kt_own, v_own, e_own = prepared
    rows = k_own.shape[1] // 2
    columns = len(pieces) * qt.shape[-1]
    f32, b16 = jnp.float32, jnp.bfloat16
    vmem = pl.BlockSpec(memory_space=pltpu.VMEM)
    dq = jax.ShapeDtypeStruct((rows, columns), b16)
    own = jax.ShapeDtypeStruct((2, 2 * rows, HD), f32)
    final = jax.ShapeDtypeStruct((2 * rows, len(pieces) * HD), b16)
    flat = [one for result in results for one in result]
    flat += [one for swapped, back in ends for one in (swapped, back[0])]
    places = tuple(back[1] for swapped, back in ends)
    outs = [dq, dq] + ([final] * 2 if ends else [own] * len(pieces))
    return pl.pallas_call(
        functools.partial(own_kernel, tuple(range(len(pieces))), places, rows),
        in_specs=[pl.BlockSpec(memory_space=pltpu.SMEM)] + [vmem] * (7 + len(flat)),
        out_specs=[vmem] * len(outs),
        scratch_shapes=[
            pltpu.VMEM((2, rows, columns), b16),
            pltpu.VMEM((2 * rows, HD), f32),
            pltpu.VMEM((2 * rows, HD), f32),
        ],
        out_shape=outs,
        compiler_params=pltpu.CompilerParams(vmem_limit_bytes=VMEM_LIMIT),
        cost_estimate=pl.CostEstimate(flops=2**32, bytes_accessed=2**22, transcendentals=0),
        name=f"own_{pieces[0]}",
    )(meta, q_gain, *prepared, *flat)


def finish_kernel(places, meta, *refs):
    outs = refs[3 * len(places) :]
    for at, at_returned in enumerate(places):
        own, swapped, returned = refs[3 * at : 3 * at + 3]
        for part in range(2):
            total = key_sum(meta[1] == 0, own[part], swapped[part], returned[at_returned, part])
            outs[part][:, at * HD : (at + 1) * HD] = total.astype(outs[part].dtype)


def finish(meta, owns, ends):
    vmem = pl.BlockSpec(memory_space=pltpu.VMEM)
    shape = jax.ShapeDtypeStruct((owns[0].shape[1], len(owns) * HD), jnp.bfloat16)
    flat = []
    for own, (swapped, back) in zip(owns, ends):
        flat += [own, swapped, back[0]]
    places = tuple(back[1] for swapped, back in ends)
    return pl.pallas_call(
        functools.partial(finish_kernel, places),
        in_specs=[pl.BlockSpec(memory_space=pltpu.SMEM)] + [vmem] * len(flat),
        out_specs=[vmem, vmem],
        out_shape=[shape, shape],
        compiler_params=pltpu.CompilerParams(vmem_limit_bytes=VMEM_LIMIT),
        cost_estimate=SMALL,
        name="finish",
    )(meta, *flat)


def join_query_kernel(count, *refs):
    core = lax.rem(lax.axis_index("ctx"), 2)
    out, sem = refs[2 * count], refs[-1]
    copies = []
    for parts, who in ((refs[:count], core), (refs[count : 2 * count], 1 - core)):
        at = 0
        for part in parts:
            width = part.shape[1]
            columns = pl.ds(pl.multiple_of(who * (out.shape[1] // 2) + at, HD), width)
            copies.append(pltpu.make_async_copy(part, out.at[:, columns], sem.at[len(copies)]))
            at += width
    for copy in copies:
        copy.start()
    for copy in copies:
        copy.wait()


def join_query(mine, theirs):
    width = 2 * sum(part.shape[1] for part in mine)
    vmem = pl.BlockSpec(memory_space=pltpu.VMEM)
    return pl.pallas_call(
        functools.partial(join_query_kernel, len(mine)),
        in_specs=[vmem] * (2 * len(mine)),
        out_specs=pl.BlockSpec(memory_space=pltpu.HBM),
        out_shape=jax.ShapeDtypeStruct((mine[0].shape[0], width), mine[0].dtype),
        scratch_shapes=[pltpu.SemaphoreType.DMA((2 * len(mine),))],
        compiler_params=pltpu.CompilerParams(vmem_limit_bytes=VMEM_LIMIT),
        cost_estimate=SMALL,
        name="join_query",
    )(*mine, *theirs)


def join_key_kernel(count, rows, k_gain, keys, *refs):
    f32 = jnp.float32
    core = lax.rem(lax.axis_index("ctx"), 2)
    key_out, value_out = refs[2 * count :]
    half = key_out.shape[1] // 2
    for parts, who in ((refs[:count], core), (refs[count : 2 * count], 1 - core)):
        at = 0
        for part in parts:
            for head in range(part.shape[1] // HD):
                columns = pl.ds(pl.multiple_of(who * half + at, HD), HD)
                inside = slice(head * HD, (head + 1) * HD)
                k = keys[:, columns].astype(f32)
                r = inverse_rms(k, -1)
                scaled = part[:rows, inside].astype(f32) * k_gain[...]
                grad = r * scaled - k * (r * r * r * jnp.mean(k * scaled, axis=-1, keepdims=True))
                key_out[:, columns] = grad.astype(key_out.dtype)
                value_out[:, columns] = part[rows:, inside]
                at += HD


def join_key(k_gain, keys, mine, theirs):
    rows, width = keys.shape
    vmem = pl.BlockSpec(memory_space=pltpu.VMEM)
    out = jax.ShapeDtypeStruct((rows, width), keys.dtype)
    return pl.pallas_call(
        functools.partial(join_key_kernel, len(mine), rows),
        in_specs=[vmem] * (2 + 2 * len(mine)),
        out_specs=[vmem, vmem],
        out_shape=[out, out],
        compiler_params=pltpu.CompilerParams(vmem_limit_bytes=VMEM_LIMIT),
        cost_estimate=SMALL,
        name="join_key",
    )(k_gain, keys, *mine, *theirs)


def lay_kernel(kv_m, kv_t, *outs):
    place = [(out, at) for out in outs for at in range(out.shape[0])]
    for part, kv in enumerate((kv_m, kv_t)):
        for head, (out, at) in enumerate(place):
            out[at, part] = kv[:, head * HD : (head + 1) * HD]


def lay(kv_m, kv_t):
    shape = lambda count: jax.ShapeDtypeStruct((count, 2, kv_m.shape[0], HD), kv_m.dtype)
    vmem = pl.BlockSpec(memory_space=pltpu.VMEM)
    return pl.pallas_call(
        lay_kernel,
        in_specs=[vmem, vmem],
        out_specs=[vmem] * 3,
        out_shape=[shape(1), shape(1), shape(kv_m.shape[1] // HD - 2)],
        compiler_params=pltpu.CompilerParams(vmem_limit_bytes=VMEM_LIMIT),
        cost_estimate=SMALL,
        name="lay",
    )(kv_m, kv_t)


def after(value, *others):
    return lax.optimization_barrier((value,) + others)[0]


def on_device(queries, keys, values, out_grad, q_gain, k_gain, doc_ids):
    f32, b16 = jnp.float32, jnp.bfloat16
    rows = queries.shape[0]
    half = keys.shape[1] // 2
    pieces = half // HD
    count = lax.axis_size("ctx")
    if WINDOW != 4 * rows or count % 4 != 0:
        raise ValueError("unsupported split")
    rank = lax.axis_index("ctx")
    core = lax.rem(rank, 2)
    parity = lax.rem(lax.div(rank, 2), 2)
    odd = parity == 1
    meta = jnp.stack([core, parity]).astype(jnp.int32)

    core_swap = [(i, i ^ 1) for i in range(count)]
    x_swap = [(i, i ^ 2) for i in range(count)]
    ahead = [(i, i + 4) for i in range(count - 4)]
    back = [(i + 4, i) for i in range(count - 4)]

    def half_of(array, who):
        width = array.shape[1] // 2
        return lax.dynamic_slice(array, (0, who * width), (rows, width))

    def both(one, two, who):
        return jnp.stack([half_of(one, who), half_of(two, who)])

    id_rows = jnp.pad((doc_ids + 1).astype(b16), (0, ID_ROWS - doc_ids.shape[0]))
    id_rows = jnp.broadcast_to(id_rows[:, None], (ID_ROWS, half))

    def pack(who):
        return jnp.concatenate([half_of(keys, who), half_of(values, who), id_rows])

    kv_t = lax.ppermute(pack(1 - core), "ctx", core_swap)
    kv_m = pack(core)

    blocks = lay(kv_m, kv_t)
    kv0, kv1, kv2 = [], [], []
    for block in blocks:
        moved = lax.ppermute(block, "ctx", ahead)
        kv0.extend((block, at) for at in range(block.shape[0]))
        kv2.extend((moved, at) for at in range(block.shape[0]))
    qg_m = both(queries, out_grad, core)
    qg_t = lax.ppermute(both(queries, out_grad, 1 - core), "ctx", core_swap)

    q_gain_row = q_gain.reshape(1, HD)
    k_gain_row = k_gain.reshape(1, HD)
    swapped, joined, returned, results, sums_h2 = [], [], [], [], []

    def x_hop(piece, turn):
        operand = jnp.where(turn, kv2[piece][0][kv2[piece][1]], kv0[piece][0][kv0[piece][1]])
        kv1.append(lax.ppermute(operand, "ctx", x_swap))
        return operand

    def send_back(group, turn):
        block = []
        for piece in group:
            arrived = jnp.where(turn, swapped[piece].astype(f32), 0.0)
            block.append((sums_h2[piece].astype(f32) + arrived).astype(b16))
        joined.append(jnp.stack(block))
        moved = lax.ppermute(joined[-1], "ctx", back)
        returned.extend((moved, at) for at in range(len(group)))

    hop_0 = x_hop(0, odd)
    middle = pieces // 2
    local_part = lambda begin, order: local(
        begin, middle, order, qg_m, qg_t, kv_m, kv_t, q_gain_row, k_gain_row
    )
    prepared = [local_part(0, after(meta, hop_0))]
    order = after(meta, x_hop(1, after(odd, prepared[0][7])))
    for piece in range(pieces):
        if piece == middle:
            prepared.append(local_part(middle, order))
        _, qn, gt, *_, total_own, out_own, doc_own = prepared[piece // middle]
        h1, h2, *result = halo(
            piece % middle, order, qn, gt, total_own, out_own, doc_own, kv1[piece], kv2[piece], k_gain_row
        )
        results.append(result)
        order = after(order, result[1])
        if piece + 2 < pieces:
            order = after(order, x_hop(piece + 2, after(odd, result[1])))
        swapped.append(lax.ppermute(h1, "ctx", x_swap))
        sums_h2.append(h2)
        if piece == 2:
            send_back((0, 1), after(odd, result[1]))
            order = after(order, joined[-1])
        elif piece > 2:
            send_back((piece - 1,), after(odd, result[1]))

    ends = lambda group: [(swapped[i], returned[i]) for i in group]
    late, soon = list(range(middle, pieces)), list(range(middle))

    def own_part(group, order, ends):
        qt, qn, _, k_own, kt_own, v_own, e_own, *_ = prepared[group[0] // middle]
        return own_keys(
            group, order, q_gain_row, (qt, qn, k_own, kt_own, v_own, e_own),
            [results[i] for i in group], ends,
        )

    order = after(order, joined[-1])
    dq_m_late, dq_t_late, *own_late = own_part(late, order, [])
    send_back((pieces - 1,), after(odd, dq_m_late))
    order = after(order, joined[-1], returned[0][0], returned[2][0])
    dq_m_soon, dq_t_soon, kv_m_soon, kv_t_soon = own_part(soon, order, ends(soon))
    swap = lambda array: lax.ppermute(array, "ctx", core_swap)
    query_grad = join_query([dq_m_soon, dq_m_late], [swap(dq_t_soon), swap(dq_t_late)])
    kv_m_late, kv_t_late = finish(order, own_late, ends(late))
    key_grad, value_grad = join_key(
        k_gain_row, keys, [kv_m_soon, kv_m_late], [swap(kv_t_soon), swap(kv_t_late)]
    )
    return (query_grad, key_grad, value_grad)


def solution(mesh):
    split = P(("groups", "ctx"), None)
    in_specs = (split, split, split, split, P(), P(), P(("groups", "ctx")))
    return jax.shard_map(
        on_device, mesh=mesh, in_specs=in_specs, out_specs=(split, split, split), check_vma=False
    )
```

```python
import functools

import jax
import jax.numpy as jnp
from jax import lax
from jax.experimental import pallas as pl
from jax.experimental.pallas import tpu as pltpu
from jax.sharding import PartitionSpec as P

HD = 128
WINDOW = 1024
BLK = 64
ID_ROWS = 16
VMEM_LIMIT = 12 * 1024 * 1024
HIDDEN = -1e30
SMALL = pl.CostEstimate(flops=2**20, bytes_accessed=2**16, transcendentals=0)

qk_scale = 168.0 ** (-0.5)
norm_epsilon = 1e-06


def inverse_rms(values_in, axis):
    return lax.rsqrt(jnp.mean(values_in * values_in, axis=axis, keepdims=True) + norm_epsilon)


def weights(scores, first, diagonal, token, e_ref, base):
    total = jnp.zeros((8, scores.shape[1]), jnp.float32)
    key = lax.broadcasted_iota(jnp.int32, (BLK, scores.shape[1]), 0)
    for at in range(0, scores.shape[0], BLK):
        block = scores[at : at + BLK] + jnp.where(first <= at, 0.0, HIDDEN)
        if diagonal == "window" and at < HD:
            block = jnp.where(key + at > token, block, HIDDEN)
        if diagonal == "causal" and at >= scores.shape[0] - HD:
            block = jnp.where(key + (at - scores.shape[0] + HD) <= token, block, HIDDEN)
        e = jnp.exp(block)
        total = total + jnp.sum(e.reshape(BLK // 8, 8, scores.shape[1]), axis=0)
        e_ref[base + at : base + at + BLK, :] = e.astype(e_ref.dtype)
    return jnp.sum(total, axis=0, keepdims=True)


def local_kernel(
    rows, meta, qg_m, qg_t, kv_m, kv_t, q_gain, k_gain,
    qt, qn, gt, k_own, kt_own, v_own, e_own, total_own, out_own, doc_own,
):
    f32, b16 = jnp.float32, jnp.bfloat16
    core = meta[0]
    wide = qt.shape[-1]
    blocks = rows // BLK
    runs = rows // HD
    gain = jnp.broadcast_to(q_gain[...], (HD, HD)).T * qk_scale
    gain = jnp.concatenate([gain] * (wide // HD), axis=1)
    for part, (qg, kv) in enumerate(((qg_m, kv_m), (qg_t, kv_t))):
        slot = core if part == 0 else 1 - core
        for head in range(wide // HD):
            columns = slice(head * HD, (head + 1) * HD)
            q, g = qg[0, :, columns].T, qg[1, :, columns].T
            for run in range(runs):
                tokens = slice(run * HD, (run + 1) * HD)
                qt[slot * runs + run, :, columns] = q[:, tokens]
                gt[slot * runs + run, :, columns] = g[:, tokens]
        off = pl.multiple_of(slot * rows, rows)
        k = kv[:rows].astype(f32)
        kn = (k * inverse_rms(k, -1) * k_gain[...]).astype(b16)
        k_own[pl.ds(off, rows), :] = kn
        kt_own[:, pl.ds(off, rows)] = kn.T
        v_own[pl.ds(off, rows), :] = kv[rows : 2 * rows]
    token = lax.rem(lax.broadcasted_iota(jnp.int32, (1, wide), 1), HD)
    ids = [[kv[2 * rows :, :1].astype(f32)[b : b + 1] for b in range(blocks)] for kv in (kv_m, kv_t)]
    base = 0
    for run in range(2 * runs):
        slot, inside = divmod(run * HD, rows)
        doc = jnp.zeros((1, wide), f32)
        for b in range(HD // BLK):
            at = inside // BLK + b
            here = jnp.where(core == slot, ids[0][at], ids[1][at])
            doc = jnp.where(token >= b * BLK, here, doc)
        doc_own[run] = doc
        earlier = jnp.zeros((1, wide), f32)
        for one in ids[0] + ids[1]:
            earlier = earlier + (one < doc).astype(f32)
        first = earlier.astype(jnp.int32) * BLK
        q = qt[run].astype(f32)
        qn_run = (q * inverse_rms(q, 0) * gain).astype(b16)
        qn[run] = qn_run
        count = (run + 1) * HD
        s = jnp.dot(k_own[:count, :], qn_run, preferred_element_type=f32)
        total_own[run] = weights(s, first, "causal", token, e_own, base)
        vt = v_own[:count, :].T
        out_own[run] = jnp.dot(vt, e_own[base : base + count, :], preferred_element_type=f32)
        base += count


def local(begin, heads, meta, qg_m, qg_t, kv_m, kv_t, q_gain, k_gain):
    f32, b16 = jnp.float32, jnp.bfloat16
    rows = qg_m.shape[1]
    group_cols = qg_m.shape[2] // (kv_m.shape[1] // HD)
    runs = 2 * rows // HD
    pairs = HD * runs * (runs + 1) // 2
    qg = pl.BlockSpec((2, rows, group_cols), lambda h, meta: (0, 0, begin + h))
    kv = pl.BlockSpec((kv_m.shape[0], HD), lambda h, meta: (0, begin + h))
    row = pl.BlockSpec((1, HD), lambda h, meta: (0, 0))
    out = lambda dtype, *shape: (
        pl.BlockSpec((None,) + shape, lambda h, meta: (h,) + (0,) * len(shape)),
        jax.ShapeDtypeStruct((heads,) + shape, dtype),
    )
    outs = [
        out(b16, runs, HD, group_cols), out(b16, runs, HD, group_cols),
        out(b16, runs, HD, group_cols), out(b16, 2 * rows, HD), out(b16, HD, 2 * rows),
        out(b16, 2 * rows, HD), out(b16, pairs, group_cols), out(f32, runs, 1, group_cols),
        out(f32, runs, HD, group_cols), out(f32, runs, 1, group_cols),
    ]
    return pl.pallas_call(
        functools.partial(local_kernel, rows),
        grid_spec=pltpu.PrefetchScalarGridSpec(
            num_scalar_prefetch=1,
            grid=(heads,),
            in_specs=[qg, qg, kv, kv, row, row],
            out_specs=[one[0] for one in outs],
        ),
        out_shape=[one[1] for one in outs],
        compiler_params=pltpu.CompilerParams(vmem_limit_bytes=VMEM_LIMIT),
        cost_estimate=SMALL,
        name=f"local_{begin}",
    )(meta, qg_m, qg_t, kv_m, kv_t, q_gain, k_gain)


def halo_kernel(
    piece, at, rows, meta, qn, gt, total_own, out_own, doc_own, kv1, kv2, k_gain,
    h1, h2, g_out, delta_out, dq_out,
    k_s, kt_s, v_s, vt_s, dk_s, dv_s, e_s,
):
    f32, b16 = jnp.float32, jnp.bfloat16
    core = meta[0]
    wide = qn.shape[-1]
    blocks = rows // BLK
    sources = ((kv2.at[at], 0), (kv1, 2 * rows))

    for source, base in sources:
        for part in range(2):
            off = pl.multiple_of(base + (core if part == 0 else 1 - core) * rows, rows)
            k = source[part, :rows].astype(f32)
            kn = (k * inverse_rms(k, -1) * k_gain[...]).astype(b16)
            k_s[pl.ds(off, rows), :] = kn
            kt_s[:, pl.ds(off, rows)] = kn.T
            v = source[part, rows : 2 * rows]
            v_s[pl.ds(off, rows), :] = v
            vt_s[:, pl.ds(off, rows)] = v.T

    token = lax.rem(lax.broadcasted_iota(jnp.int32, (1, wide), 1), HD)
    nt = (((1,), (1,)), ((), ()))
    ids = [
        source[part, 2 * rows :, :1].astype(f32)[b : b + 1]
        for source, base in sources
        for part in range(2)
        for b in range(blocks)
    ]
    for run in range(2 * rows // HD):
        low = run * HD
        doc = doc_own[piece, run]
        earlier = jnp.zeros((1, wide), f32)
        for one in ids:
            earlier = earlier + (one < doc).astype(f32)
        first = earlier.astype(jnp.int32) * BLK - low
        qn_run = qn[piece, run]
        s = jnp.dot(k_s[low:, :], qn_run, preferred_element_type=f32)
        total = total_own[piece, run] + weights(s, first, "window", token, e_s, low)
        e = e_s[low:, :]
        out = out_own[piece, run] + jnp.dot(vt_s[:, low:], e, preferred_element_type=f32)
        inverse = 1.0 / total
        g_l = (gt[piece, run].astype(f32) * inverse).astype(b16)
        delta = jnp.sum(g_l.astype(f32) * (out * inverse), axis=0, keepdims=True)
        g_out[run] = g_l
        delta_out[run] = delta
        dp = jnp.dot(v_s[low:, :], g_l, preferred_element_type=f32)
        ds = (e.astype(f32) * (dp - delta)).astype(b16)
        dv = lax.dot_general(e, g_l, nt, preferred_element_type=f32)
        dk = lax.dot_general(ds, qn_run, nt, preferred_element_type=f32)
        dv_s[low:, :] = dv if run == 0 else dv_s[low:, :] + dv
        dk_s[low:, :] = dk if run == 0 else dk_s[low:, :] + dk
        dq_out[run] = jnp.dot(kt_s[:, low:], ds, preferred_element_type=f32)

    for target, base in ((h2, 0), (h1, 2 * rows)):
        for part in range(2):
            off = pl.multiple_of(base + (core if part == 0 else 1 - core) * rows, rows)
            target[part, :rows] = dk_s[pl.ds(off, rows), :].astype(b16)
            target[part, rows:] = dv_s[pl.ds(off, rows), :].astype(b16)


def halo(piece, meta, qn, gt, total_own, out_own, doc_own, kv1, kv2, k_gain):
    array, at = kv2
    rows = (array.shape[2] - ID_ROWS) // 2
    runs, wide = qn.shape[1], qn.shape[-1]
    f32, b16 = jnp.float32, jnp.bfloat16
    vmem = pl.BlockSpec(memory_space=pltpu.VMEM)
    return pl.pallas_call(
        functools.partial(halo_kernel, piece, at, rows),
        in_specs=[pl.BlockSpec(memory_space=pltpu.SMEM)] + [vmem] * 8,
        out_specs=[vmem] * 5,
        scratch_shapes=[
            pltpu.VMEM((WINDOW, HD), b16),
            pltpu.VMEM((HD, WINDOW), b16),
            pltpu.VMEM((WINDOW, HD), b16),
            pltpu.VMEM((HD, WINDOW), b16),
            pltpu.VMEM((WINDOW, HD), f32),
            pltpu.VMEM((WINDOW, HD), f32),
            pltpu.VMEM((WINDOW, wide), b16),
        ],
        out_shape=[
            jax.ShapeDtypeStruct((2, 2 * rows, HD), b16),
            jax.ShapeDtypeStruct((2, 2 * rows, HD), b16),
            jax.ShapeDtypeStruct((runs, HD, wide), b16),
            jax.ShapeDtypeStruct((runs, 1, wide), f32),
            jax.ShapeDtypeStruct((runs, HD, wide), f32),
        ],
        compiler_params=pltpu.CompilerParams(vmem_limit_bytes=VMEM_LIMIT),
        cost_estimate=SMALL,
        name=f"halo_{piece}",
    )(meta, qn, gt, total_own, out_own, doc_own, kv1, array, k_gain)


def key_sum(even, own, swapped, returned):
    f32 = jnp.float32
    return own + returned.astype(f32) + jnp.where(even, swapped.astype(f32), 0.0)


def own_kernel(
    pieces, places, rows, meta, q_gain, qt, qn, k_own, kt_own, v_own, e_own, *refs
):
    f32, b16 = jnp.float32, jnp.bfloat16
    core, even = meta[0], meta[1] == 0
    count = len(pieces)
    inputs, refs = refs[: 3 * count], refs[3 * count :]
    ends, refs = refs[: 2 * len(places)], refs[2 * len(places) :]
    (dq_m, dq_t), outs, (dq_s, dk_s, dv_s) = refs[:2], refs[2:-3], refs[-3:]
    runs, wide = qt.shape[1], qt.shape[-1]
    nt = (((1,), (1,)), ((), ()))
    gain = jnp.broadcast_to(q_gain[...], (HD, HD)).T * qk_scale
    gain = jnp.concatenate([gain] * (wide // HD), axis=1)
    for at, piece in enumerate(pieces):
        g_in, delta_in, dq_in = inputs[3 * at : 3 * at + 3]
        base = runs * (runs + 1) // 2 * HD
        for run in reversed(range(runs)):
            keys = (run + 1) * HD
            base -= keys
            g_l, qn_run = g_in[run], qn[piece, run]
            e = e_own[piece, base : base + keys, :]
            dp = jnp.dot(v_own[piece, :keys, :], g_l, preferred_element_type=f32)
            ds = (e.astype(f32) * (dp - delta_in[run])).astype(b16)
            dv = lax.dot_general(e, g_l, nt, preferred_element_type=f32)
            dk = lax.dot_general(ds, qn_run, nt, preferred_element_type=f32)
            dv_s[:keys, :] = dv if run == runs - 1 else dv_s[:keys, :] + dv
            dk_s[:keys, :] = dk if run == runs - 1 else dk_s[:keys, :] + dk
            dq = dq_in[run] + jnp.dot(kt_own[piece, :, :keys], ds, preferred_element_type=f32)
            q = qt[piece, run].astype(f32)
            r = inverse_rms(q, 0)
            scaled = dq * gain
            dq = r * scaled - q * (r * r * r * jnp.mean(q * scaled, axis=0, keepdims=True))
            slot, inside = divmod(run * HD, rows)
            for head in range(wide // HD):
                lanes = slice(head * HD, (head + 1) * HD)
                columns = slice(at * wide + head * HD, at * wide + (head + 1) * HD)
                dq_s[slot, inside : inside + HD, columns] = dq[:, lanes].T.astype(b16)
        for part in range(2):
            tokens = pl.ds(pl.multiple_of((core if part == 0 else 1 - core) * rows, rows), rows)
            if places:
                swapped, returned = ends[2 * at : 2 * at + 2]
                columns = slice(at * HD, (at + 1) * HD)
                for which, sums in enumerate((dk_s, dv_s)):
                    span = slice(which * rows, (which + 1) * rows)
                    total = key_sum(
                        even, sums[tokens, :], swapped[part, span], returned[places[at], part, span]
                    )
                    outs[part][span, columns] = total.astype(b16)
            else:
                outs[at][part, :rows] = dk_s[tokens, :]
                outs[at][part, rows:] = dv_s[tokens, :]
    dq_m[...] = dq_s[core]
    dq_t[...] = dq_s[1 - core]


def own_keys(pieces, meta, q_gain, prepared, results, ends):
    qt, qn, k_own, kt_own, v_own, e_own = prepared
    rows = k_own.shape[1] // 2
    columns = len(pieces) * qt.shape[-1]
    f32, b16 = jnp.float32, jnp.bfloat16
    vmem = pl.BlockSpec(memory_space=pltpu.VMEM)
    dq = jax.ShapeDtypeStruct((rows, columns), b16)
    own = jax.ShapeDtypeStruct((2, 2 * rows, HD), f32)
    final = jax.ShapeDtypeStruct((2 * rows, len(pieces) * HD), b16)
    flat = [one for result in results for one in result]
    flat += [one for swapped, back in ends for one in (swapped, back[0])]
    places = tuple(back[1] for swapped, back in ends)
    outs = [dq, dq] + ([final] * 2 if ends else [own] * len(pieces))
    return pl.pallas_call(
        functools.partial(own_kernel, tuple(range(len(pieces))), places, rows),
        in_specs=[pl.BlockSpec(memory_space=pltpu.SMEM)] + [vmem] * (7 + len(flat)),
        out_specs=[vmem] * len(outs),
        scratch_shapes=[
            pltpu.VMEM((2, rows, columns), b16),
            pltpu.VMEM((2 * rows, HD), f32),
            pltpu.VMEM((2 * rows, HD), f32),
        ],
        out_shape=outs,
        compiler_params=pltpu.CompilerParams(vmem_limit_bytes=VMEM_LIMIT),
        cost_estimate=pl.CostEstimate(flops=2**32, bytes_accessed=2**22, transcendentals=0),
        name=f"own_{pieces[0]}",
    )(meta, q_gain, *prepared, *flat)


def finish_kernel(places, meta, *refs):
    outs = refs[3 * len(places) :]
    for at, at_returned in enumerate(places):
        own, swapped, returned = refs[3 * at : 3 * at + 3]
        for part in range(2):
            total = key_sum(meta[1] == 0, own[part], swapped[part], returned[at_returned, part])
            outs[part][:, at * HD : (at + 1) * HD] = total.astype(outs[part].dtype)


def finish(meta, owns, ends):
    vmem = pl.BlockSpec(memory_space=pltpu.VMEM)
    shape = jax.ShapeDtypeStruct((owns[0].shape[1], len(owns) * HD), jnp.bfloat16)
    flat = []
    for own, (swapped, back) in zip(owns, ends):
        flat += [own, swapped, back[0]]
    places = tuple(back[1] for swapped, back in ends)
    return pl.pallas_call(
        functools.partial(finish_kernel, places),
        in_specs=[pl.BlockSpec(memory_space=pltpu.SMEM)] + [vmem] * len(flat),
        out_specs=[vmem, vmem],
        out_shape=[shape, shape],
        compiler_params=pltpu.CompilerParams(vmem_limit_bytes=VMEM_LIMIT),
        cost_estimate=SMALL,
        name="finish",
    )(meta, *flat)


def join_query_kernel(count, *refs):
    core = lax.rem(lax.axis_index("ctx"), 2)
    out, sem = refs[2 * count], refs[-1]
    copies = []
    for parts, who in ((refs[:count], core), (refs[count : 2 * count], 1 - core)):
        at = 0
        for part in parts:
            width = part.shape[1]
            columns = pl.ds(pl.multiple_of(who * (out.shape[1] // 2) + at, HD), width)
            copies.append(pltpu.make_async_copy(part, out.at[:, columns], sem.at[len(copies)]))
            at += width
    for copy in copies:
        copy.start()
    for copy in copies:
        copy.wait()


def join_query(mine, theirs):
    width = 2 * sum(part.shape[1] for part in mine)
    vmem = pl.BlockSpec(memory_space=pltpu.VMEM)
    return pl.pallas_call(
        functools.partial(join_query_kernel, len(mine)),
        in_specs=[vmem] * (2 * len(mine)),
        out_specs=pl.BlockSpec(memory_space=pltpu.HBM),
        out_shape=jax.ShapeDtypeStruct((mine[0].shape[0], width), mine[0].dtype),
        scratch_shapes=[pltpu.SemaphoreType.DMA((2 * len(mine),))],
        compiler_params=pltpu.CompilerParams(vmem_limit_bytes=VMEM_LIMIT),
        cost_estimate=SMALL,
        name="join_query",
    )(*mine, *theirs)


def join_key_kernel(count, rows, k_gain, keys, *refs):
    f32 = jnp.float32
    core = lax.rem(lax.axis_index("ctx"), 2)
    key_out, value_out = refs[2 * count :]
    half = key_out.shape[1] // 2
    for parts, who in ((refs[:count], core), (refs[count : 2 * count], 1 - core)):
        at = 0
        for part in parts:
            for head in range(part.shape[1] // HD):
                columns = pl.ds(pl.multiple_of(who * half + at, HD), HD)
                inside = slice(head * HD, (head + 1) * HD)
                k = keys[:, columns].astype(f32)
                r = inverse_rms(k, -1)
                scaled = part[:rows, inside].astype(f32) * k_gain[...]
                grad = r * scaled - k * (r * r * r * jnp.mean(k * scaled, axis=-1, keepdims=True))
                key_out[:, columns] = grad.astype(key_out.dtype)
                value_out[:, columns] = part[rows:, inside]
                at += HD


def join_key(k_gain, keys, mine, theirs):
    rows, width = keys.shape
    vmem = pl.BlockSpec(memory_space=pltpu.VMEM)
    out = jax.ShapeDtypeStruct((rows, width), keys.dtype)
    return pl.pallas_call(
        functools.partial(join_key_kernel, len(mine), rows),
        in_specs=[vmem] * (2 + 2 * len(mine)),
        out_specs=[vmem, vmem],
        out_shape=[out, out],
        compiler_params=pltpu.CompilerParams(vmem_limit_bytes=VMEM_LIMIT),
        cost_estimate=SMALL,
        name="join_key",
    )(k_gain, keys, *mine, *theirs)


def lay_kernel(kv_m, kv_t, *outs):
    place = [(out, at) for out in outs for at in range(out.shape[0])]
    for part, kv in enumerate((kv_m, kv_t)):
        for head, (out, at) in enumerate(place):
            out[at, part] = kv[:, head * HD : (head + 1) * HD]


def lay(kv_m, kv_t):
    shape = lambda count: jax.ShapeDtypeStruct((count, 2, kv_m.shape[0], HD), kv_m.dtype)
    vmem = pl.BlockSpec(memory_space=pltpu.VMEM)
    return pl.pallas_call(
        lay_kernel,
        in_specs=[vmem, vmem],
        out_specs=[vmem] * (kv_m.shape[1] // HD),
        out_shape=[shape(1)] * (kv_m.shape[1] // HD),
        compiler_params=pltpu.CompilerParams(vmem_limit_bytes=VMEM_LIMIT),
        cost_estimate=SMALL,
        name="lay",
    )(kv_m, kv_t)


def after(value, *others):
    return lax.optimization_barrier((value,) + others)[0]


def on_device(queries, keys, values, out_grad, q_gain, k_gain, doc_ids):
    f32, b16 = jnp.float32, jnp.bfloat16
    rows = queries.shape[0]
    half = keys.shape[1] // 2
    pieces = half // HD
    count = lax.axis_size("ctx")
    if WINDOW != 4 * rows or count % 4 != 0:
        raise ValueError("unsupported split")
    rank = lax.axis_index("ctx")
    core = lax.rem(rank, 2)
    parity = lax.rem(lax.div(rank, 2), 2)
    odd = parity == 1
    meta = jnp.stack([core, parity]).astype(jnp.int32)

    core_swap = [(i, i ^ 1) for i in range(count)]
    x_swap = [(i, i ^ 2) for i in range(count)]
    ahead = [(i, i + 4) for i in range(count - 4)]
    back = [(i + 4, i) for i in range(count - 4)]

    def half_of(array, who):
        width = array.shape[1] // 2
        return lax.dynamic_slice(array, (0, who * width), (rows, width))

    def both(one, two, who):
        return jnp.stack([half_of(one, who), half_of(two, who)])

    id_rows = jnp.pad((doc_ids + 1).astype(b16), (0, ID_ROWS - doc_ids.shape[0]))
    id_rows = jnp.broadcast_to(id_rows[:, None], (ID_ROWS, half))

    def pack(who):
        return jnp.concatenate([half_of(keys, who), half_of(values, who), id_rows])

    kv_t = lax.ppermute(pack(1 - core), "ctx", core_swap)
    kv_m = pack(core)

    kv0 = lay(kv_m, kv_t)
    kv1, kv2 = [], []
    for block in kv0[:-1]:
        kv2.append((lax.ppermute(block, "ctx", ahead), 0))
    neighbour = lax.ppermute(kv0[-1], "ctx", x_swap)
    qg_m = both(queries, out_grad, core)
    qg_t = lax.ppermute(both(queries, out_grad, 1 - core), "ctx", core_swap)

    q_gain_row = q_gain.reshape(1, HD)
    k_gain_row = k_gain.reshape(1, HD)
    swapped, joined, returned, results, sums_h2 = [], [], [], [], []

    def x_hop(piece, turn):
        operand = jnp.where(turn, kv2[piece][0][0], kv0[piece][0])
        kv1.append(lax.ppermute(operand, "ctx", x_swap))
        return operand

    def far_hop(turn):
        theirs = after(neighbour, turn)
        block = jnp.concatenate([kv0[-1], theirs])
        moved = lax.ppermute(block, "ctx", ahead)
        kv2.append((moved, 0))
        kv1.append(jnp.where(odd, theirs[0], moved[1]))
        return block

    def send_back(group, turn):
        block = []
        for piece in group:
            arrived = jnp.where(turn, swapped[piece].astype(f32), 0.0)
            block.append((sums_h2[piece].astype(f32) + arrived).astype(b16))
        joined.append(jnp.stack(block))
        moved = lax.ppermute(joined[-1], "ctx", back)
        returned.extend((moved, at) for at in range(len(group)))

    hop_0 = x_hop(0, odd)
    middle = pieces // 2
    local_part = lambda begin, order: local(
        begin, middle, order, qg_m, qg_t, kv_m, kv_t, q_gain_row, k_gain_row
    )
    prepared = [local_part(0, after(meta, hop_0, neighbour))]
    order = after(meta, x_hop(1, after(odd, prepared[0][7])))
    for piece in range(pieces):
        if piece == middle:
            prepared.append(local_part(middle, order))
        _, qn, gt, *_, total_own, out_own, doc_own = prepared[piece // middle]
        h1, h2, *result = halo(
            piece % middle, order, qn, gt, total_own, out_own, doc_own, kv1[piece], kv2[piece], k_gain_row
        )
        results.append(result)
        order = after(order, result[1])
        if piece + 3 < pieces:
            order = after(order, x_hop(piece + 2, after(odd, result[1])), far_hop(result[1]))
        swapped.append(lax.ppermute(h1, "ctx", x_swap))
        sums_h2.append(h2)
        if piece == 2:
            send_back((0, 1), after(odd, result[1]))
            order = after(order, joined[-1])
        elif piece > 2:
            send_back((piece - 1,), after(odd, result[1]))

    ends = lambda group: [(swapped[i], returned[i]) for i in group]
    late, soon = list(range(middle, pieces)), list(range(middle))

    def own_part(group, order, ends):
        qt, qn, _, k_own, kt_own, v_own, e_own, *_ = prepared[group[0] // middle]
        return own_keys(
            group, order, q_gain_row, (qt, qn, k_own, kt_own, v_own, e_own),
            [results[i] for i in group], ends,
        )

    order = after(order, joined[-1])
    dq_m_late, dq_t_late, *own_late = own_part(late, order, [])
    send_back((pieces - 1,), after(odd, dq_m_late))
    order = after(order, joined[-1], returned[0][0], returned[2][0])
    dq_m_soon, dq_t_soon, kv_m_soon, kv_t_soon = own_part(soon, order, ends(soon))
    swap = lambda array: lax.ppermute(array, "ctx", core_swap)
    query_grad = join_query([dq_m_soon, dq_m_late], [swap(dq_t_soon), swap(dq_t_late)])
    kv_m_late, kv_t_late = finish(order, own_late, ends(late))
    key_grad, value_grad = join_key(
        k_gain_row, keys, [kv_m_soon, kv_m_late], [swap(kv_t_soon), swap(kv_t_late)]
    )
    return (query_grad, key_grad, value_grad)


def solution(mesh):
    split = P(("groups", "ctx"), None)
    in_specs = (split, split, split, split, P(), P(), P(("groups", "ctx")))
    return jax.shard_map(
        on_device, mesh=mesh, in_specs=in_specs, out_specs=(split, split, split), check_vma=False
    )
```

```python
import functools

import jax
import jax.numpy as jnp
from jax import lax
from jax.experimental import pallas as pl
from jax.experimental.pallas import tpu as pltpu
from jax.sharding import PartitionSpec as P

HD = 128
WINDOW = 1024
BLK = 64
ID_ROWS = 16
VMEM_LIMIT = 12 * 1024 * 1024
HIDDEN = -1e30
SMALL = pl.CostEstimate(flops=2**20, bytes_accessed=2**16, transcendentals=0)

qk_scale = 168.0 ** (-0.5)
norm_epsilon = 1e-06


def inverse_rms(values_in, axis):
    return lax.rsqrt(jnp.mean(values_in * values_in, axis=axis, keepdims=True) + norm_epsilon)


def weights(scores, first, diagonal, token, e_ref, base):
    total = jnp.zeros((8, scores.shape[1]), jnp.float32)
    key = lax.broadcasted_iota(jnp.int32, (BLK, scores.shape[1]), 0)
    for at in range(0, scores.shape[0], BLK):
        block = scores[at : at + BLK] + jnp.where(first <= at, 0.0, HIDDEN)
        if diagonal == "window" and at < HD:
            block = jnp.where(key + at > token, block, HIDDEN)
        if diagonal == "causal" and at >= scores.shape[0] - HD:
            block = jnp.where(key + (at - scores.shape[0] + HD) <= token, block, HIDDEN)
        e = jnp.exp(block)
        total = total + jnp.sum(e.reshape(BLK // 8, 8, scores.shape[1]), axis=0)
        e_ref[base + at : base + at + BLK, :] = e.astype(e_ref.dtype)
    return jnp.sum(total, axis=0, keepdims=True)


def local_kernel(
    rows, meta, q_m, g_m, k_m, v_m, ids_m, q_t, g_t, k_t, v_t, ids_t, q_gain, k_gain,
    qt, qn, gt, k_own, kt_own, v_own, e_own, total_own, out_own, doc_own,
):
    f32, b16 = jnp.float32, jnp.bfloat16
    core = meta[0]
    wide = qt.shape[-1]
    blocks = rows // BLK
    runs = rows // HD
    gain = jnp.broadcast_to(q_gain[...], (HD, HD)).T * qk_scale
    gain = jnp.concatenate([gain] * (wide // HD), axis=1)
    sides = ((q_m, g_m, k_m, v_m), (q_t, g_t, k_t, v_t))
    for part, (q_ref, g_ref, k_ref, v_ref) in enumerate(sides):
        slot = core if part == 0 else 1 - core
        for head in range(wide // HD):
            columns = slice(head * HD, (head + 1) * HD)
            q, g = q_ref[:, columns].T, g_ref[:, columns].T
            for run in range(runs):
                tokens = slice(run * HD, (run + 1) * HD)
                qt[slot * runs + run, :, columns] = q[:, tokens]
                gt[slot * runs + run, :, columns] = g[:, tokens]
        off = pl.multiple_of(slot * rows, rows)
        k = k_ref[...].astype(f32)
        kn = (k * inverse_rms(k, -1) * k_gain[...]).astype(b16)
        k_own[pl.ds(off, rows), :] = kn
        kt_own[:, pl.ds(off, rows)] = kn.T
        v_own[pl.ds(off, rows), :] = v_ref[...]
    token = lax.rem(lax.broadcasted_iota(jnp.int32, (1, wide), 1), HD)
    ids = [[one[:, :1].astype(f32)[b : b + 1] for b in range(blocks)] for one in (ids_m, ids_t)]
    base = 0
    for run in range(2 * runs):
        slot, inside = divmod(run * HD, rows)
        doc = jnp.zeros((1, wide), f32)
        for b in range(HD // BLK):
            at = inside // BLK + b
            here = jnp.where(core == slot, ids[0][at], ids[1][at])
            doc = jnp.where(token >= b * BLK, here, doc)
        doc_own[run] = doc
        earlier = jnp.zeros((1, wide), f32)
        for one in ids[0] + ids[1]:
            earlier = earlier + (one < doc).astype(f32)
        first = earlier.astype(jnp.int32) * BLK
        q = qt[run].astype(f32)
        qn_run = (q * inverse_rms(q, 0) * gain).astype(b16)
        qn[run] = qn_run
        count = (run + 1) * HD
        s = jnp.dot(k_own[:count, :], qn_run, preferred_element_type=f32)
        total_own[run] = weights(s, first, "causal", token, e_own, base)
        vt = v_own[:count, :].T
        out_own[run] = jnp.dot(vt, e_own[base : base + count, :], preferred_element_type=f32)
        base += count


def local(begin, heads, meta, mine, theirs, q_gain, k_gain):
    f32, b16 = jnp.float32, jnp.bfloat16
    rows, q_columns = mine[0].shape
    group_cols = q_columns // (mine[2].shape[1] // HD)
    runs = 2 * rows // HD
    pairs = HD * runs * (runs + 1) // 2
    qg = pl.BlockSpec((rows, group_cols), lambda h, meta: (0, begin + h))
    kv = pl.BlockSpec((rows, HD), lambda h, meta: (0, begin + h))
    ids = pl.BlockSpec((ID_ROWS, HD), lambda h, meta: (0, 0))
    row = pl.BlockSpec((1, HD), lambda h, meta: (0, 0))
    out = lambda dtype, *shape: (
        pl.BlockSpec((None,) + shape, lambda h, meta: (h,) + (0,) * len(shape)),
        jax.ShapeDtypeStruct((heads,) + shape, dtype),
    )
    outs = [
        out(b16, runs, HD, group_cols), out(b16, runs, HD, group_cols),
        out(b16, runs, HD, group_cols), out(b16, 2 * rows, HD), out(b16, HD, 2 * rows),
        out(b16, 2 * rows, HD), out(b16, pairs, group_cols), out(f32, runs, 1, group_cols),
        out(f32, runs, HD, group_cols), out(f32, runs, 1, group_cols),
    ]
    return pl.pallas_call(
        functools.partial(local_kernel, rows),
        grid_spec=pltpu.PrefetchScalarGridSpec(
            num_scalar_prefetch=1,
            grid=(heads,),
            in_specs=[qg, qg, kv, kv, ids] * 2 + [row, row],
            out_specs=[one[0] for one in outs],
        ),
        out_shape=[one[1] for one in outs],
        compiler_params=pltpu.CompilerParams(vmem_limit_bytes=VMEM_LIMIT),
        cost_estimate=SMALL,
        name=f"local_{begin}",
    )(meta, *mine, *theirs, q_gain, k_gain)


def halo_kernel(
    piece, at, rows, meta, qn, gt, total_own, out_own, doc_own, kv1, kv2, k_gain,
    h1, h2, g_out, delta_out, dq_out,
    k_s, kt_s, v_s, vt_s, dk_s, dv_s, e_s,
):
    f32, b16 = jnp.float32, jnp.bfloat16
    core = meta[0]
    wide = qn.shape[-1]
    blocks = rows // BLK
    sources = ((kv2.at[at], 0), (kv1, 2 * rows))

    for source, base in sources:
        for part in range(2):
            off = pl.multiple_of(base + (core if part == 0 else 1 - core) * rows, rows)
            k = source[part, :rows].astype(f32)
            kn = (k * inverse_rms(k, -1) * k_gain[...]).astype(b16)
            k_s[pl.ds(off, rows), :] = kn
            kt_s[:, pl.ds(off, rows)] = kn.T
            v = source[part, rows : 2 * rows]
            v_s[pl.ds(off, rows), :] = v
            vt_s[:, pl.ds(off, rows)] = v.T

    token = lax.rem(lax.broadcasted_iota(jnp.int32, (1, wide), 1), HD)
    nt = (((1,), (1,)), ((), ()))
    ids = [
        source[part, 2 * rows :, :1].astype(f32)[b : b + 1]
        for source, base in sources
        for part in range(2)
        for b in range(blocks)
    ]
    for run in range(2 * rows // HD):
        low = run * HD
        doc = doc_own[piece, run]
        earlier = jnp.zeros((1, wide), f32)
        for one in ids:
            earlier = earlier + (one < doc).astype(f32)
        first = earlier.astype(jnp.int32) * BLK - low
        qn_run = qn[piece, run]
        s = jnp.dot(k_s[low:, :], qn_run, preferred_element_type=f32)
        total = total_own[piece, run] + weights(s, first, "window", token, e_s, low)
        e = e_s[low:, :]
        out = out_own[piece, run] + jnp.dot(vt_s[:, low:], e, preferred_element_type=f32)
        inverse = 1.0 / total
        g_l = (gt[piece, run].astype(f32) * inverse).astype(b16)
        delta = jnp.sum(g_l.astype(f32) * (out * inverse), axis=0, keepdims=True)
        g_out[run] = g_l
        delta_out[run] = delta
        dp = jnp.dot(v_s[low:, :], g_l, preferred_element_type=f32)
        ds = (e.astype(f32) * (dp - delta)).astype(b16)
        dv = lax.dot_general(e, g_l, nt, preferred_element_type=f32)
        dk = lax.dot_general(ds, qn_run, nt, preferred_element_type=f32)
        dv_s[low:, :] = dv if run == 0 else dv_s[low:, :] + dv
        dk_s[low:, :] = dk if run == 0 else dk_s[low:, :] + dk
        dq_out[run] = jnp.dot(kt_s[:, low:], ds, preferred_element_type=f32)

    for target, base in ((h2, 0), (h1, 2 * rows)):
        for part in range(2):
            off = pl.multiple_of(base + (core if part == 0 else 1 - core) * rows, rows)
            target[part, :rows] = dk_s[pl.ds(off, rows), :].astype(b16)
            target[part, rows:] = dv_s[pl.ds(off, rows), :].astype(b16)


def halo(piece, meta, qn, gt, total_own, out_own, doc_own, kv1, kv2, k_gain):
    array, at = kv2
    rows = (array.shape[-2] - ID_ROWS) // 2
    runs, wide = qn.shape[1], qn.shape[-1]
    f32, b16 = jnp.float32, jnp.bfloat16
    vmem = pl.BlockSpec(memory_space=pltpu.VMEM)
    return pl.pallas_call(
        functools.partial(halo_kernel, piece, at, rows),
        in_specs=[pl.BlockSpec(memory_space=pltpu.SMEM)] + [vmem] * 8,
        out_specs=[vmem] * 5,
        scratch_shapes=[
            pltpu.VMEM((WINDOW, HD), b16),
            pltpu.VMEM((HD, WINDOW), b16),
            pltpu.VMEM((WINDOW, HD), b16),
            pltpu.VMEM((HD, WINDOW), b16),
            pltpu.VMEM((WINDOW, HD), f32),
            pltpu.VMEM((WINDOW, HD), f32),
            pltpu.VMEM((WINDOW, wide), b16),
        ],
        out_shape=[
            jax.ShapeDtypeStruct((2, 2 * rows, HD), b16),
            jax.ShapeDtypeStruct((2, 2 * rows, HD), b16),
            jax.ShapeDtypeStruct((runs, HD, wide), b16),
            jax.ShapeDtypeStruct((runs, 1, wide), f32),
            jax.ShapeDtypeStruct((runs, HD, wide), f32),
        ],
        compiler_params=pltpu.CompilerParams(vmem_limit_bytes=VMEM_LIMIT),
        cost_estimate=SMALL,
        name=f"halo_{piece}",
    )(meta, qn, gt, total_own, out_own, doc_own, kv1, array, k_gain)


def key_sum(even, own, swapped, returned):
    f32 = jnp.float32
    return own + returned.astype(f32) + jnp.where(even, swapped.astype(f32), 0.0)


def own_kernel(
    pieces, places, rows, meta, q_gain, qt, qn, k_own, kt_own, v_own, e_own, *refs
):
    f32, b16 = jnp.float32, jnp.bfloat16
    core, even = meta[0], meta[1] == 0
    count = len(pieces)
    inputs, refs = refs[: 3 * count], refs[3 * count :]
    ends, refs = refs[: 2 * len(places)], refs[2 * len(places) :]
    (dq_m, dq_t), outs, (dq_s, dk_s, dv_s) = refs[:2], refs[2:-3], refs[-3:]
    runs, wide = qt.shape[1], qt.shape[-1]
    nt = (((1,), (1,)), ((), ()))
    gain = jnp.broadcast_to(q_gain[...], (HD, HD)).T * qk_scale
    gain = jnp.concatenate([gain] * (wide // HD), axis=1)
    for at, piece in enumerate(pieces):
        g_in, delta_in, dq_in = inputs[3 * at : 3 * at + 3]
        base = runs * (runs + 1) // 2 * HD
        for run in reversed(range(runs)):
            keys = (run + 1) * HD
            base -= keys
            g_l, qn_run = g_in[run], qn[piece, run]
            e = e_own[piece, base : base + keys, :]
            dp = jnp.dot(v_own[piece, :keys, :], g_l, preferred_element_type=f32)
            ds = (e.astype(f32) * (dp - delta_in[run])).astype(b16)
            dv = lax.dot_general(e, g_l, nt, preferred_element_type=f32)
            dk = lax.dot_general(ds, qn_run, nt, preferred_element_type=f32)
            dv_s[:keys, :] = dv if run == runs - 1 else dv_s[:keys, :] + dv
            dk_s[:keys, :] = dk if run == runs - 1 else dk_s[:keys, :] + dk
            dq = dq_in[run] + jnp.dot(kt_own[piece, :, :keys], ds, preferred_element_type=f32)
            q = qt[piece, run].astype(f32)
            r = inverse_rms(q, 0)
            scaled = dq * gain
            dq = r * scaled - q * (r * r * r * jnp.mean(q * scaled, axis=0, keepdims=True))
            slot, inside = divmod(run * HD, rows)
            for head in range(wide // HD):
                lanes = slice(head * HD, (head + 1) * HD)
                columns = slice(at * wide + head * HD, at * wide + (head + 1) * HD)
                dq_s[slot, inside : inside + HD, columns] = dq[:, lanes].T.astype(b16)
        for part in range(2):
            tokens = pl.ds(pl.multiple_of((core if part == 0 else 1 - core) * rows, rows), rows)
            if places:
                swapped, returned = ends[2 * at : 2 * at + 2]
                columns = slice(at * HD, (at + 1) * HD)
                for which, sums in enumerate((dk_s, dv_s)):
                    span = slice(which * rows, (which + 1) * rows)
                    total = key_sum(
                        even, sums[tokens, :], swapped[part, span], returned[places[at], part, span]
                    )
                    outs[part][span, columns] = total.astype(b16)
            else:
                outs[at][part, :rows] = dk_s[tokens, :]
                outs[at][part, rows:] = dv_s[tokens, :]
    dq_m[...] = dq_s[core]
    dq_t[...] = dq_s[1 - core]


def own_keys(pieces, meta, q_gain, prepared, results, ends):
    qt, qn, k_own, kt_own, v_own, e_own = prepared
    rows = k_own.shape[1] // 2
    columns = len(pieces) * qt.shape[-1]
    f32, b16 = jnp.float32, jnp.bfloat16
    vmem = pl.BlockSpec(memory_space=pltpu.VMEM)
    dq = jax.ShapeDtypeStruct((rows, columns), b16)
    own = jax.ShapeDtypeStruct((2, 2 * rows, HD), f32)
    final = jax.ShapeDtypeStruct((2 * rows, len(pieces) * HD), b16)
    flat = [one for result in results for one in result]
    flat += [one for swapped, back in ends for one in (swapped, back[0])]
    places = tuple(back[1] for swapped, back in ends)
    outs = [dq, dq] + ([final] * 2 if ends else [own] * len(pieces))
    return pl.pallas_call(
        functools.partial(own_kernel, tuple(range(len(pieces))), places, rows),
        in_specs=[pl.BlockSpec(memory_space=pltpu.SMEM)] + [vmem] * (7 + len(flat)),
        out_specs=[vmem] * len(outs),
        scratch_shapes=[
            pltpu.VMEM((2, rows, columns), b16),
            pltpu.VMEM((2 * rows, HD), f32),
            pltpu.VMEM((2 * rows, HD), f32),
        ],
        out_shape=outs,
        compiler_params=pltpu.CompilerParams(vmem_limit_bytes=VMEM_LIMIT),
        cost_estimate=pl.CostEstimate(flops=2**32, bytes_accessed=2**22, transcendentals=0),
        name=f"own_{pieces[0]}",
    )(meta, q_gain, *prepared, *flat)


def finish_kernel(places, meta, *refs):
    outs = refs[3 * len(places) :]
    for at, at_returned in enumerate(places):
        own, swapped, returned = refs[3 * at : 3 * at + 3]
        for part in range(2):
            total = key_sum(meta[1] == 0, own[part], swapped[part], returned[at_returned, part])
            outs[part][:, at * HD : (at + 1) * HD] = total.astype(outs[part].dtype)


def finish(meta, owns, ends):
    vmem = pl.BlockSpec(memory_space=pltpu.VMEM)
    shape = jax.ShapeDtypeStruct((owns[0].shape[1], len(owns) * HD), jnp.bfloat16)
    flat = []
    for own, (swapped, back) in zip(owns, ends):
        flat += [own, swapped, back[0]]
    places = tuple(back[1] for swapped, back in ends)
    return pl.pallas_call(
        functools.partial(finish_kernel, places),
        in_specs=[pl.BlockSpec(memory_space=pltpu.SMEM)] + [vmem] * len(flat),
        out_specs=[vmem, vmem],
        out_shape=[shape, shape],
        compiler_params=pltpu.CompilerParams(vmem_limit_bytes=VMEM_LIMIT),
        cost_estimate=SMALL,
        name="finish",
    )(meta, *flat)


def join_query_kernel(count, *refs):
    core = lax.rem(lax.axis_index("ctx"), 2)
    out, sem = refs[2 * count], refs[-1]
    copies = []
    for parts, who in ((refs[:count], core), (refs[count : 2 * count], 1 - core)):
        at = 0
        for part in parts:
            width = part.shape[1]
            columns = pl.ds(pl.multiple_of(who * (out.shape[1] // 2) + at, HD), width)
            copies.append(pltpu.make_async_copy(part, out.at[:, columns], sem.at[len(copies)]))
            at += width
    for copy in copies:
        copy.start()
    for copy in copies:
        copy.wait()


def join_query(mine, theirs):
    width = 2 * sum(part.shape[1] for part in mine)
    vmem = pl.BlockSpec(memory_space=pltpu.VMEM)
    return pl.pallas_call(
        functools.partial(join_query_kernel, len(mine)),
        in_specs=[vmem] * (2 * len(mine)),
        out_specs=pl.BlockSpec(memory_space=pltpu.HBM),
        out_shape=jax.ShapeDtypeStruct((mine[0].shape[0], width), mine[0].dtype),
        scratch_shapes=[pltpu.SemaphoreType.DMA((2 * len(mine),))],
        compiler_params=pltpu.CompilerParams(vmem_limit_bytes=VMEM_LIMIT),
        cost_estimate=SMALL,
        name="join_query",
    )(*mine, *theirs)


def join_key_kernel(count, rows, k_gain, keys, *refs):
    f32 = jnp.float32
    core = lax.rem(lax.axis_index("ctx"), 2)
    key_out, value_out = refs[2 * count :]
    half = key_out.shape[1] // 2
    for parts, who in ((refs[:count], core), (refs[count : 2 * count], 1 - core)):
        at = 0
        for part in parts:
            for head in range(part.shape[1] // HD):
                columns = pl.ds(pl.multiple_of(who * half + at, HD), HD)
                inside = slice(head * HD, (head + 1) * HD)
                k = keys[:, columns].astype(f32)
                r = inverse_rms(k, -1)
                scaled = part[:rows, inside].astype(f32) * k_gain[...]
                grad = r * scaled - k * (r * r * r * jnp.mean(k * scaled, axis=-1, keepdims=True))
                key_out[:, columns] = grad.astype(key_out.dtype)
                value_out[:, columns] = part[rows:, inside]
                at += HD


def join_key(k_gain, keys, mine, theirs):
    rows, width = keys.shape
    vmem = pl.BlockSpec(memory_space=pltpu.VMEM)
    out = jax.ShapeDtypeStruct((rows, width), keys.dtype)
    return pl.pallas_call(
        functools.partial(join_key_kernel, len(mine), rows),
        in_specs=[vmem] * (2 + 2 * len(mine)),
        out_specs=[vmem, vmem],
        out_shape=[out, out],
        compiler_params=pltpu.CompilerParams(vmem_limit_bytes=VMEM_LIMIT),
        cost_estimate=SMALL,
        name="join_key",
    )(k_gain, keys, *mine, *theirs)


def lay_kernel(k_m, v_m, ids_m, k_t, v_t, ids_t, *outs):
    rows = k_m.shape[0]
    for part, (k, v, ids) in enumerate(((k_m, v_m, ids_m), (k_t, v_t, ids_t))):
        place = [(out, at) for out in outs for at in range(out.shape[0])]
        for head, (out, at) in enumerate(place):
            columns = slice(head * HD, (head + 1) * HD)
            out[at, part, :rows] = k[:, columns]
            out[at, part, rows : 2 * rows] = v[:, columns]
            out[at, part, 2 * rows :] = ids[...]


def lay(mine, theirs):
    rows, columns = mine[0].shape
    shape = lambda count: jax.ShapeDtypeStruct((count, 2, 2 * rows + ID_ROWS, HD), mine[0].dtype)
    counts = [2] + [1] * (columns // HD - 2)
    vmem = pl.BlockSpec(memory_space=pltpu.VMEM)
    return pl.pallas_call(
        lay_kernel,
        in_specs=[vmem] * 6,
        out_specs=[vmem] * len(counts),
        out_shape=[shape(count) for count in counts],
        compiler_params=pltpu.CompilerParams(vmem_limit_bytes=VMEM_LIMIT),
        cost_estimate=SMALL,
        name="lay",
    )(*mine, *theirs)


def after(value, *others):
    return lax.optimization_barrier((value,) + others)[0]


def on_device(queries, keys, values, out_grad, q_gain, k_gain, doc_ids):
    f32, b16 = jnp.float32, jnp.bfloat16
    rows = queries.shape[0]
    half = keys.shape[1] // 2
    pieces = half // HD
    count = lax.axis_size("ctx")
    if WINDOW != 4 * rows or count % 4 != 0:
        raise ValueError("unsupported split")
    rank = lax.axis_index("ctx")
    core = lax.rem(rank, 2)
    parity = lax.rem(lax.div(rank, 2), 2)
    odd = parity == 1
    meta = jnp.stack([core, parity]).astype(jnp.int32)

    core_swap = [(i, i ^ 1) for i in range(count)]
    x_swap = [(i, i ^ 2) for i in range(count)]
    ahead = [(i, i + 4) for i in range(count - 4)]
    back = [(i + 4, i) for i in range(count - 4)]

    def half_of(array, who):
        width = array.shape[1] // 2
        return lax.dynamic_slice(array, (0, who * width), (rows, width))

    id_rows = jnp.pad((doc_ids + 1).astype(b16), (0, ID_ROWS - doc_ids.shape[0]))
    id_rows = jnp.broadcast_to(id_rows[:, None], (ID_ROWS, HD))
    swap = lambda array: lax.ppermute(array, "ctx", core_swap)
    arrays = (queries, out_grad, keys, values)
    q_m, g_m, k_m, v_m = (half_of(array, core) for array in arrays)
    q_t, g_t, k_t, v_t = (swap(half_of(array, 1 - core)) for array in arrays)
    ids_t = swap(id_rows)

    far = pieces - 2
    pair, *single = lay((k_m, v_m, id_rows), (k_t, v_t, ids_t))
    kv0 = [(pair, 0), (pair, 1)] + [(block, 0) for block in single]
    kv1, kv2 = {}, {}
    moved = lax.ppermute(pair, "ctx", ahead)
    kv2[0], kv2[1] = (moved, 0), (moved, 1)
    neighbour = lax.ppermute(kv0[far][0], "ctx", x_swap)
    for piece in range(2, pieces):
        if piece != far:
            kv2[piece] = (lax.ppermute(kv0[piece][0], "ctx", ahead), 0)

    q_gain_row = q_gain.reshape(1, HD)
    k_gain_row = k_gain.reshape(1, HD)

    swapped, joined, returned, results, sums_h2 = [], [], [], [], []

    def x_hop(piece, turn):
        operand = jnp.where(turn, kv2[piece][0][kv2[piece][1]], kv0[piece][0][kv0[piece][1]])
        kv1[piece] = lax.ppermute(operand, "ctx", x_swap)
        return operand

    def far_hop(turn):
        theirs = after(neighbour, turn)
        block = jnp.concatenate([kv0[far][0], theirs])
        moved = lax.ppermute(block, "ctx", ahead)
        kv2[far] = (moved, 0)
        kv1[far] = jnp.where(odd, theirs[0], moved[1])
        return block

    def send_back(group, turn):
        block = []
        for piece in group:
            arrived = jnp.where(turn, swapped[piece].astype(f32), 0.0)
            block.append((sums_h2[piece].astype(f32) + arrived).astype(b16))
        joined.append(jnp.stack(block))
        moved = lax.ppermute(joined[-1], "ctx", back)
        returned.extend((moved, at) for at in range(len(group)))

    middle = pieces // 2
    local_part = lambda begin, order: local(
        begin, middle, order, (q_m, g_m, k_m, v_m, id_rows), (q_t, g_t, k_t, v_t, ids_t),
        q_gain_row, k_gain_row,
    )
    prepared = [local_part(0, meta)]
    far_block = far_hop(prepared[0][7])
    hop_0 = x_hop(0, after(odd, far_block))
    hop_1 = x_hop(1, after(odd, hop_0))
    prepared.append(local_part(middle, after(meta, hop_1)))
    order = after(meta, prepared[1][7])
    for piece in range(pieces):
        _, qn, gt, *_, total_own, out_own, doc_own = prepared[piece // middle]
        h1, h2, *result = halo(
            piece % middle, order, qn, gt, total_own, out_own, doc_own, kv1[piece], kv2[piece], k_gain_row
        )
        results.append(result)
        order = after(order, result[1])
        if piece == 1:
            order = after(order, x_hop(pieces - 1, after(odd, result[1])))
        swapped.append(lax.ppermute(h1, "ctx", x_swap))
        sums_h2.append(h2)
        if piece == 2:
            send_back((0, 1), after(odd, result[1]))
            order = after(order, joined[-1])
        elif piece > 2:
            send_back((piece - 1,), after(odd, result[1]))

    ends = lambda group: [(swapped[i], returned[i]) for i in group]
    late, soon = list(range(middle, pieces)), list(range(middle))

    def own_part(group, order, ends):
        qt, qn, _, k_own, kt_own, v_own, e_own, *_ = prepared[group[0] // middle]
        return own_keys(
            group, order, q_gain_row, (qt, qn, k_own, kt_own, v_own, e_own),
            [results[i] for i in group], ends,
        )

    order = after(order, joined[-1])
    dq_m_late, dq_t_late, *own_late = own_part(late, order, [])
    send_back((pieces - 1,), after(odd, dq_m_late))
    order = after(order, joined[-1], returned[0][0], returned[2][0])
    dq_m_soon, dq_t_soon, kv_m_soon, kv_t_soon = own_part(soon, order, ends(soon))
    query_grad = join_query([dq_m_soon, dq_m_late], [swap(dq_t_soon), swap(dq_t_late)])
    kv_m_late, kv_t_late = finish(order, own_late, ends(late))
    key_grad, value_grad = join_key(
        k_gain_row, keys, [kv_m_soon, kv_m_late], [swap(kv_t_soon), swap(kv_t_late)]
    )
    return (query_grad, key_grad, value_grad)


def solution(mesh):
    split = P(("groups", "ctx"), None)
    in_specs = (split, split, split, split, P(), P(), P(("groups", "ctx")))
    return jax.shard_map(
        on_device, mesh=mesh, in_specs=in_specs, out_specs=(split, split, split), check_vma=False
    )
```

```python
import functools

import jax
import jax.numpy as jnp
from jax import lax
from jax.experimental import pallas as pl
from jax.experimental.pallas import tpu as pltpu
from jax.sharding import PartitionSpec as P

HD = 128
WINDOW = 1024
BLK = 64
ID_ROWS = 16
VMEM_LIMIT = 12 * 1024 * 1024
HIDDEN = -1e30
SMALL = pl.CostEstimate(flops=2**20, bytes_accessed=2**16, transcendentals=0)

qk_scale = 168.0 ** (-0.5)
norm_epsilon = 1e-06


def inverse_rms(values_in, axis):
    return lax.rsqrt(jnp.mean(values_in * values_in, axis=axis, keepdims=True) + norm_epsilon)


def weights(scores, first, diagonal, token, e_ref, base):
    total = jnp.zeros((8, scores.shape[1]), jnp.float32)
    key = lax.broadcasted_iota(jnp.int32, (BLK, scores.shape[1]), 0)
    for at in range(0, scores.shape[0], BLK):
        block = scores[at : at + BLK] + jnp.where(first <= at, 0.0, HIDDEN)
        if diagonal == "window" and at < HD:
            block = jnp.where(key + at > token, block, HIDDEN)
        if diagonal == "causal" and at >= scores.shape[0] - HD:
            block = jnp.where(key + (at - scores.shape[0] + HD) <= token, block, HIDDEN)
        e = jnp.exp(block)
        total = total + jnp.sum(e.reshape(BLK // 8, 8, scores.shape[1]), axis=0)
        e_ref[base + at : base + at + BLK, :] = e.astype(e_ref.dtype)
    return jnp.sum(total, axis=0, keepdims=True)


def local_kernel(
    rows, meta, q_m, g_m, qg_t, kv_m, kv_t, q_gain, k_gain,
    qt, qn, gt, k_own, kt_own, v_own, e_own, total_own, out_own, doc_own,
):
    f32, b16 = jnp.float32, jnp.bfloat16
    core = meta[0]
    wide = qt.shape[-1]
    blocks = rows // BLK
    runs = rows // HD
    gain = jnp.broadcast_to(q_gain[...], (HD, HD)).T * qk_scale
    gain = jnp.concatenate([gain] * (wide // HD), axis=1)
    sides = ((q_m, g_m, kv_m), (qg_t.at[0], qg_t.at[1], kv_t))
    for part, (q_ref, g_ref, kv) in enumerate(sides):
        slot = core if part == 0 else 1 - core
        for head in range(wide // HD):
            columns = slice(head * HD, (head + 1) * HD)
            q, g = q_ref[:, columns].T, g_ref[:, columns].T
            for run in range(runs):
                tokens = slice(run * HD, (run + 1) * HD)
                qt[slot * runs + run, :, columns] = q[:, tokens]
                gt[slot * runs + run, :, columns] = g[:, tokens]
        off = pl.multiple_of(slot * rows, rows)
        k = kv[:rows].astype(f32)
        kn = (k * inverse_rms(k, -1) * k_gain[...]).astype(b16)
        k_own[pl.ds(off, rows), :] = kn
        kt_own[:, pl.ds(off, rows)] = kn.T
        v_own[pl.ds(off, rows), :] = kv[rows : 2 * rows]
    token = lax.rem(lax.broadcasted_iota(jnp.int32, (1, wide), 1), HD)
    ids = [[kv[2 * rows :, :1].astype(f32)[b : b + 1] for b in range(blocks)] for kv in (kv_m, kv_t)]
    base = 0
    for run in range(2 * runs):
        slot, inside = divmod(run * HD, rows)
        doc = jnp.zeros((1, wide), f32)
        for b in range(HD // BLK):
            at = inside // BLK + b
            here = jnp.where(core == slot, ids[0][at], ids[1][at])
            doc = jnp.where(token >= b * BLK, here, doc)
        doc_own[run] = doc
        earlier = jnp.zeros((1, wide), f32)
        for one in ids[0] + ids[1]:
            earlier = earlier + (one < doc).astype(f32)
        first = earlier.astype(jnp.int32) * BLK
        q = qt[run].astype(f32)
        qn_run = (q * inverse_rms(q, 0) * gain).astype(b16)
        qn[run] = qn_run
        count = (run + 1) * HD
        s = jnp.dot(k_own[:count, :], qn_run, preferred_element_type=f32)
        total_own[run] = weights(s, first, "causal", token, e_own, base)
        vt = v_own[:count, :].T
        out_own[run] = jnp.dot(vt, e_own[base : base + count, :], preferred_element_type=f32)
        base += count


def local(begin, heads, meta, q_m, g_m, qg_t, kv_m, kv_t, q_gain, k_gain):
    f32, b16 = jnp.float32, jnp.bfloat16
    rows, q_columns = q_m.shape
    group_cols = q_columns // (kv_m.shape[1] // HD)
    runs = 2 * rows // HD
    pairs = HD * runs * (runs + 1) // 2
    qg = pl.BlockSpec((2, rows, group_cols), lambda h, meta: (0, 0, begin + h))
    q_mine = pl.BlockSpec((rows, group_cols), lambda h, meta: (0, begin + h))
    kv = pl.BlockSpec((kv_m.shape[0], HD), lambda h, meta: (0, begin + h))
    row = pl.BlockSpec((1, HD), lambda h, meta: (0, 0))
    out = lambda dtype, *shape: (
        pl.BlockSpec((None,) + shape, lambda h, meta: (h,) + (0,) * len(shape)),
        jax.ShapeDtypeStruct((heads,) + shape, dtype),
    )
    outs = [
        out(b16, runs, HD, group_cols), out(b16, runs, HD, group_cols),
        out(b16, runs, HD, group_cols), out(b16, 2 * rows, HD), out(b16, HD, 2 * rows),
        out(b16, 2 * rows, HD), out(b16, pairs, group_cols), out(f32, runs, 1, group_cols),
        out(f32, runs, HD, group_cols), out(f32, runs, 1, group_cols),
    ]
    return pl.pallas_call(
        functools.partial(local_kernel, rows),
        grid_spec=pltpu.PrefetchScalarGridSpec(
            num_scalar_prefetch=1,
            grid=(heads,),
            in_specs=[q_mine, q_mine, qg, kv, kv, row, row],
            out_specs=[one[0] for one in outs],
        ),
        out_shape=[one[1] for one in outs],
        compiler_params=pltpu.CompilerParams(vmem_limit_bytes=VMEM_LIMIT),
        cost_estimate=SMALL,
        name=f"local_{begin}",
    )(meta, q_m, g_m, qg_t, kv_m, kv_t, q_gain, k_gain)


def halo_kernel(
    piece, at, rows, meta, qn, gt, total_own, out_own, doc_own, kv1, kv2, k_gain,
    h1, h2, g_out, delta_out, dq_out,
    k_s, kt_s, v_s, vt_s, dk_s, dv_s, e_s,
):
    f32, b16 = jnp.float32, jnp.bfloat16
    core = meta[0]
    wide = qn.shape[-1]
    blocks = rows // BLK
    sources = ((kv2.at[at], 0), (kv1, 2 * rows))

    for source, base in sources:
        for part in range(2):
            off = pl.multiple_of(base + (core if part == 0 else 1 - core) * rows, rows)
            k = source[part, :rows].astype(f32)
            kn = (k * inverse_rms(k, -1) * k_gain[...]).astype(b16)
            k_s[pl.ds(off, rows), :] = kn
            kt_s[:, pl.ds(off, rows)] = kn.T
            v = source[part, rows : 2 * rows]
            v_s[pl.ds(off, rows), :] = v
            vt_s[:, pl.ds(off, rows)] = v.T

    token = lax.rem(lax.broadcasted_iota(jnp.int32, (1, wide), 1), HD)
    nt = (((1,), (1,)), ((), ()))
    ids = [
        source[part, 2 * rows :, :1].astype(f32)[b : b + 1]
        for source, base in sources
        for part in range(2)
        for b in range(blocks)
    ]
    for run in range(2 * rows // HD):
        low = run * HD
        doc = doc_own[piece, run]
        earlier = jnp.zeros((1, wide), f32)
        for one in ids:
            earlier = earlier + (one < doc).astype(f32)
        first = earlier.astype(jnp.int32) * BLK - low
        qn_run = qn[piece, run]
        s = jnp.dot(k_s[low:, :], qn_run, preferred_element_type=f32)
        total = total_own[piece, run] + weights(s, first, "window", token, e_s, low)
        e = e_s[low:, :]
        out = out_own[piece, run] + jnp.dot(vt_s[:, low:], e, preferred_element_type=f32)
        inverse = 1.0 / total
        g_l = (gt[piece, run].astype(f32) * inverse).astype(b16)
        delta = jnp.sum(g_l.astype(f32) * (out * inverse), axis=0, keepdims=True)
        g_out[run] = g_l
        delta_out[run] = delta
        dp = jnp.dot(v_s[low:, :], g_l, preferred_element_type=f32)
        ds = (e.astype(f32) * (dp - delta)).astype(b16)
        dv = lax.dot_general(e, g_l, nt, preferred_element_type=f32)
        dk = lax.dot_general(ds, qn_run, nt, preferred_element_type=f32)
        dv_s[low:, :] = dv if run == 0 else dv_s[low:, :] + dv
        dk_s[low:, :] = dk if run == 0 else dk_s[low:, :] + dk
        dq_out[run] = jnp.dot(kt_s[:, low:], ds, preferred_element_type=f32)

    for target, base in ((h2, 0), (h1, 2 * rows)):
        for part in range(2):
            off = pl.multiple_of(base + (core if part == 0 else 1 - core) * rows, rows)
            target[part, :rows] = dk_s[pl.ds(off, rows), :].astype(b16)
            target[part, rows:] = dv_s[pl.ds(off, rows), :].astype(b16)


def halo(piece, meta, qn, gt, total_own, out_own, doc_own, kv1, kv2, k_gain):
    array, at = kv2
    rows = (array.shape[2] - ID_ROWS) // 2
    runs, wide = qn.shape[1], qn.shape[-1]
    f32, b16 = jnp.float32, jnp.bfloat16
    vmem = pl.BlockSpec(memory_space=pltpu.VMEM)
    return pl.pallas_call(
        functools.partial(halo_kernel, piece, at, rows),
        in_specs=[pl.BlockSpec(memory_space=pltpu.SMEM)] + [vmem] * 8,
        out_specs=[vmem] * 5,
        scratch_shapes=[
            pltpu.VMEM((WINDOW, HD), b16),
            pltpu.VMEM((HD, WINDOW), b16),
            pltpu.VMEM((WINDOW, HD), b16),
            pltpu.VMEM((HD, WINDOW), b16),
            pltpu.VMEM((WINDOW, HD), f32),
            pltpu.VMEM((WINDOW, HD), f32),
            pltpu.VMEM((WINDOW, wide), b16),
        ],
        out_shape=[
            jax.ShapeDtypeStruct((2, 2 * rows, HD), b16),
            jax.ShapeDtypeStruct((2, 2 * rows, HD), b16),
            jax.ShapeDtypeStruct((runs, HD, wide), b16),
            jax.ShapeDtypeStruct((runs, 1, wide), f32),
            jax.ShapeDtypeStruct((runs, HD, wide), f32),
        ],
        compiler_params=pltpu.CompilerParams(vmem_limit_bytes=VMEM_LIMIT),
        cost_estimate=SMALL,
        name=f"halo_{piece}",
    )(meta, qn, gt, total_own, out_own, doc_own, kv1, array, k_gain)


def key_sum(even, own, swapped, returned):
    f32 = jnp.float32
    return own + returned.astype(f32) + jnp.where(even, swapped.astype(f32), 0.0)


def own_kernel(
    pieces, places, rows, meta, q_gain, qt, qn, k_own, kt_own, v_own, e_own, *refs
):
    f32, b16 = jnp.float32, jnp.bfloat16
    core, even = meta[0], meta[1] == 0
    count = len(pieces)
    inputs, refs = refs[: 3 * count], refs[3 * count :]
    ends, refs = refs[: 2 * len(places)], refs[2 * len(places) :]
    (dq_m, dq_t), outs, (dq_s, dk_s, dv_s) = refs[:2], refs[2:-3], refs[-3:]
    runs, wide = qt.shape[1], qt.shape[-1]
    nt = (((1,), (1,)), ((), ()))
    gain = jnp.broadcast_to(q_gain[...], (HD, HD)).T * qk_scale
    gain = jnp.concatenate([gain] * (wide // HD), axis=1)
    for at, piece in enumerate(pieces):
        g_in, delta_in, dq_in = inputs[3 * at : 3 * at + 3]
        base = runs * (runs + 1) // 2 * HD
        for run in reversed(range(runs)):
            keys = (run + 1) * HD
            base -= keys
            g_l, qn_run = g_in[run], qn[piece, run]
            e = e_own[piece, base : base + keys, :]
            dp = jnp.dot(v_own[piece, :keys, :], g_l, preferred_element_type=f32)
            ds = (e.astype(f32) * (dp - delta_in[run])).astype(b16)
            dv = lax.dot_general(e, g_l, nt, preferred_element_type=f32)
            dk = lax.dot_general(ds, qn_run, nt, preferred_element_type=f32)
            dv_s[:keys, :] = dv if run == runs - 1 else dv_s[:keys, :] + dv
            dk_s[:keys, :] = dk if run == runs - 1 else dk_s[:keys, :] + dk
            dq = dq_in[run] + jnp.dot(kt_own[piece, :, :keys], ds, preferred_element_type=f32)
            q = qt[piece, run].astype(f32)
            r = inverse_rms(q, 0)
            scaled = dq * gain
            dq = r * scaled - q * (r * r * r * jnp.mean(q * scaled, axis=0, keepdims=True))
            slot, inside = divmod(run * HD, rows)
            for head in range(wide // HD):
                lanes = slice(head * HD, (head + 1) * HD)
                columns = slice(at * wide + head * HD, at * wide + (head + 1) * HD)
                dq_s[slot, inside : inside + HD, columns] = dq[:, lanes].T.astype(b16)
        for part in range(2):
            tokens = pl.ds(pl.multiple_of((core if part == 0 else 1 - core) * rows, rows), rows)
            if places:
                swapped, returned = ends[2 * at : 2 * at + 2]
                columns = slice(at * HD, (at + 1) * HD)
                for which, sums in enumerate((dk_s, dv_s)):
                    span = slice(which * rows, (which + 1) * rows)
                    total = key_sum(
                        even, sums[tokens, :], swapped[part, span], returned[places[at], part, span]
                    )
                    outs[part][span, columns] = total.astype(b16)
            else:
                outs[at][part, :rows] = dk_s[tokens, :]
                outs[at][part, rows:] = dv_s[tokens, :]
    dq_m[...] = dq_s[core]
    dq_t[...] = dq_s[1 - core]


def own_keys(pieces, meta, q_gain, prepared, results, ends):
    qt, qn, k_own, kt_own, v_own, e_own = prepared
    rows = k_own.shape[1] // 2
    columns = len(pieces) * qt.shape[-1]
    f32, b16 = jnp.float32, jnp.bfloat16
    vmem = pl.BlockSpec(memory_space=pltpu.VMEM)
    dq = jax.ShapeDtypeStruct((rows, columns), b16)
    own = jax.ShapeDtypeStruct((2, 2 * rows, HD), f32)
    final = jax.ShapeDtypeStruct((2 * rows, len(pieces) * HD), b16)
    flat = [one for result in results for one in result]
    flat += [one for swapped, back in ends for one in (swapped, back[0])]
    places = tuple(back[1] for swapped, back in ends)
    outs = [dq, dq] + ([final] * 2 if ends else [own] * len(pieces))
    return pl.pallas_call(
        functools.partial(own_kernel, tuple(range(len(pieces))), places, rows),
        in_specs=[pl.BlockSpec(memory_space=pltpu.SMEM)] + [vmem] * (7 + len(flat)),
        out_specs=[vmem] * len(outs),
        scratch_shapes=[
            pltpu.VMEM((2, rows, columns), b16),
            pltpu.VMEM((2 * rows, HD), f32),
            pltpu.VMEM((2 * rows, HD), f32),
        ],
        out_shape=outs,
        compiler_params=pltpu.CompilerParams(vmem_limit_bytes=VMEM_LIMIT),
        cost_estimate=pl.CostEstimate(flops=2**32, bytes_accessed=2**22, transcendentals=0)
        if ends else SMALL,
        name=f"own_{pieces[0]}",
    )(meta, q_gain, *prepared, *flat)


def finish_kernel(places, meta, *refs):
    outs = refs[3 * len(places) :]
    for at, at_returned in enumerate(places):
        own, swapped, returned = refs[3 * at : 3 * at + 3]
        for part in range(2):
            total = key_sum(meta[1] == 0, own[part], swapped[part], returned[at_returned, part])
            outs[part][:, at * HD : (at + 1) * HD] = total.astype(outs[part].dtype)


def finish(meta, owns, ends):
    vmem = pl.BlockSpec(memory_space=pltpu.VMEM)
    shape = jax.ShapeDtypeStruct((owns[0].shape[1], len(owns) * HD), jnp.bfloat16)
    flat = []
    for own, (swapped, back) in zip(owns, ends):
        flat += [own, swapped, back[0]]
    places = tuple(back[1] for swapped, back in ends)
    return pl.pallas_call(
        functools.partial(finish_kernel, places),
        in_specs=[pl.BlockSpec(memory_space=pltpu.SMEM)] + [vmem] * len(flat),
        out_specs=[vmem, vmem],
        out_shape=[shape, shape],
        compiler_params=pltpu.CompilerParams(vmem_limit_bytes=VMEM_LIMIT),
        cost_estimate=SMALL,
        name="finish",
    )(meta, *flat)


def join_query_kernel(count, *refs):
    core = lax.rem(lax.axis_index("ctx"), 2)
    out, sem = refs[2 * count], refs[-1]
    copies = []
    for parts, who in ((refs[:count], core), (refs[count : 2 * count], 1 - core)):
        at = 0
        for part in parts:
            width = part.shape[1]
            columns = pl.ds(pl.multiple_of(who * (out.shape[1] // 2) + at, HD), width)
            copies.append(pltpu.make_async_copy(part, out.at[:, columns], sem.at[len(copies)]))
            at += width
    for copy in copies:
        copy.start()
    for copy in copies:
        copy.wait()


def join_query(mine, theirs):
    width = 2 * sum(part.shape[1] for part in mine)
    vmem = pl.BlockSpec(memory_space=pltpu.VMEM)
    return pl.pallas_call(
        functools.partial(join_query_kernel, len(mine)),
        in_specs=[vmem] * (2 * len(mine)),
        out_specs=pl.BlockSpec(memory_space=pltpu.HBM),
        out_shape=jax.ShapeDtypeStruct((mine[0].shape[0], width), mine[0].dtype),
        scratch_shapes=[pltpu.SemaphoreType.DMA((2 * len(mine),))],
        compiler_params=pltpu.CompilerParams(vmem_limit_bytes=VMEM_LIMIT),
        cost_estimate=SMALL,
        name="join_query",
    )(*mine, *theirs)


def join_key_kernel(count, rows, k_gain, keys, *refs):
    f32 = jnp.float32
    core = lax.rem(lax.axis_index("ctx"), 2)
    key_out, value_out = refs[2 * count :]
    half = key_out.shape[1] // 2
    for parts, who in ((refs[:count], core), (refs[count : 2 * count], 1 - core)):
        at = 0
        for part in parts:
            for head in range(part.shape[1] // HD):
                columns = pl.ds(pl.multiple_of(who * half + at, HD), HD)
                inside = slice(head * HD, (head + 1) * HD)
                k = keys[:, columns].astype(f32)
                r = inverse_rms(k, -1)
                scaled = part[:rows, inside].astype(f32) * k_gain[...]
                grad = r * scaled - k * (r * r * r * jnp.mean(k * scaled, axis=-1, keepdims=True))
                key_out[:, columns] = grad.astype(key_out.dtype)
                value_out[:, columns] = part[rows:, inside]
                at += HD


def join_key(k_gain, keys, mine, theirs):
    rows, width = keys.shape
    vmem = pl.BlockSpec(memory_space=pltpu.VMEM)
    out = jax.ShapeDtypeStruct((rows, width), keys.dtype)
    return pl.pallas_call(
        functools.partial(join_key_kernel, len(mine), rows),
        in_specs=[vmem] * (2 + 2 * len(mine)),
        out_specs=[vmem, vmem],
        out_shape=[out, out],
        compiler_params=pltpu.CompilerParams(vmem_limit_bytes=VMEM_LIMIT),
        cost_estimate=SMALL,
        name="join_key",
    )(k_gain, keys, *mine, *theirs)


def lay_kernel(kv_m, kv_t, *outs):
    place = [(out, at) for out in outs for at in range(out.shape[0])]
    for part, kv in enumerate((kv_m, kv_t)):
        for head, (out, at) in enumerate(place):
            out[at, part] = kv[:, head * HD : (head + 1) * HD]


def lay(kv_m, kv_t):
    shape = lambda count: jax.ShapeDtypeStruct((count, 2, kv_m.shape[0], HD), kv_m.dtype)
    vmem = pl.BlockSpec(memory_space=pltpu.VMEM)
    return pl.pallas_call(
        lay_kernel,
        in_specs=[vmem, vmem],
        out_specs=[vmem] * (kv_m.shape[1] // HD),
        out_shape=[shape(1)] * (kv_m.shape[1] // HD),
        compiler_params=pltpu.CompilerParams(vmem_limit_bytes=VMEM_LIMIT),
        cost_estimate=SMALL,
        name="lay",
    )(kv_m, kv_t)


def after(value, *others):
    return lax.optimization_barrier((value,) + others)[0]


def on_device(queries, keys, values, out_grad, q_gain, k_gain, doc_ids):
    f32, b16 = jnp.float32, jnp.bfloat16
    rows = queries.shape[0]
    half = keys.shape[1] // 2
    pieces = half // HD
    count = lax.axis_size("ctx")
    if WINDOW != 4 * rows or count % 4 != 0:
        raise ValueError("unsupported split")
    rank = lax.axis_index("ctx")
    core = lax.rem(rank, 2)
    parity = lax.rem(lax.div(rank, 2), 2)
    odd = parity == 1
    meta = jnp.stack([core, parity]).astype(jnp.int32)

    core_swap = [(i, i ^ 1) for i in range(count)]
    x_swap = [(i, i ^ 2) for i in range(count)]
    ahead = [(i, i + 4) for i in range(count - 4)]
    back = [(i + 4, i) for i in range(count - 4)]

    def half_of(array, who):
        width = array.shape[1] // 2
        return lax.dynamic_slice(array, (0, who * width), (rows, width))

    def both(one, two, who):
        return jnp.stack([half_of(one, who), half_of(two, who)])

    id_rows = jnp.pad((doc_ids + 1).astype(b16), (0, ID_ROWS - doc_ids.shape[0]))
    id_rows = jnp.broadcast_to(id_rows[:, None], (ID_ROWS, half))

    def pack(who):
        return jnp.concatenate([half_of(keys, who), half_of(values, who), id_rows])

    kv_t = lax.ppermute(pack(1 - core), "ctx", core_swap)
    kv_m = pack(core)

    kv0 = lay(kv_m, kv_t)
    kv1, kv2 = [], []
    for block in kv0[:-1]:
        kv2.append((lax.ppermute(block, "ctx", ahead), 0))
    neighbour = lax.ppermute(kv0[-1], "ctx", x_swap)
    q_m, g_m = half_of(queries, core), half_of(out_grad, core)
    qg_t = lax.ppermute(both(queries, out_grad, 1 - core), "ctx", core_swap)

    q_gain_row = q_gain.reshape(1, HD)
    k_gain_row = k_gain.reshape(1, HD)
    swapped, joined, returned, results, sums_h2 = [], [], [], [], []

    def x_hop(piece, turn):
        operand = jnp.where(turn, kv2[piece][0][0], kv0[piece][0])
        kv1.append(lax.ppermute(operand, "ctx", x_swap))
        return operand

    def far_hop(turn):
        theirs = after(neighbour, turn)
        block = jnp.concatenate([kv0[-1], theirs])
        moved = lax.ppermute(block, "ctx", ahead)
        kv2.append((moved, 0))
        kv1.append(jnp.where(odd, theirs[0], moved[1]))
        return block

    def send_back(group, turn):
        block = []
        for piece in group:
            arrived = jnp.where(turn, swapped[piece].astype(f32), 0.0)
            block.append((sums_h2[piece].astype(f32) + arrived).astype(b16))
        joined.append(jnp.stack(block))
        moved = lax.ppermute(joined[-1], "ctx", back)
        returned.extend((moved, at) for at in range(len(group)))

    hop_0 = x_hop(0, odd)
    middle = pieces // 2
    local_part = lambda begin, order: local(
        begin, middle, order, q_m, g_m, qg_t, kv_m, kv_t, q_gain_row, k_gain_row
    )
    prepared = [local_part(0, after(meta, hop_0, neighbour))]
    hop_1 = x_hop(1, after(odd, prepared[0][7]))
    prepared.append(local_part(middle, after(meta, hop_1)))
    order = after(meta, prepared[1][7])
    for piece in range(pieces):
        _, qn, gt, *_, total_own, out_own, doc_own = prepared[piece // middle]
        h1, h2, *result = halo(
            piece % middle, order, qn, gt, total_own, out_own, doc_own, kv1[piece], kv2[piece], k_gain_row
        )
        results.append(result)
        order = after(order, result[1])
        if piece + 3 < pieces:
            order = after(order, x_hop(piece + 2, after(odd, result[1])), far_hop(after(result[1], kv1[1])))
        swapped.append(lax.ppermute(h1, "ctx", x_swap))
        sums_h2.append(h2)
        if piece == 2:
            send_back((0, 1), after(odd, result[1], kv1[-1]))
            order = after(order, joined[-1])
        elif piece > 2:
            send_back((piece - 1,), after(odd, result[1]))

    ends = lambda group: [(swapped[i], returned[i]) for i in group]
    late, soon = list(range(middle, pieces)), list(range(middle))

    def own_part(group, order, ends):
        qt, qn, _, k_own, kt_own, v_own, e_own, *_ = prepared[group[0] // middle]
        return own_keys(
            group, order, q_gain_row, (qt, qn, k_own, kt_own, v_own, e_own),
            [results[i] for i in group], ends,
        )

    order = after(order, joined[-1])
    dq_m_late, dq_t_late, *own_late = own_part(late, order, [])
    send_back((pieces - 1,), after(odd, dq_m_late))
    order = after(order, joined[-1], returned[0][0], returned[2][0])
    dq_m_soon, dq_t_soon, kv_m_soon, kv_t_soon = own_part(soon, order, ends(soon))
    swap = lambda array: lax.ppermute(array, "ctx", core_swap)
    query_grad = join_query([dq_m_soon, dq_m_late], [swap(dq_t_soon), swap(dq_t_late)])
    kv_m_late, kv_t_late = finish(order, own_late, ends(late))
    key_grad, value_grad = join_key(
        k_gain_row, keys, [kv_m_soon, kv_m_late], [swap(kv_t_soon), swap(kv_t_late)]
    )
    return (query_grad, key_grad, value_grad)


def solution(mesh):
    split = P(("groups", "ctx"), None)
    in_specs = (split, split, split, split, P(), P(), P(("groups", "ctx")))
    return jax.shard_map(
        on_device, mesh=mesh, in_specs=in_specs, out_specs=(split, split, split), check_vma=False
    )
```

```python
import functools

import jax
import jax.numpy as jnp
from jax import lax
from jax.experimental import pallas as pl
from jax.experimental.pallas import tpu as pltpu
from jax.sharding import PartitionSpec as P

HD = 128
WINDOW = 1024
BLK = 64
ID_ROWS = 16
VMEM_LIMIT = 10 * 1024 * 1024
HIDDEN = -1e30
SMALL = pl.CostEstimate(flops=2**20, bytes_accessed=2**16, transcendentals=0)

qk_scale = 168.0 ** (-0.5)
norm_epsilon = 1e-06


def inverse_rms(values_in, axis):
    return lax.rsqrt(jnp.mean(values_in * values_in, axis=axis, keepdims=True) + norm_epsilon)


def weights(scores, first, diagonal, token, e_ref, base):
    total = jnp.zeros((8, scores.shape[1]), jnp.float32)
    key = lax.broadcasted_iota(jnp.int32, (BLK, scores.shape[1]), 0)
    for at in range(0, scores.shape[0], BLK):
        block = scores[at : at + BLK] + jnp.where(first <= at, 0.0, HIDDEN)
        if diagonal == "window" and at < HD:
            block = jnp.where(key + at > token, block, HIDDEN)
        if diagonal == "causal" and at >= scores.shape[0] - HD:
            block = jnp.where(key + (at - scores.shape[0] + HD) <= token, block, HIDDEN)
        e = jnp.exp(block)
        total = total + jnp.sum(e.reshape(BLK // 8, 8, scores.shape[1]), axis=0)
        e_ref[base + at : base + at + BLK, :] = e.astype(e_ref.dtype)
    return jnp.sum(total, axis=0, keepdims=True)


def local_kernel(
    rows, meta, q_m, g_m, qg_t, kv_m, kv_t, q_gain, k_gain,
    qt, qn, gt, k_own, kt_own, v_own, e_own, total_own, out_own, doc_own,
):
    f32, b16 = jnp.float32, jnp.bfloat16
    core = meta[0]
    wide = qt.shape[-1]
    blocks = rows // BLK
    runs = rows // HD
    gain = jnp.broadcast_to(q_gain[...], (HD, HD)).T * qk_scale
    gain = jnp.concatenate([gain] * (wide // HD), axis=1)
    sides = ((q_m, g_m, kv_m), (qg_t.at[0], qg_t.at[1], kv_t))
    for part, (q_ref, g_ref, kv) in enumerate(sides):
        slot = core if part == 0 else 1 - core
        for head in range(wide // HD):
            columns = slice(head * HD, (head + 1) * HD)
            q, g = q_ref[:, columns].T, g_ref[:, columns].T
            for run in range(runs):
                tokens = slice(run * HD, (run + 1) * HD)
                qt[slot * runs + run, :, columns] = q[:, tokens]
                gt[slot * runs + run, :, columns] = g[:, tokens]
        off = pl.multiple_of(slot * rows, rows)
        k = kv[:rows].astype(f32)
        kn = (k * inverse_rms(k, -1) * k_gain[...]).astype(b16)
        k_own[pl.ds(off, rows), :] = kn
        kt_own[:, pl.ds(off, rows)] = kn.T
        v_own[pl.ds(off, rows), :] = kv[rows : 2 * rows]
    token = lax.rem(lax.broadcasted_iota(jnp.int32, (1, wide), 1), HD)
    ids = [[kv[2 * rows :, :1].astype(f32)[b : b + 1] for b in range(blocks)] for kv in (kv_m, kv_t)]
    base = 0
    for run in range(2 * runs):
        slot, inside = divmod(run * HD, rows)
        doc = jnp.zeros((1, wide), f32)
        for b in range(HD // BLK):
            at = inside // BLK + b
            here = jnp.where(core == slot, ids[0][at], ids[1][at])
            doc = jnp.where(token >= b * BLK, here, doc)
        doc_own[run] = doc
        earlier = jnp.zeros((1, wide), f32)
        for one in ids[0] + ids[1]:
            earlier = earlier + (one < doc).astype(f32)
        first = earlier.astype(jnp.int32) * BLK
        q = qt[run].astype(f32)
        qn_run = (q * inverse_rms(q, 0) * gain).astype(b16)
        qn[run] = qn_run
        count = (run + 1) * HD
        s = jnp.dot(k_own[:count, :], qn_run, preferred_element_type=f32)
        total_own[run] = weights(s, first, "causal", token, e_own, base)
        vt = v_own[:count, :].T
        out_own[run] = jnp.dot(vt, e_own[base : base + count, :], preferred_element_type=f32)
        base += count


def local(begin, heads, meta, q_m, g_m, qg_t, kv_m, kv_t, q_gain, k_gain):
    f32, b16 = jnp.float32, jnp.bfloat16
    rows, q_columns = q_m.shape
    group_cols = q_columns // (kv_m.shape[1] // HD)
    runs = 2 * rows // HD
    pairs = HD * runs * (runs + 1) // 2
    qg = pl.BlockSpec((2, rows, group_cols), lambda h, meta: (0, 0, begin + h))
    q_mine = pl.BlockSpec((rows, group_cols), lambda h, meta: (0, begin + h))
    kv = pl.BlockSpec((kv_m.shape[0], HD), lambda h, meta: (0, begin + h))
    row = pl.BlockSpec((1, HD), lambda h, meta: (0, 0))
    out = lambda dtype, *shape: (
        pl.BlockSpec((None,) + shape, lambda h, meta: (h,) + (0,) * len(shape)),
        jax.ShapeDtypeStruct((heads,) + shape, dtype),
    )
    outs = [
        out(b16, runs, HD, group_cols), out(b16, runs, HD, group_cols),
        out(b16, runs, HD, group_cols), out(b16, 2 * rows, HD), out(b16, HD, 2 * rows),
        out(b16, 2 * rows, HD), out(b16, pairs, group_cols), out(f32, runs, 1, group_cols),
        out(f32, runs, HD, group_cols), out(f32, runs, 1, group_cols),
    ]
    return pl.pallas_call(
        functools.partial(local_kernel, rows),
        grid_spec=pltpu.PrefetchScalarGridSpec(
            num_scalar_prefetch=1,
            grid=(heads,),
            in_specs=[q_mine, q_mine, qg, kv, kv, row, row],
            out_specs=[one[0] for one in outs],
        ),
        out_shape=[one[1] for one in outs],
        compiler_params=pltpu.CompilerParams(vmem_limit_bytes=VMEM_LIMIT),
        cost_estimate=SMALL,
        name=f"local_{begin}",
    )(meta, q_m, g_m, qg_t, kv_m, kv_t, q_gain, k_gain)


def halo_kernel(
    piece, at, rows, meta, qn, gt, total_own, out_own, doc_own, kv1, kv2, k_gain,
    h1, h2, g_out, delta_out, dq_out,
    k_s, kt_s, v_s, vt_s, dk_s, dv_s, e_s,
):
    f32, b16 = jnp.float32, jnp.bfloat16
    core = meta[0]
    wide = qn.shape[-1]
    blocks = rows // BLK
    sources = ((kv2.at[at], 0), (kv1, 2 * rows))

    for source, base in sources:
        for part in range(2):
            off = pl.multiple_of(base + (core if part == 0 else 1 - core) * rows, rows)
            k = source[part, :rows].astype(f32)
            kn = (k * inverse_rms(k, -1) * k_gain[...]).astype(b16)
            k_s[pl.ds(off, rows), :] = kn
            kt_s[:, pl.ds(off, rows)] = kn.T
            v = source[part, rows : 2 * rows]
            v_s[pl.ds(off, rows), :] = v
            vt_s[:, pl.ds(off, rows)] = v.T

    token = lax.rem(lax.broadcasted_iota(jnp.int32, (1, wide), 1), HD)
    nt = (((1,), (1,)), ((), ()))
    ids = [
        source[part, 2 * rows :, :1].astype(f32)[b : b + 1]
        for source, base in sources
        for part in range(2)
        for b in range(blocks)
    ]
    for run in range(2 * rows // HD):
        low = run * HD
        doc = doc_own[piece, run]
        earlier = jnp.zeros((1, wide), f32)
        for one in ids:
            earlier = earlier + (one < doc).astype(f32)
        first = earlier.astype(jnp.int32) * BLK - low
        qn_run = qn[piece, run]
        s = jnp.dot(k_s[low:, :], qn_run, preferred_element_type=f32)
        total = total_own[piece, run] + weights(s, first, "window", token, e_s, low)
        e = e_s[low:, :]
        out = out_own[piece, run] + jnp.dot(vt_s[:, low:], e, preferred_element_type=f32)
        inverse = 1.0 / total
        g_l = (gt[piece, run].astype(f32) * inverse).astype(b16)
        delta = jnp.sum(g_l.astype(f32) * (out * inverse), axis=0, keepdims=True)
        g_out[run] = g_l
        delta_out[run] = delta
        dp = jnp.dot(v_s[low:, :], g_l, preferred_element_type=f32)
        ds = (e.astype(f32) * (dp - delta)).astype(b16)
        dv = lax.dot_general(e, g_l, nt, preferred_element_type=f32)
        dk = lax.dot_general(ds, qn_run, nt, preferred_element_type=f32)
        dv_s[low:, :] = dv if run == 0 else dv_s[low:, :] + dv
        dk_s[low:, :] = dk if run == 0 else dk_s[low:, :] + dk
        dq_out[run] = jnp.dot(kt_s[:, low:], ds, preferred_element_type=f32)

    for target, base in ((h2, 0), (h1, 2 * rows)):
        for part in range(2):
            off = pl.multiple_of(base + (core if part == 0 else 1 - core) * rows, rows)
            target[part, :rows] = dk_s[pl.ds(off, rows), :].astype(b16)
            target[part, rows:] = dv_s[pl.ds(off, rows), :].astype(b16)


def halo(piece, meta, qn, gt, total_own, out_own, doc_own, kv1, kv2, k_gain):
    array, at = kv2
    rows = (array.shape[2] - ID_ROWS) // 2
    runs, wide = qn.shape[1], qn.shape[-1]
    f32, b16 = jnp.float32, jnp.bfloat16
    vmem = pl.BlockSpec(memory_space=pltpu.VMEM)
    return pl.pallas_call(
        functools.partial(halo_kernel, piece, at, rows),
        in_specs=[pl.BlockSpec(memory_space=pltpu.SMEM)] + [vmem] * 8,
        out_specs=[vmem] * 5,
        scratch_shapes=[
            pltpu.VMEM((WINDOW, HD), b16),
            pltpu.VMEM((HD, WINDOW), b16),
            pltpu.VMEM((WINDOW, HD), b16),
            pltpu.VMEM((HD, WINDOW), b16),
            pltpu.VMEM((WINDOW, HD), f32),
            pltpu.VMEM((WINDOW, HD), f32),
            pltpu.VMEM((WINDOW, wide), b16),
        ],
        out_shape=[
            jax.ShapeDtypeStruct((2, 2 * rows, HD), b16),
            jax.ShapeDtypeStruct((2, 2 * rows, HD), b16),
            jax.ShapeDtypeStruct((runs, HD, wide), b16),
            jax.ShapeDtypeStruct((runs, 1, wide), f32),
            jax.ShapeDtypeStruct((runs, HD, wide), f32),
        ],
        compiler_params=pltpu.CompilerParams(vmem_limit_bytes=VMEM_LIMIT),
        cost_estimate=SMALL,
        name=f"halo_{piece}",
    )(meta, qn, gt, total_own, out_own, doc_own, kv1, array, k_gain)


def key_sum(even, own, swapped, returned):
    f32 = jnp.float32
    return own + returned.astype(f32) + jnp.where(even, swapped.astype(f32), 0.0)


def own_kernel(
    pieces, places, rows, meta, q_gain, qt, qn, k_own, kt_own, v_own, e_own, *refs
):
    f32, b16 = jnp.float32, jnp.bfloat16
    core, even = meta[0], meta[1] == 0
    count = len(pieces)
    inputs, refs = refs[: 3 * count], refs[3 * count :]
    ends, refs = refs[: 2 * len(places)], refs[2 * len(places) :]
    (dq_m, dq_t), outs, (dq_s, dk_s, dv_s) = refs[:2], refs[2:-3], refs[-3:]
    runs, wide = qt.shape[1], qt.shape[-1]
    nt = (((1,), (1,)), ((), ()))
    gain = jnp.broadcast_to(q_gain[...], (HD, HD)).T * qk_scale
    gain = jnp.concatenate([gain] * (wide // HD), axis=1)
    for at, piece in enumerate(pieces):
        g_in, delta_in, dq_in = inputs[3 * at : 3 * at + 3]
        base = runs * (runs + 1) // 2 * HD
        for run in reversed(range(runs)):
            keys = (run + 1) * HD
            base -= keys
            g_l, qn_run = g_in[run], qn[piece, run]
            e = e_own[piece, base : base + keys, :]
            dp = jnp.dot(v_own[piece, :keys, :], g_l, preferred_element_type=f32)
            ds = (e.astype(f32) * (dp - delta_in[run])).astype(b16)
            dv = lax.dot_general(e, g_l, nt, preferred_element_type=f32)
            dk = lax.dot_general(ds, qn_run, nt, preferred_element_type=f32)
            dv_s[:keys, :] = dv if run == runs - 1 else dv_s[:keys, :] + dv
            dk_s[:keys, :] = dk if run == runs - 1 else dk_s[:keys, :] + dk
            dq = dq_in[run] + jnp.dot(kt_own[piece, :, :keys], ds, preferred_element_type=f32)
            q = qt[piece, run].astype(f32)
            r = inverse_rms(q, 0)
            scaled = dq * gain
            dq = r * scaled - q * (r * r * r * jnp.mean(q * scaled, axis=0, keepdims=True))
            slot, inside = divmod(run * HD, rows)
            for head in range(wide // HD):
                lanes = slice(head * HD, (head + 1) * HD)
                columns = slice(at * wide + head * HD, at * wide + (head + 1) * HD)
                dq_s[slot, inside : inside + HD, columns] = dq[:, lanes].T.astype(b16)
        for part in range(2):
            tokens = pl.ds(pl.multiple_of((core if part == 0 else 1 - core) * rows, rows), rows)
            if places:
                swapped, returned = ends[2 * at : 2 * at + 2]
                columns = slice(at * HD, (at + 1) * HD)
                for which, sums in enumerate((dk_s, dv_s)):
                    span = slice(which * rows, (which + 1) * rows)
                    total = key_sum(
                        even, sums[tokens, :], swapped[part, span], returned[places[at], part, span]
                    )
                    outs[part][span, columns] = total.astype(b16)
            else:
                outs[at][part, :rows] = dk_s[tokens, :]
                outs[at][part, rows:] = dv_s[tokens, :]
    dq_m[...] = dq_s[core]
    dq_t[...] = dq_s[1 - core]


def own_keys(pieces, meta, q_gain, prepared, results, ends):
    qt, qn, k_own, kt_own, v_own, e_own = prepared
    rows = k_own.shape[1] // 2
    columns = len(pieces) * qt.shape[-1]
    f32, b16 = jnp.float32, jnp.bfloat16
    vmem = pl.BlockSpec(memory_space=pltpu.VMEM)
    dq = jax.ShapeDtypeStruct((rows, columns), b16)
    own = jax.ShapeDtypeStruct((2, 2 * rows, HD), f32)
    final = jax.ShapeDtypeStruct((2 * rows, len(pieces) * HD), b16)
    flat = [one for result in results for one in result]
    flat += [one for swapped, back in ends for one in (swapped, back[0])]
    places = tuple(back[1] for swapped, back in ends)
    outs = [dq, dq] + ([final] * 2 if ends else [own] * len(pieces))
    return pl.pallas_call(
        functools.partial(own_kernel, tuple(range(len(pieces))), places, rows),
        in_specs=[pl.BlockSpec(memory_space=pltpu.SMEM)] + [vmem] * (7 + len(flat)),
        out_specs=[vmem] * len(outs),
        scratch_shapes=[
            pltpu.VMEM((2, rows, columns), b16),
            pltpu.VMEM((2 * rows, HD), f32),
            pltpu.VMEM((2 * rows, HD), f32),
        ],
        out_shape=outs,
        compiler_params=pltpu.CompilerParams(vmem_limit_bytes=VMEM_LIMIT),
        cost_estimate=pl.CostEstimate(flops=2**32, bytes_accessed=2**22, transcendentals=0),
        name=f"own_{pieces[0]}",
    )(meta, q_gain, *prepared, *flat)


def finish_kernel(places, meta, *refs):
    outs = refs[3 * len(places) :]
    for at, at_returned in enumerate(places):
        own, swapped, returned = refs[3 * at : 3 * at + 3]
        for part in range(2):
            total = key_sum(meta[1] == 0, own[part], swapped[part], returned[at_returned, part])
            outs[part][:, at * HD : (at + 1) * HD] = total.astype(outs[part].dtype)


def finish(meta, owns, ends):
    vmem = pl.BlockSpec(memory_space=pltpu.VMEM)
    shape = jax.ShapeDtypeStruct((owns[0].shape[1], len(owns) * HD), jnp.bfloat16)
    flat = []
    for own, (swapped, back) in zip(owns, ends):
        flat += [own, swapped, back[0]]
    places = tuple(back[1] for swapped, back in ends)
    return pl.pallas_call(
        functools.partial(finish_kernel, places),
        in_specs=[pl.BlockSpec(memory_space=pltpu.SMEM)] + [vmem] * len(flat),
        out_specs=[vmem, vmem],
        out_shape=[shape, shape],
        compiler_params=pltpu.CompilerParams(vmem_limit_bytes=VMEM_LIMIT),
        cost_estimate=SMALL,
        name="finish",
    )(meta, *flat)


def join_query_kernel(count, *refs):
    core = lax.rem(lax.axis_index("ctx"), 2)
    out, sem = refs[2 * count], refs[-1]
    copies = []
    for parts, who in ((refs[:count], core), (refs[count : 2 * count], 1 - core)):
        at = 0
        for part in parts:
            width = part.shape[1]
            columns = pl.ds(pl.multiple_of(who * (out.shape[1] // 2) + at, HD), width)
            copies.append(pltpu.make_async_copy(part, out.at[:, columns], sem.at[len(copies)]))
            at += width
    for copy in copies:
        copy.start()
    for copy in copies:
        copy.wait()


def join_query(mine, theirs):
    width = 2 * sum(part.shape[1] for part in mine)
    vmem = pl.BlockSpec(memory_space=pltpu.VMEM)
    return pl.pallas_call(
        functools.partial(join_query_kernel, len(mine)),
        in_specs=[vmem] * (2 * len(mine)),
        out_specs=pl.BlockSpec(memory_space=pltpu.HBM),
        out_shape=jax.ShapeDtypeStruct((mine[0].shape[0], width), mine[0].dtype),
        scratch_shapes=[pltpu.SemaphoreType.DMA((2 * len(mine),))],
        compiler_params=pltpu.CompilerParams(vmem_limit_bytes=VMEM_LIMIT),
        cost_estimate=SMALL,
        name="join_query",
    )(*mine, *theirs)


def join_key_kernel(count, rows, k_gain, keys, *refs):
    f32 = jnp.float32
    core = lax.rem(lax.axis_index("ctx"), 2)
    key_out, value_out = refs[2 * count :]
    half = key_out.shape[1] // 2
    for parts, who in ((refs[:count], core), (refs[count : 2 * count], 1 - core)):
        at = 0
        for part in parts:
            for head in range(part.shape[1] // HD):
                columns = pl.ds(pl.multiple_of(who * half + at, HD), HD)
                inside = slice(head * HD, (head + 1) * HD)
                k = keys[:, columns].astype(f32)
                r = inverse_rms(k, -1)
                scaled = part[:rows, inside].astype(f32) * k_gain[...]
                grad = r * scaled - k * (r * r * r * jnp.mean(k * scaled, axis=-1, keepdims=True))
                key_out[:, columns] = grad.astype(key_out.dtype)
                value_out[:, columns] = part[rows:, inside]
                at += HD


def join_key(k_gain, keys, mine, theirs):
    rows, width = keys.shape
    vmem = pl.BlockSpec(memory_space=pltpu.VMEM)
    out = jax.ShapeDtypeStruct((rows, width), keys.dtype)
    return pl.pallas_call(
        functools.partial(join_key_kernel, len(mine), rows),
        in_specs=[vmem] * (2 + 2 * len(mine)),
        out_specs=[vmem, vmem],
        out_shape=[out, out],
        compiler_params=pltpu.CompilerParams(vmem_limit_bytes=VMEM_LIMIT),
        cost_estimate=SMALL,
        name="join_key",
    )(k_gain, keys, *mine, *theirs)


def lay_kernel(kv_m, kv_t, *outs):
    place = [(out, at) for out in outs for at in range(out.shape[0])]
    for part, kv in enumerate((kv_m, kv_t)):
        for head, (out, at) in enumerate(place):
            out[at, part] = kv[:, head * HD : (head + 1) * HD]


def lay(kv_m, kv_t):
    shape = lambda count: jax.ShapeDtypeStruct((count, 2, kv_m.shape[0], HD), kv_m.dtype)
    vmem = pl.BlockSpec(memory_space=pltpu.VMEM)
    return pl.pallas_call(
        lay_kernel,
        in_specs=[vmem, vmem],
        out_specs=[vmem] * (kv_m.shape[1] // HD),
        out_shape=[shape(1)] * (kv_m.shape[1] // HD),
        compiler_params=pltpu.CompilerParams(vmem_limit_bytes=VMEM_LIMIT),
        cost_estimate=SMALL,
        name="lay",
    )(kv_m, kv_t)


def after(value, *others):
    return lax.optimization_barrier((value,) + others)[0]


def on_device(queries, keys, values, out_grad, q_gain, k_gain, doc_ids):
    f32, b16 = jnp.float32, jnp.bfloat16
    rows = queries.shape[0]
    half = keys.shape[1] // 2
    pieces = half // HD
    count = lax.axis_size("ctx")
    if WINDOW != 4 * rows or count % 4 != 0:
        raise ValueError("unsupported split")
    rank = lax.axis_index("ctx")
    core = lax.rem(rank, 2)
    parity = lax.rem(lax.div(rank, 2), 2)
    odd = parity == 1
    meta = jnp.stack([core, parity]).astype(jnp.int32)

    core_swap = [(i, i ^ 1) for i in range(count)]
    x_swap = [(i, i ^ 2) for i in range(count)]
    ahead = [(i, i + 4) for i in range(count - 4)]
    back = [(i + 4, i) for i in range(count - 4)]

    def half_of(array, who):
        width = array.shape[1] // 2
        return lax.dynamic_slice(array, (0, who * width), (rows, width))

    def both(one, two, who):
        return jnp.stack([half_of(one, who), half_of(two, who)])

    id_rows = jnp.pad((doc_ids + 1).astype(b16), (0, ID_ROWS - doc_ids.shape[0]))
    id_rows = jnp.broadcast_to(id_rows[:, None], (ID_ROWS, half))

    def pack(who):
        return jnp.concatenate([half_of(keys, who), half_of(values, who), id_rows])

    kv_t = lax.ppermute(pack(1 - core), "ctx", core_swap)
    kv_m = pack(core)

    kv0 = lay(kv_m, kv_t)
    kv1, kv2 = [], []
    for block in kv0[:-1]:
        kv2.append((lax.ppermute(block, "ctx", ahead), 0))
    neighbour = lax.ppermute(kv0[-1], "ctx", x_swap)
    q_m, g_m = half_of(queries, core), half_of(out_grad, core)
    qg_t = lax.ppermute(both(queries, out_grad, 1 - core), "ctx", core_swap)

    q_gain_row = q_gain.reshape(1, HD)
    k_gain_row = k_gain.reshape(1, HD)
    swapped, joined, returned, results, sums_h2 = [], [], [], [], []

    def x_hop(piece, turn):
        operand = jnp.where(turn, kv2[piece][0][0], kv0[piece][0])
        kv1.append(lax.ppermute(operand, "ctx", x_swap))
        return operand

    def far_hop(turn):
        theirs = after(neighbour, turn)
        block = jnp.concatenate([kv0[-1], theirs])
        moved = lax.ppermute(block, "ctx", ahead)
        kv2.append((moved, 0))
        kv1.append(jnp.where(odd, theirs[0], moved[1]))
        return block

    def send_back(group, turn):
        block = []
        for piece in group:
            arrived = jnp.where(turn, swapped[piece].astype(f32), 0.0)
            block.append((sums_h2[piece].astype(f32) + arrived).astype(b16))
        joined.append(jnp.stack(block))
        moved = lax.ppermute(joined[-1], "ctx", back)
        returned.extend((moved, at) for at in range(len(group)))

    hop_0 = x_hop(0, odd)
    middle = pieces // 2
    local_part = lambda begin, order: local(
        begin, middle, order, q_m, g_m, qg_t, kv_m, kv_t, q_gain_row, k_gain_row
    )
    prepared = [local_part(0, after(meta, hop_0, neighbour))]
    order = after(meta, x_hop(1, after(odd, prepared[0][7])))
    for piece in range(pieces):
        if piece == middle:
            prepared.append(local_part(middle, order))
        _, qn, gt, *_, total_own, out_own, doc_own = prepared[piece // middle]
        h1, h2, *result = halo(
            piece % middle, order, qn, gt, total_own, out_own, doc_own, kv1[piece], kv2[piece], k_gain_row
        )
        results.append(result)
        order = after(order, result[1])
        if piece + 3 < pieces:
            order = after(order, x_hop(piece + 2, after(odd, result[1])), far_hop(result[1]))
        swapped.append(lax.ppermute(h1, "ctx", x_swap))
        sums_h2.append(h2)
        if piece == 2:
            send_back((0, 1), after(odd, result[1]))
            order = after(order, joined[-1])
        elif piece > 2:
            send_back((piece - 1,), after(odd, result[1]))

    ends = lambda group: [(swapped[i], returned[i]) for i in group]
    late, soon = list(range(middle, pieces)), list(range(middle))

    def own_part(group, order, ends):
        qt, qn, _, k_own, kt_own, v_own, e_own, *_ = prepared[group[0] // middle]
        return own_keys(
            group, order, q_gain_row, (qt, qn, k_own, kt_own, v_own, e_own),
            [results[i] for i in group], ends,
        )

    order = after(order, joined[-1])
    dq_m_late, dq_t_late, *own_late = own_part(late, order, [])
    send_back((pieces - 1,), after(odd, dq_m_late))
    order = after(order, joined[-1], returned[0][0], returned[2][0])
    dq_m_soon, dq_t_soon, kv_m_soon, kv_t_soon = own_part(soon, order, ends(soon))
    swap = lambda array: lax.ppermute(array, "ctx", core_swap)
    query_grad = join_query([dq_m_soon, dq_m_late], [swap(dq_t_soon), swap(dq_t_late)])
    kv_m_late, kv_t_late = finish(order, own_late, ends(late))
    key_grad, value_grad = join_key(
        k_gain_row, keys, [kv_m_soon, kv_m_late], [swap(kv_t_soon), swap(kv_t_late)]
    )
    return (query_grad, key_grad, value_grad)


def solution(mesh):
    split = P(("groups", "ctx"), None)
    in_specs = (split, split, split, split, P(), P(), P(("groups", "ctx")))
    return jax.shard_map(
        on_device, mesh=mesh, in_specs=in_specs, out_specs=(split, split, split), check_vma=False
    )
```

```python
import functools

import jax
import jax.numpy as jnp
from jax import lax
from jax.experimental import pallas as pl
from jax.experimental.pallas import tpu as pltpu
from jax.sharding import PartitionSpec as P

HD = 128
WINDOW = 1024
BLK = 64
ID_ROWS = 16
VMEM_LIMIT = 12 * 1024 * 1024
HIDDEN = -1e30
SMALL = pl.CostEstimate(flops=2**20, bytes_accessed=2**16, transcendentals=0)

qk_scale = 168.0 ** (-0.5)
norm_epsilon = 1e-06


def inverse_rms(values_in, axis):
    return lax.rsqrt(jnp.mean(values_in * values_in, axis=axis, keepdims=True) + norm_epsilon)


def weights(scores, first, diagonal, token, e_ref, base):
    total = jnp.zeros((8, scores.shape[1]), jnp.float32)
    key = lax.broadcasted_iota(jnp.int32, (BLK, scores.shape[1]), 0)
    for at in range(0, scores.shape[0], BLK):
        block = scores[at : at + BLK] + jnp.where(first <= at, 0.0, HIDDEN)
        if diagonal == "window" and at < HD:
            block = jnp.where(key + at > token, block, HIDDEN)
        if diagonal == "causal" and at >= scores.shape[0] - HD:
            block = jnp.where(key + (at - scores.shape[0] + HD) <= token, block, HIDDEN)
        e = jnp.exp(block)
        total = total + jnp.sum(e.reshape(BLK // 8, 8, scores.shape[1]), axis=0)
        e_ref[base + at : base + at + BLK, :] = e.astype(e_ref.dtype)
    return jnp.sum(total, axis=0, keepdims=True)


def local_kernel(
    rows, meta, qg_m, qg_t, kv_m, kv_t, q_gain, k_gain,
    qt, qn, gt, k_own, kt_own, v_own, e_own, total_own, out_own, doc_own,
):
    f32, b16 = jnp.float32, jnp.bfloat16
    core = meta[0]
    wide = qt.shape[-1]
    blocks = rows // BLK
    runs = rows // HD
    gain = jnp.broadcast_to(q_gain[...], (HD, HD)).T * qk_scale
    gain = jnp.concatenate([gain] * (wide // HD), axis=1)
    for part, (qg, kv) in enumerate(((qg_m, kv_m), (qg_t, kv_t))):
        slot = core if part == 0 else 1 - core
        for head in range(wide // HD):
            columns = slice(head * HD, (head + 1) * HD)
            q, g = qg[0, :, columns].T, qg[1, :, columns].T
            for run in range(runs):
                tokens = slice(run * HD, (run + 1) * HD)
                qt[slot * runs + run, :, columns] = q[:, tokens]
                gt[slot * runs + run, :, columns] = g[:, tokens]
        off = pl.multiple_of(slot * rows, rows)
        k = kv[:rows].astype(f32)
        kn = (k * inverse_rms(k, -1) * k_gain[...]).astype(b16)
        k_own[pl.ds(off, rows), :] = kn
        kt_own[:, pl.ds(off, rows)] = kn.T
        v_own[pl.ds(off, rows), :] = kv[rows : 2 * rows]
    token = lax.rem(lax.broadcasted_iota(jnp.int32, (1, wide), 1), HD)
    ids = [[kv[2 * rows :, :1].astype(f32)[b : b + 1] for b in range(blocks)] for kv in (kv_m, kv_t)]
    base = 0
    for run in range(2 * runs):
        slot, inside = divmod(run * HD, rows)
        doc = jnp.zeros((1, wide), f32)
        for b in range(HD // BLK):
            at = inside // BLK + b
            here = jnp.where(core == slot, ids[0][at], ids[1][at])
            doc = jnp.where(token >= b * BLK, here, doc)
        doc_own[run] = doc
        earlier = jnp.zeros((1, wide), f32)
        for one in ids[0] + ids[1]:
            earlier = earlier + (one < doc).astype(f32)
        first = earlier.astype(jnp.int32) * BLK
        q = qt[run].astype(f32)
        qn_run = (q * inverse_rms(q, 0) * gain).astype(b16)
        qn[run] = qn_run
        count = (run + 1) * HD
        s = jnp.dot(k_own[:count, :], qn_run, preferred_element_type=f32)
        total_own[run] = weights(s, first, "causal", token, e_own, base)
        vt = v_own[:count, :].T
        out_own[run] = jnp.dot(vt, e_own[base : base + count, :], preferred_element_type=f32)
        base += count


def local(begin, heads, meta, qg_m, qg_t, kv_m, kv_t, q_gain, k_gain):
    f32, b16 = jnp.float32, jnp.bfloat16
    rows = qg_m.shape[1]
    group_cols = qg_m.shape[2] // (kv_m.shape[1] // HD)
    runs = 2 * rows // HD
    pairs = HD * runs * (runs + 1) // 2
    qg = pl.BlockSpec((2, rows, group_cols), lambda h, meta: (0, 0, begin + h))
    kv = pl.BlockSpec((kv_m.shape[0], HD), lambda h, meta: (0, begin + h))
    row = pl.BlockSpec((1, HD), lambda h, meta: (0, 0))
    out = lambda dtype, *shape: (
        pl.BlockSpec((None,) + shape, lambda h, meta: (h,) + (0,) * len(shape)),
        jax.ShapeDtypeStruct((heads,) + shape, dtype),
    )
    outs = [
        out(b16, runs, HD, group_cols), out(b16, runs, HD, group_cols),
        out(b16, runs, HD, group_cols), out(b16, 2 * rows, HD), out(b16, HD, 2 * rows),
        out(b16, 2 * rows, HD), out(b16, pairs, group_cols), out(f32, runs, 1, group_cols),
        out(f32, runs, HD, group_cols), out(f32, runs, 1, group_cols),
    ]
    return pl.pallas_call(
        functools.partial(local_kernel, rows),
        grid_spec=pltpu.PrefetchScalarGridSpec(
            num_scalar_prefetch=1,
            grid=(heads,),
            in_specs=[qg, qg, kv, kv, row, row],
            out_specs=[one[0] for one in outs],
        ),
        out_shape=[one[1] for one in outs],
        compiler_params=pltpu.CompilerParams(vmem_limit_bytes=VMEM_LIMIT),
        cost_estimate=SMALL,
        name=f"local_{begin}",
    )(meta, qg_m, qg_t, kv_m, kv_t, q_gain, k_gain)


def halo_kernel(
    piece, at, rows, meta, qn, gt, total_own, out_own, doc_own, kv1, kv2, k_gain,
    h1, h2, g_out, delta_out, dq_out,
    k_s, kt_s, v_s, vt_s, dk_s, dv_s, e_s,
):
    f32, b16 = jnp.float32, jnp.bfloat16
    core = meta[0]
    wide = qn.shape[-1]
    blocks = rows // BLK
    sources = ((kv2.at[at], 0), (kv1, 2 * rows))

    for source, base in sources:
        for part in range(2):
            off = pl.multiple_of(base + (core if part == 0 else 1 - core) * rows, rows)
            k = source[part, :rows].astype(f32)
            kn = (k * inverse_rms(k, -1) * k_gain[...]).astype(b16)
            k_s[pl.ds(off, rows), :] = kn
            kt_s[:, pl.ds(off, rows)] = kn.T
            v = source[part, rows : 2 * rows]
            v_s[pl.ds(off, rows), :] = v
            vt_s[:, pl.ds(off, rows)] = v.T

    token = lax.rem(lax.broadcasted_iota(jnp.int32, (1, wide), 1), HD)
    nt = (((1,), (1,)), ((), ()))
    ids = [
        source[part, 2 * rows :, :1].astype(f32)[b : b + 1]
        for source, base in sources
        for part in range(2)
        for b in range(blocks)
    ]
    runs = 2 * rows // HD

    def forward(run):
        low = run * HD
        doc = doc_own[piece, run]
        earlier = jnp.zeros((1, wide), f32)
        for one in ids:
            earlier = earlier + (one < doc).astype(f32)
        first = earlier.astype(jnp.int32) * BLK - low
        s = jnp.dot(k_s[low:, :], qn[piece, run], preferred_element_type=f32)
        e_run = e_s.at[run % 2]
        total = total_own[piece, run] + weights(s, first, "window", token, e_run, low)
        out = jnp.dot(vt_s[:, low:], e_run[low:, :], preferred_element_type=f32)
        return total, out_own[piece, run] + out

    def backward(run, total, out):
        low = run * HD
        qn_run = qn[piece, run]
        e = e_s[run % 2, low:, :]
        inverse = 1.0 / total
        g_l = (gt[piece, run].astype(f32) * inverse).astype(b16)
        delta = jnp.sum(g_l.astype(f32) * (out * inverse), axis=0, keepdims=True)
        g_out[run] = g_l
        delta_out[run] = delta
        dp = jnp.dot(v_s[low:, :], g_l, preferred_element_type=f32)
        ds = (e.astype(f32) * (dp - delta)).astype(b16)
        dv = lax.dot_general(e, g_l, nt, preferred_element_type=f32)
        dk = lax.dot_general(ds, qn_run, nt, preferred_element_type=f32)
        dv_s[low:, :] = dv if run == 0 else dv_s[low:, :] + dv
        dk_s[low:, :] = dk if run == 0 else dk_s[low:, :] + dk
        dq_out[run] = jnp.dot(kt_s[:, low:], ds, preferred_element_type=f32)

    state = forward(0)
    for run in range(runs):
        following = forward(run + 1) if run + 1 < runs else None
        backward(run, *state)
        state = following

    for target, base in ((h2, 0), (h1, 2 * rows)):
        for part in range(2):
            off = pl.multiple_of(base + (core if part == 0 else 1 - core) * rows, rows)
            target[part, :rows] = dk_s[pl.ds(off, rows), :].astype(b16)
            target[part, rows:] = dv_s[pl.ds(off, rows), :].astype(b16)


def halo(piece, meta, qn, gt, total_own, out_own, doc_own, kv1, kv2, k_gain):
    array, at = kv2
    rows = (array.shape[2] - ID_ROWS) // 2
    runs, wide = qn.shape[1], qn.shape[-1]
    f32, b16 = jnp.float32, jnp.bfloat16
    vmem = pl.BlockSpec(memory_space=pltpu.VMEM)
    return pl.pallas_call(
        functools.partial(halo_kernel, piece, at, rows),
        in_specs=[pl.BlockSpec(memory_space=pltpu.SMEM)] + [vmem] * 8,
        out_specs=[vmem] * 5,
        scratch_shapes=[
            pltpu.VMEM((WINDOW, HD), b16),
            pltpu.VMEM((HD, WINDOW), b16),
            pltpu.VMEM((WINDOW, HD), b16),
            pltpu.VMEM((HD, WINDOW), b16),
            pltpu.VMEM((WINDOW, HD), f32),
            pltpu.VMEM((WINDOW, HD), f32),
            pltpu.VMEM((2, WINDOW, wide), b16),
        ],
        out_shape=[
            jax.ShapeDtypeStruct((2, 2 * rows, HD), b16),
            jax.ShapeDtypeStruct((2, 2 * rows, HD), b16),
            jax.ShapeDtypeStruct((runs, HD, wide), b16),
            jax.ShapeDtypeStruct((runs, 1, wide), f32),
            jax.ShapeDtypeStruct((runs, HD, wide), f32),
        ],
        compiler_params=pltpu.CompilerParams(vmem_limit_bytes=VMEM_LIMIT),
        cost_estimate=SMALL,
        name=f"halo_{piece}",
    )(meta, qn, gt, total_own, out_own, doc_own, kv1, array, k_gain)


def key_sum(even, own, swapped, returned):
    f32 = jnp.float32
    return own + returned.astype(f32) + jnp.where(even, swapped.astype(f32), 0.0)


def own_kernel(
    pieces, places, rows, meta, q_gain, qt, qn, k_own, kt_own, v_own, e_own, *refs
):
    f32, b16 = jnp.float32, jnp.bfloat16
    core, even = meta[0], meta[1] == 0
    count = len(pieces)
    inputs, refs = refs[: 3 * count], refs[3 * count :]
    ends, refs = refs[: 2 * len(places)], refs[2 * len(places) :]
    (dq_m, dq_t), outs, (dq_s, dk_s, dv_s) = refs[:2], refs[2:-3], refs[-3:]
    runs, wide = qt.shape[1], qt.shape[-1]
    nt = (((1,), (1,)), ((), ()))
    gain = jnp.broadcast_to(q_gain[...], (HD, HD)).T * qk_scale
    gain = jnp.concatenate([gain] * (wide // HD), axis=1)
    for at, piece in enumerate(pieces):
        g_in, delta_in, dq_in = inputs[3 * at : 3 * at + 3]
        base = runs * (runs + 1) // 2 * HD
        for run in reversed(range(runs)):
            keys = (run + 1) * HD
            base -= keys
            g_l, qn_run = g_in[run], qn[piece, run]
            e = e_own[piece, base : base + keys, :]
            dp = jnp.dot(v_own[piece, :keys, :], g_l, preferred_element_type=f32)
            ds = (e.astype(f32) * (dp - delta_in[run])).astype(b16)
            dv = lax.dot_general(e, g_l, nt, preferred_element_type=f32)
            dk = lax.dot_general(ds, qn_run, nt, preferred_element_type=f32)
            dv_s[:keys, :] = dv if run == runs - 1 else dv_s[:keys, :] + dv
            dk_s[:keys, :] = dk if run == runs - 1 else dk_s[:keys, :] + dk
            dq = dq_in[run] + jnp.dot(kt_own[piece, :, :keys], ds, preferred_element_type=f32)
            q = qt[piece, run].astype(f32)
            r = inverse_rms(q, 0)
            scaled = dq * gain
            dq = r * scaled - q * (r * r * r * jnp.mean(q * scaled, axis=0, keepdims=True))
            slot, inside = divmod(run * HD, rows)
            for head in range(wide // HD):
                lanes = slice(head * HD, (head + 1) * HD)
                columns = slice(at * wide + head * HD, at * wide + (head + 1) * HD)
                dq_s[slot, inside : inside + HD, columns] = dq[:, lanes].T.astype(b16)
        for part in range(2):
            tokens = pl.ds(pl.multiple_of((core if part == 0 else 1 - core) * rows, rows), rows)
            if places:
                swapped, returned = ends[2 * at : 2 * at + 2]
                columns = slice(at * HD, (at + 1) * HD)
                for which, sums in enumerate((dk_s, dv_s)):
                    span = slice(which * rows, (which + 1) * rows)
                    total = key_sum(
                        even, sums[tokens, :], swapped[part, span], returned[places[at], part, span]
                    )
                    outs[part][span, columns] = total.astype(b16)
            else:
                outs[at][part, :rows] = dk_s[tokens, :]
                outs[at][part, rows:] = dv_s[tokens, :]
    dq_m[...] = dq_s[core]
    dq_t[...] = dq_s[1 - core]


def own_keys(pieces, meta, q_gain, prepared, results, ends):
    qt, qn, k_own, kt_own, v_own, e_own = prepared
    rows = k_own.shape[1] // 2
    columns = len(pieces) * qt.shape[-1]
    f32, b16 = jnp.float32, jnp.bfloat16
    vmem = pl.BlockSpec(memory_space=pltpu.VMEM)
    dq = jax.ShapeDtypeStruct((rows, columns), b16)
    own = jax.ShapeDtypeStruct((2, 2 * rows, HD), f32)
    final = jax.ShapeDtypeStruct((2 * rows, len(pieces) * HD), b16)
    flat = [one for result in results for one in result]
    flat += [one for swapped, back in ends for one in (swapped, back[0])]
    places = tuple(back[1] for swapped, back in ends)
    outs = [dq, dq] + ([final] * 2 if ends else [own] * len(pieces))
    return pl.pallas_call(
        functools.partial(own_kernel, tuple(range(len(pieces))), places, rows),
        in_specs=[pl.BlockSpec(memory_space=pltpu.SMEM)] + [vmem] * (7 + len(flat)),
        out_specs=[vmem] * len(outs),
        scratch_shapes=[
            pltpu.VMEM((2, rows, columns), b16),
            pltpu.VMEM((2 * rows, HD), f32),
            pltpu.VMEM((2 * rows, HD), f32),
        ],
        out_shape=outs,
        compiler_params=pltpu.CompilerParams(vmem_limit_bytes=VMEM_LIMIT),
        cost_estimate=pl.CostEstimate(flops=2**32, bytes_accessed=2**22, transcendentals=0),
        name=f"own_{pieces[0]}",
    )(meta, q_gain, *prepared, *flat)


def finish_kernel(places, meta, *refs):
    outs = refs[3 * len(places) :]
    for at, at_returned in enumerate(places):
        own, swapped, returned = refs[3 * at : 3 * at + 3]
        for part in range(2):
            total = key_sum(meta[1] == 0, own[part], swapped[part], returned[at_returned, part])
            outs[part][:, at * HD : (at + 1) * HD] = total.astype(outs[part].dtype)


def finish(meta, owns, ends):
    vmem = pl.BlockSpec(memory_space=pltpu.VMEM)
    shape = jax.ShapeDtypeStruct((owns[0].shape[1], len(owns) * HD), jnp.bfloat16)
    flat = []
    for own, (swapped, back) in zip(owns, ends):
        flat += [own, swapped, back[0]]
    places = tuple(back[1] for swapped, back in ends)
    return pl.pallas_call(
        functools.partial(finish_kernel, places),
        in_specs=[pl.BlockSpec(memory_space=pltpu.SMEM)] + [vmem] * len(flat),
        out_specs=[vmem, vmem],
        out_shape=[shape, shape],
        compiler_params=pltpu.CompilerParams(vmem_limit_bytes=VMEM_LIMIT),
        cost_estimate=SMALL,
        name="finish",
    )(meta, *flat)


def join_query_kernel(count, *refs):
    core = lax.rem(lax.axis_index("ctx"), 2)
    out, sem = refs[2 * count], refs[-1]
    copies = []
    for parts, who in ((refs[:count], core), (refs[count : 2 * count], 1 - core)):
        at = 0
        for part in parts:
            width = part.shape[1]
            columns = pl.ds(pl.multiple_of(who * (out.shape[1] // 2) + at, HD), width)
            copies.append(pltpu.make_async_copy(part, out.at[:, columns], sem.at[len(copies)]))
            at += width
    for copy in copies:
        copy.start()
    for copy in copies:
        copy.wait()


def join_query(mine, theirs):
    width = 2 * sum(part.shape[1] for part in mine)
    vmem = pl.BlockSpec(memory_space=pltpu.VMEM)
    return pl.pallas_call(
        functools.partial(join_query_kernel, len(mine)),
        in_specs=[vmem] * (2 * len(mine)),
        out_specs=pl.BlockSpec(memory_space=pltpu.HBM),
        out_shape=jax.ShapeDtypeStruct((mine[0].shape[0], width), mine[0].dtype),
        scratch_shapes=[pltpu.SemaphoreType.DMA((2 * len(mine),))],
        compiler_params=pltpu.CompilerParams(vmem_limit_bytes=VMEM_LIMIT),
        cost_estimate=SMALL,
        name="join_query",
    )(*mine, *theirs)


def join_key_kernel(count, rows, k_gain, keys, *refs):
    f32 = jnp.float32
    core = lax.rem(lax.axis_index("ctx"), 2)
    key_out, value_out = refs[2 * count :]
    half = key_out.shape[1] // 2
    for parts, who in ((refs[:count], core), (refs[count : 2 * count], 1 - core)):
        at = 0
        for part in parts:
            for head in range(part.shape[1] // HD):
                columns = pl.ds(pl.multiple_of(who * half + at, HD), HD)
                inside = slice(head * HD, (head + 1) * HD)
                k = keys[:, columns].astype(f32)
                r = inverse_rms(k, -1)
                scaled = part[:rows, inside].astype(f32) * k_gain[...]
                grad = r * scaled - k * (r * r * r * jnp.mean(k * scaled, axis=-1, keepdims=True))
                key_out[:, columns] = grad.astype(key_out.dtype)
                value_out[:, columns] = part[rows:, inside]
                at += HD


def join_key(k_gain, keys, mine, theirs):
    rows, width = keys.shape
    vmem = pl.BlockSpec(memory_space=pltpu.VMEM)
    out = jax.ShapeDtypeStruct((rows, width), keys.dtype)
    return pl.pallas_call(
        functools.partial(join_key_kernel, len(mine), rows),
        in_specs=[vmem] * (2 + 2 * len(mine)),
        out_specs=[vmem, vmem],
        out_shape=[out, out],
        compiler_params=pltpu.CompilerParams(vmem_limit_bytes=VMEM_LIMIT),
        cost_estimate=SMALL,
        name="join_key",
    )(k_gain, keys, *mine, *theirs)


def lay_kernel(kv_m, kv_t, *outs):
    place = [(out, at) for out in outs for at in range(out.shape[0])]
    for part, kv in enumerate((kv_m, kv_t)):
        for head, (out, at) in enumerate(place):
            out[at, part] = kv[:, head * HD : (head + 1) * HD]


def lay(kv_m, kv_t):
    shape = lambda count: jax.ShapeDtypeStruct((count, 2, kv_m.shape[0], HD), kv_m.dtype)
    vmem = pl.BlockSpec(memory_space=pltpu.VMEM)
    return pl.pallas_call(
        lay_kernel,
        in_specs=[vmem, vmem],
        out_specs=[vmem] * (kv_m.shape[1] // HD),
        out_shape=[shape(1)] * (kv_m.shape[1] // HD),
        compiler_params=pltpu.CompilerParams(vmem_limit_bytes=VMEM_LIMIT),
        cost_estimate=SMALL,
        name="lay",
    )(kv_m, kv_t)


def after(value, *others):
    return lax.optimization_barrier((value,) + others)[0]


def on_device(queries, keys, values, out_grad, q_gain, k_gain, doc_ids):
    f32, b16 = jnp.float32, jnp.bfloat16
    rows = queries.shape[0]
    half = keys.shape[1] // 2
    pieces = half // HD
    count = lax.axis_size("ctx")
    if WINDOW != 4 * rows or count % 4 != 0:
        raise ValueError("unsupported split")
    rank = lax.axis_index("ctx")
    core = lax.rem(rank, 2)
    parity = lax.rem(lax.div(rank, 2), 2)
    odd = parity == 1
    meta = jnp.stack([core, parity]).astype(jnp.int32)

    core_swap = [(i, i ^ 1) for i in range(count)]
    x_swap = [(i, i ^ 2) for i in range(count)]
    ahead = [(i, i + 4) for i in range(count - 4)]
    back = [(i + 4, i) for i in range(count - 4)]

    def half_of(array, who):
        width = array.shape[1] // 2
        return lax.dynamic_slice(array, (0, who * width), (rows, width))

    def both(one, two, who):
        return jnp.stack([half_of(one, who), half_of(two, who)])

    id_rows = jnp.pad((doc_ids + 1).astype(b16), (0, ID_ROWS - doc_ids.shape[0]))
    id_rows = jnp.broadcast_to(id_rows[:, None], (ID_ROWS, half))

    def pack(who):
        return jnp.concatenate([half_of(keys, who), half_of(values, who), id_rows])

    kv_t = lax.ppermute(pack(1 - core), "ctx", core_swap)
    kv_m = pack(core)

    kv0 = lay(kv_m, kv_t)
    kv1, kv2 = [], []
    for block in kv0[:-1]:
        kv2.append((lax.ppermute(block, "ctx", ahead), 0))
    neighbour = lax.ppermute(kv0[-1], "ctx", x_swap)
    qg_m = both(queries, out_grad, core)
    qg_t = lax.ppermute(both(queries, out_grad, 1 - core), "ctx", core_swap)

    q_gain_row = q_gain.reshape(1, HD)
    k_gain_row = k_gain.reshape(1, HD)
    swapped, joined, returned, results, sums_h2 = [], [], [], [], []

    def x_hop(piece, turn):
        operand = jnp.where(turn, kv2[piece][0][0], kv0[piece][0])
        kv1.append(lax.ppermute(operand, "ctx", x_swap))
        return operand

    def far_hop(turn):
        theirs = after(neighbour, turn)
        block = jnp.concatenate([kv0[-1], theirs])
        moved = lax.ppermute(block, "ctx", ahead)
        kv2.append((moved, 0))
        kv1.append(jnp.where(odd, theirs[0], moved[1]))
        return block

    def send_back(group, turn):
        block = []
        for piece in group:
            arrived = jnp.where(turn, swapped[piece].astype(f32), 0.0)
            block.append((sums_h2[piece].astype(f32) + arrived).astype(b16))
        joined.append(jnp.stack(block))
        moved = lax.ppermute(joined[-1], "ctx", back)
        returned.extend((moved, at) for at in range(len(group)))

    hop_0 = x_hop(0, odd)
    middle = pieces // 2
    local_part = lambda begin, order: local(
        begin, middle, order, qg_m, qg_t, kv_m, kv_t, q_gain_row, k_gain_row
    )
    prepared = [local_part(0, after(meta, hop_0, neighbour))]
    order = after(meta, x_hop(1, after(odd, prepared[0][7])))
    for piece in range(pieces):
        if piece == middle:
            prepared.append(local_part(middle, order))
        _, qn, gt, *_, total_own, out_own, doc_own = prepared[piece // middle]
        h1, h2, *result = halo(
            piece % middle, order, qn, gt, total_own, out_own, doc_own, kv1[piece], kv2[piece], k_gain_row
        )
        results.append(result)
        order = after(order, result[1])
        if piece + 3 < pieces:
            order = after(order, x_hop(piece + 2, after(odd, result[1])), far_hop(result[1]))
        swapped.append(lax.ppermute(h1, "ctx", x_swap))
        sums_h2.append(h2)
        if piece == 2:
            send_back((0, 1), after(odd, result[1]))
            order = after(order, joined[-1])
        elif piece > 2:
            send_back((piece - 1,), after(odd, result[1]))

    ends = lambda group: [(swapped[i], returned[i]) for i in group]
    late, soon = list(range(middle, pieces)), list(range(middle))

    def own_part(group, order, ends):
        qt, qn, _, k_own, kt_own, v_own, e_own, *_ = prepared[group[0] // middle]
        return own_keys(
            group, order, q_gain_row, (qt, qn, k_own, kt_own, v_own, e_own),
            [results[i] for i in group], ends,
        )

    order = after(order, joined[-1])
    dq_m_late, dq_t_late, *own_late = own_part(late, order, [])
    send_back((pieces - 1,), after(odd, dq_m_late))
    order = after(order, joined[-1], returned[0][0], returned[2][0])
    dq_m_soon, dq_t_soon, kv_m_soon, kv_t_soon = own_part(soon, order, ends(soon))
    swap = lambda array: lax.ppermute(array, "ctx", core_swap)
    query_grad = join_query([dq_m_soon, dq_m_late], [swap(dq_t_soon), swap(dq_t_late)])
    kv_m_late, kv_t_late = finish(order, own_late, ends(late))
    key_grad, value_grad = join_key(
        k_gain_row, keys, [kv_m_soon, kv_m_late], [swap(kv_t_soon), swap(kv_t_late)]
    )
    return (query_grad, key_grad, value_grad)


def solution(mesh):
    split = P(("groups", "ctx"), None)
    in_specs = (split, split, split, split, P(), P(), P(("groups", "ctx")))
    return jax.shard_map(
        on_device, mesh=mesh, in_specs=in_specs, out_specs=(split, split, split), check_vma=False
    )
```

```python
import functools

import jax
import jax.numpy as jnp
from jax import lax
from jax.experimental import pallas as pl
from jax.experimental.pallas import tpu as pltpu
from jax.sharding import PartitionSpec as P

HD = 128
WINDOW = 1024
BLK = 64
ID_ROWS = 16
VMEM_LIMIT = 12 * 1024 * 1024
HIDDEN = -1e30
SMALL = pl.CostEstimate(flops=2**20, bytes_accessed=2**16, transcendentals=0)

qk_scale = 168.0 ** (-0.5)
norm_epsilon = 1e-06


def inverse_rms(values_in, axis):
    return lax.rsqrt(jnp.mean(values_in * values_in, axis=axis, keepdims=True) + norm_epsilon)


def weights(scores, first, diagonal, token, e_ref, base):
    total = jnp.zeros((8, scores.shape[1]), jnp.float32)
    key = lax.broadcasted_iota(jnp.int32, (BLK, scores.shape[1]), 0)
    for at in range(0, scores.shape[0], BLK):
        block = scores[at : at + BLK] + jnp.where(first <= at, 0.0, HIDDEN)
        if diagonal == "window" and at < HD:
            block = jnp.where(key + at > token, block, HIDDEN)
        if diagonal == "causal" and at >= scores.shape[0] - HD:
            block = jnp.where(key + (at - scores.shape[0] + HD) <= token, block, HIDDEN)
        e = jnp.exp(block)
        total = total + jnp.sum(e.reshape(BLK // 8, 8, scores.shape[1]), axis=0)
        e_ref[base + at : base + at + BLK, :] = e.astype(e_ref.dtype)
    return jnp.sum(total, axis=0, keepdims=True)


def local_kernel(
    rows, meta, qg_m, qg_t, kv_m, kv_t, q_gain, k_gain,
    qt, qn, gt, k_own, kt_own, v_own, e_own, total_own, out_own, doc_own,
):
    f32, b16 = jnp.float32, jnp.bfloat16
    core = meta[0]
    wide = qt.shape[-1]
    blocks = rows // BLK
    runs = rows // HD
    gain = jnp.broadcast_to(q_gain[...], (HD, HD)).T * qk_scale
    gain = jnp.concatenate([gain] * (wide // HD), axis=1)
    for part, (qg, kv) in enumerate(((qg_m, kv_m), (qg_t, kv_t))):
        slot = core if part == 0 else 1 - core
        for head in range(wide // HD):
            columns = slice(head * HD, (head + 1) * HD)
            q, g = qg[0, :, columns].T, qg[1, :, columns].T
            for run in range(runs):
                tokens = slice(run * HD, (run + 1) * HD)
                qt[slot * runs + run, :, columns] = q[:, tokens]
                gt[slot * runs + run, :, columns] = g[:, tokens]
        off = pl.multiple_of(slot * rows, rows)
        k = kv[:rows].astype(f32)
        kn = (k * inverse_rms(k, -1) * k_gain[...]).astype(b16)
        k_own[pl.ds(off, rows), :] = kn
        kt_own[:, pl.ds(off, rows)] = kn.T
        v_own[pl.ds(off, rows), :] = kv[rows : 2 * rows]
    token = lax.rem(lax.broadcasted_iota(jnp.int32, (1, wide), 1), HD)
    ids = [[kv[2 * rows :, :1].astype(f32)[b : b + 1] for b in range(blocks)] for kv in (kv_m, kv_t)]
    base = 0
    for run in range(2 * runs):
        slot, inside = divmod(run * HD, rows)
        doc = jnp.zeros((1, wide), f32)
        for b in range(HD // BLK):
            at = inside // BLK + b
            here = jnp.where(core == slot, ids[0][at], ids[1][at])
            doc = jnp.where(token >= b * BLK, here, doc)
        doc_own[run] = doc
        earlier = jnp.zeros((1, wide), f32)
        for one in ids[0] + ids[1]:
            earlier = earlier + (one < doc).astype(f32)
        first = earlier.astype(jnp.int32) * BLK
        q = qt[run].astype(f32)
        qn_run = (q * inverse_rms(q, 0) * gain).astype(b16)
        qn[run] = qn_run
        count = (run + 1) * HD
        s = jnp.dot(k_own[:count, :], qn_run, preferred_element_type=f32)
        total_own[run] = weights(s, first, "causal", token, e_own, base)
        vt = v_own[:count, :].T
        out_own[run] = jnp.dot(vt, e_own[base : base + count, :], preferred_element_type=f32)
        base += count


def local(begin, heads, meta, qg_m, qg_t, kv_m, kv_t, q_gain, k_gain):
    f32, b16 = jnp.float32, jnp.bfloat16
    rows = qg_m.shape[1]
    group_cols = qg_m.shape[2] // (kv_m.shape[1] // HD)
    runs = 2 * rows // HD
    pairs = HD * runs * (runs + 1) // 2
    qg = pl.BlockSpec((2, rows, group_cols), lambda h, meta: (0, 0, begin + h))
    kv = pl.BlockSpec((kv_m.shape[0], HD), lambda h, meta: (0, begin + h))
    row = pl.BlockSpec((1, HD), lambda h, meta: (0, 0))
    out = lambda dtype, *shape: (
        pl.BlockSpec((None,) + shape, lambda h, meta: (h,) + (0,) * len(shape)),
        jax.ShapeDtypeStruct((heads,) + shape, dtype),
    )
    outs = [
        out(b16, runs, HD, group_cols), out(b16, runs, HD, group_cols),
        out(b16, runs, HD, group_cols), out(b16, 2 * rows, HD), out(b16, HD, 2 * rows),
        out(b16, 2 * rows, HD), out(b16, pairs, group_cols), out(f32, runs, 1, group_cols),
        out(f32, runs, HD, group_cols), out(f32, runs, 1, group_cols),
    ]
    return pl.pallas_call(
        functools.partial(local_kernel, rows),
        grid_spec=pltpu.PrefetchScalarGridSpec(
            num_scalar_prefetch=1,
            grid=(heads,),
            in_specs=[qg, qg, kv, kv, row, row],
            out_specs=[one[0] for one in outs],
        ),
        out_shape=[one[1] for one in outs],
        compiler_params=pltpu.CompilerParams(vmem_limit_bytes=VMEM_LIMIT),
        cost_estimate=SMALL,
        name=f"local_{begin}",
    )(meta, qg_m, qg_t, kv_m, kv_t, q_gain, k_gain)


def halo_kernel(
    piece, at, rows, meta, qn, gt, total_own, out_own, doc_own, kv1, kv2, k_gain,
    h1, h2, g_out, delta_out, dq_out,
    k_s, kt_s, v_s, vt_s, dk_s, dv_s, e_s,
):
    f32, b16 = jnp.float32, jnp.bfloat16
    core = meta[0]
    wide = qn.shape[-1]
    blocks = rows // BLK
    sources = ((kv2.at[at], 0), (kv1, 2 * rows))

    for source, base in sources:
        for part in range(2):
            off = pl.multiple_of(base + (core if part == 0 else 1 - core) * rows, rows)
            k = source[part, :rows].astype(f32)
            kn = (k * inverse_rms(k, -1) * k_gain[...]).astype(b16)
            k_s[pl.ds(off, rows), :] = kn
            kt_s[:, pl.ds(off, rows)] = kn.T
            v = source[part, rows : 2 * rows]
            v_s[pl.ds(off, rows), :] = v
            vt_s[:, pl.ds(off, rows)] = v.T

    token = lax.rem(lax.broadcasted_iota(jnp.int32, (1, wide), 1), HD)
    nt = (((1,), (1,)), ((), ()))
    ids = [
        source[part, 2 * rows :, :1].astype(f32)[b : b + 1]
        for source, base in sources
        for part in range(2)
        for b in range(blocks)
    ]
    runs = 2 * rows // HD

    def forward(run):
        low = run * HD
        doc = doc_own[piece, run]
        earlier = jnp.zeros((1, wide), f32)
        for one in ids:
            earlier = earlier + (one < doc).astype(f32)
        first = earlier.astype(jnp.int32) * BLK - low
        s = jnp.dot(k_s[low:, :], qn[piece, run], preferred_element_type=f32)
        e_run = e_s.at[run % 2]
        total = total_own[piece, run] + weights(s, first, "window", token, e_run, low)
        out = jnp.dot(vt_s[:, low:], e_run[low:, :], preferred_element_type=f32)
        return total, out_own[piece, run] + out

    def backward(run, total, out):
        low = run * HD
        qn_run = qn[piece, run]
        e = e_s[run % 2, low:, :]
        inverse = 1.0 / total
        g_l = (gt[piece, run].astype(f32) * inverse).astype(b16)
        delta = jnp.sum(g_l.astype(f32) * (out * inverse), axis=0, keepdims=True)
        g_out[run] = g_l
        delta_out[run] = delta
        dp = jnp.dot(v_s[low:, :], g_l, preferred_element_type=f32)
        ds = (e.astype(f32) * (dp - delta)).astype(b16)
        dv = lax.dot_general(e, g_l, nt, preferred_element_type=f32)
        dk = lax.dot_general(ds, qn_run, nt, preferred_element_type=f32)
        dv_s[low:, :] = dv if run == 0 else dv_s[low:, :] + dv
        dk_s[low:, :] = dk if run == 0 else dk_s[low:, :] + dk
        dq_out[run] = jnp.dot(kt_s[:, low:], ds, preferred_element_type=f32)

    state = forward(0)
    for run in range(runs):
        following = forward(run + 1) if run + 1 < runs else None
        backward(run, *state)
        state = following

    for target, base in ((h2, 0), (h1, 2 * rows)):
        for part in range(2):
            off = pl.multiple_of(base + (core if part == 0 else 1 - core) * rows, rows)
            target[part, :rows] = dk_s[pl.ds(off, rows), :].astype(b16)
            target[part, rows:] = dv_s[pl.ds(off, rows), :].astype(b16)


def halo(piece, meta, qn, gt, total_own, out_own, doc_own, kv1, kv2, k_gain):
    array, at = kv2
    rows = (array.shape[2] - ID_ROWS) // 2
    runs, wide = qn.shape[1], qn.shape[-1]
    f32, b16 = jnp.float32, jnp.bfloat16
    vmem = pl.BlockSpec(memory_space=pltpu.VMEM)
    return pl.pallas_call(
        functools.partial(halo_kernel, piece, at, rows),
        in_specs=[pl.BlockSpec(memory_space=pltpu.SMEM)] + [vmem] * 8,
        out_specs=[vmem] * 5,
        scratch_shapes=[
            pltpu.VMEM((WINDOW, HD), b16),
            pltpu.VMEM((HD, WINDOW), b16),
            pltpu.VMEM((WINDOW, HD), b16),
            pltpu.VMEM((HD, WINDOW), b16),
            pltpu.VMEM((WINDOW, HD), f32),
            pltpu.VMEM((WINDOW, HD), f32),
            pltpu.VMEM((2, WINDOW, wide), b16),
        ],
        out_shape=[
            jax.ShapeDtypeStruct((2, 2 * rows, HD), b16),
            jax.ShapeDtypeStruct((2, 2 * rows, HD), b16),
            jax.ShapeDtypeStruct((runs, HD, wide), b16),
            jax.ShapeDtypeStruct((runs, 1, wide), f32),
            jax.ShapeDtypeStruct((runs, HD, wide), f32),
        ],
        compiler_params=pltpu.CompilerParams(vmem_limit_bytes=VMEM_LIMIT),
        cost_estimate=SMALL,
        name=f"halo_{piece}",
    )(meta, qn, gt, total_own, out_own, doc_own, kv1, array, k_gain)


def key_sum(even, own, swapped, returned):
    f32 = jnp.float32
    return own + returned.astype(f32) + jnp.where(even, swapped.astype(f32), 0.0)


def own_kernel(
    pieces, places, rows, meta, q_gain, qt, qn, k_own, kt_own, v_own, e_own, *refs
):
    f32, b16 = jnp.float32, jnp.bfloat16
    core, even = meta[0], meta[1] == 0
    count = len(pieces)
    inputs, refs = refs[: 3 * count], refs[3 * count :]
    ends, refs = refs[: 2 * len(places)], refs[2 * len(places) :]
    (dq_m, dq_t), outs, (dq_s, dk_s, dv_s) = refs[:2], refs[2:-3], refs[-3:]
    runs, wide = qt.shape[1], qt.shape[-1]
    nt = (((1,), (1,)), ((), ()))
    gain = jnp.broadcast_to(q_gain[...], (HD, HD)).T * qk_scale
    gain = jnp.concatenate([gain] * (wide // HD), axis=1)
    for at, piece in enumerate(pieces):
        g_in, delta_in, dq_in = inputs[3 * at : 3 * at + 3]
        base = runs * (runs + 1) // 2 * HD
        for run in reversed(range(runs)):
            keys = (run + 1) * HD
            base -= keys
            g_l, qn_run = g_in[run], qn[piece, run]
            e = e_own[piece, base : base + keys, :]
            dp = jnp.dot(v_own[piece, :keys, :], g_l, preferred_element_type=f32)
            ds = (e.astype(f32) * (dp - delta_in[run])).astype(b16)
            dv = lax.dot_general(e, g_l, nt, preferred_element_type=f32)
            dk = lax.dot_general(ds, qn_run, nt, preferred_element_type=f32)
            dv_s[:keys, :] = dv if run == runs - 1 else dv_s[:keys, :] + dv
            dk_s[:keys, :] = dk if run == runs - 1 else dk_s[:keys, :] + dk
            dq = dq_in[run] + jnp.dot(kt_own[piece, :, :keys], ds, preferred_element_type=f32)
            q = qt[piece, run].astype(f32)
            r = inverse_rms(q, 0)
            scaled = dq * gain
            dq = r * scaled - q * (r * r * r * jnp.mean(q * scaled, axis=0, keepdims=True))
            slot, inside = divmod(run * HD, rows)
            for head in range(wide // HD):
                lanes = slice(head * HD, (head + 1) * HD)
                columns = slice(at * wide + head * HD, at * wide + (head + 1) * HD)
                dq_s[slot, inside : inside + HD, columns] = dq[:, lanes].T.astype(b16)
        for part in range(2):
            tokens = pl.ds(pl.multiple_of((core if part == 0 else 1 - core) * rows, rows), rows)
            if places:
                swapped, returned = ends[2 * at : 2 * at + 2]
                columns = slice(at * HD, (at + 1) * HD)
                for which, sums in enumerate((dk_s, dv_s)):
                    span = slice(which * rows, (which + 1) * rows)
                    total = key_sum(
                        even, sums[tokens, :], swapped[part, span], returned[places[at], part, span]
                    )
                    outs[part][span, columns] = total.astype(b16)
            else:
                outs[at][part, :rows] = dk_s[tokens, :]
                outs[at][part, rows:] = dv_s[tokens, :]
    dq_m[...] = dq_s[core]
    dq_t[...] = dq_s[1 - core]


def own_keys(pieces, meta, q_gain, prepared, results, ends):
    qt, qn, k_own, kt_own, v_own, e_own = prepared
    rows = k_own.shape[1] // 2
    columns = len(pieces) * qt.shape[-1]
    f32, b16 = jnp.float32, jnp.bfloat16
    vmem = pl.BlockSpec(memory_space=pltpu.VMEM)
    dq = jax.ShapeDtypeStruct((rows, columns), b16)
    own = jax.ShapeDtypeStruct((2, 2 * rows, HD), f32)
    final = jax.ShapeDtypeStruct((2 * rows, len(pieces) * HD), b16)
    flat = [one for result in results for one in result]
    flat += [one for swapped, back in ends for one in (swapped, back[0])]
    places = tuple(back[1] for swapped, back in ends)
    outs = [dq, dq] + ([final] * 2 if ends else [own] * len(pieces))
    return pl.pallas_call(
        functools.partial(own_kernel, tuple(range(len(pieces))), places, rows),
        in_specs=[pl.BlockSpec(memory_space=pltpu.SMEM)] + [vmem] * (7 + len(flat)),
        out_specs=[vmem] * len(outs),
        scratch_shapes=[
            pltpu.VMEM((2, rows, columns), b16),
            pltpu.VMEM((2 * rows, HD), f32),
            pltpu.VMEM((2 * rows, HD), f32),
        ],
        out_shape=outs,
        compiler_params=pltpu.CompilerParams(vmem_limit_bytes=VMEM_LIMIT),
        cost_estimate=pl.CostEstimate(flops=2**32, bytes_accessed=2**22, transcendentals=0),
        name=f"own_{pieces[0]}",
    )(meta, q_gain, *prepared, *flat)


def finish_kernel(places, meta, *refs):
    outs = refs[3 * len(places) :]
    for at, at_returned in enumerate(places):
        own, swapped, returned = refs[3 * at : 3 * at + 3]
        for part in range(2):
            total = key_sum(meta[1] == 0, own[part], swapped[part], returned[at_returned, part])
            outs[part][:, at * HD : (at + 1) * HD] = total.astype(outs[part].dtype)


def finish(meta, owns, ends):
    vmem = pl.BlockSpec(memory_space=pltpu.VMEM)
    shape = jax.ShapeDtypeStruct((owns[0].shape[1], len(owns) * HD), jnp.bfloat16)
    flat = []
    for own, (swapped, back) in zip(owns, ends):
        flat += [own, swapped, back[0]]
    places = tuple(back[1] for swapped, back in ends)
    return pl.pallas_call(
        functools.partial(finish_kernel, places),
        in_specs=[pl.BlockSpec(memory_space=pltpu.SMEM)] + [vmem] * len(flat),
        out_specs=[vmem, vmem],
        out_shape=[shape, shape],
        compiler_params=pltpu.CompilerParams(vmem_limit_bytes=VMEM_LIMIT),
        cost_estimate=SMALL,
        name="finish",
    )(meta, *flat)


def join_query_kernel(count, *refs):
    core = lax.rem(lax.axis_index("ctx"), 2)
    out, sem = refs[2 * count], refs[-1]
    copies = []
    for parts, who in ((refs[:count], core), (refs[count : 2 * count], 1 - core)):
        at = 0
        for part in parts:
            width = part.shape[1]
            columns = pl.ds(pl.multiple_of(who * (out.shape[1] // 2) + at, HD), width)
            copies.append(pltpu.make_async_copy(part, out.at[:, columns], sem.at[len(copies)]))
            at += width
    for copy in copies:
        copy.start()
    for copy in copies:
        copy.wait()


def join_query(mine, theirs):
    width = 2 * sum(part.shape[1] for part in mine)
    vmem = pl.BlockSpec(memory_space=pltpu.VMEM)
    return pl.pallas_call(
        functools.partial(join_query_kernel, len(mine)),
        in_specs=[vmem] * (2 * len(mine)),
        out_specs=pl.BlockSpec(memory_space=pltpu.HBM),
        out_shape=jax.ShapeDtypeStruct((mine[0].shape[0], width), mine[0].dtype),
        scratch_shapes=[pltpu.SemaphoreType.DMA((2 * len(mine),))],
        compiler_params=pltpu.CompilerParams(vmem_limit_bytes=VMEM_LIMIT),
        cost_estimate=SMALL,
        name="join_query",
    )(*mine, *theirs)


def join_key_kernel(count, rows, k_gain, keys, *refs):
    f32 = jnp.float32
    core = lax.rem(lax.axis_index("ctx"), 2)
    key_out, value_out = refs[2 * count :]
    half = key_out.shape[1] // 2
    for parts, who in ((refs[:count], core), (refs[count : 2 * count], 1 - core)):
        at = 0
        for part in parts:
            for head in range(part.shape[1] // HD):
                columns = pl.ds(pl.multiple_of(who * half + at, HD), HD)
                inside = slice(head * HD, (head + 1) * HD)
                k = keys[:, columns].astype(f32)
                r = inverse_rms(k, -1)
                scaled = part[:rows, inside].astype(f32) * k_gain[...]
                grad = r * scaled - k * (r * r * r * jnp.mean(k * scaled, axis=-1, keepdims=True))
                key_out[:, columns] = grad.astype(key_out.dtype)
                value_out[:, columns] = part[rows:, inside]
                at += HD


def join_key(k_gain, keys, mine, theirs):
    rows, width = keys.shape
    vmem = pl.BlockSpec(memory_space=pltpu.VMEM)
    out = jax.ShapeDtypeStruct((rows, width), keys.dtype)
    return pl.pallas_call(
        functools.partial(join_key_kernel, len(mine), rows),
        in_specs=[vmem] * (2 + 2 * len(mine)),
        out_specs=[vmem, vmem],
        out_shape=[out, out],
        compiler_params=pltpu.CompilerParams(vmem_limit_bytes=VMEM_LIMIT),
        cost_estimate=SMALL,
        name="join_key",
    )(k_gain, keys, *mine, *theirs)


def lay_kernel(kv_m, kv_t, *outs):
    place = [(out, at) for out in outs for at in range(out.shape[0])]
    for part, kv in enumerate((kv_m, kv_t)):
        for head, (out, at) in enumerate(place):
            out[at, part] = kv[:, head * HD : (head + 1) * HD]


def lay(kv_m, kv_t):
    shape = lambda count: jax.ShapeDtypeStruct((count, 2, kv_m.shape[0], HD), kv_m.dtype)
    vmem = pl.BlockSpec(memory_space=pltpu.VMEM)
    return pl.pallas_call(
        lay_kernel,
        in_specs=[vmem, vmem],
        out_specs=[vmem] * (kv_m.shape[1] // HD),
        out_shape=[shape(1)] * (kv_m.shape[1] // HD),
        compiler_params=pltpu.CompilerParams(vmem_limit_bytes=VMEM_LIMIT),
        cost_estimate=SMALL,
        name="lay",
    )(kv_m, kv_t)


def after(value, *others):
    return lax.optimization_barrier((value,) + others)[0]


def on_device(queries, keys, values, out_grad, q_gain, k_gain, doc_ids):
    f32, b16 = jnp.float32, jnp.bfloat16
    rows = queries.shape[0]
    half = keys.shape[1] // 2
    pieces = half // HD
    count = lax.axis_size("ctx")
    if WINDOW != 4 * rows or count % 4 != 0:
        raise ValueError("unsupported split")
    rank = lax.axis_index("ctx")
    core = lax.rem(rank, 2)
    parity = lax.rem(lax.div(rank, 2), 2)
    odd = parity == 1
    meta = jnp.stack([core, parity]).astype(jnp.int32)

    core_swap = [(i, i ^ 1) for i in range(count)]
    x_swap = [(i, i ^ 2) for i in range(count)]
    ahead = [(i, i + 4) for i in range(count - 4)]
    back = [(i + 4, i) for i in range(count - 4)]

    def half_of(array, who):
        width = array.shape[1] // 2
        return lax.dynamic_slice(array, (0, who * width), (rows, width))

    def both(one, two, who):
        return jnp.stack([half_of(one, who), half_of(two, who)])

    id_rows = jnp.pad((doc_ids + 1).astype(b16), (0, ID_ROWS - doc_ids.shape[0]))
    id_rows = jnp.broadcast_to(id_rows[:, None], (ID_ROWS, half))

    def pack(who):
        return jnp.concatenate([half_of(keys, who), half_of(values, who), id_rows])

    kv_t = lax.ppermute(pack(1 - core), "ctx", core_swap)
    kv_m = pack(core)

    kv0 = lay(kv_m, kv_t)
    kv1, kv2 = [], []
    for block in kv0[:-1]:
        kv2.append((lax.ppermute(block, "ctx", ahead), 0))
    neighbour = lax.ppermute(kv0[-1], "ctx", x_swap)
    qg_t = lax.ppermute(both(queries, out_grad, 1 - core), "ctx", core_swap)

    q_gain_row = q_gain.reshape(1, HD)
    k_gain_row = k_gain.reshape(1, HD)
    swapped, joined, returned, results, sums_h2 = [], [], [], [], []

    def x_hop(piece, turn):
        operand = jnp.where(turn, kv2[piece][0][0], kv0[piece][0])
        kv1.append(lax.ppermute(operand, "ctx", x_swap))
        return operand

    def far_hop(turn):
        theirs = after(neighbour, turn)
        block = jnp.concatenate([kv0[-1], theirs])
        moved = lax.ppermute(block, "ctx", ahead)
        kv2.append((moved, 0))
        kv1.append(jnp.where(odd, theirs[0], moved[1]))
        return block

    def send_back(group, turn):
        block = []
        for piece in group:
            arrived = jnp.where(turn, swapped[piece].astype(f32), 0.0)
            block.append((sums_h2[piece].astype(f32) + arrived).astype(b16))
        joined.append(jnp.stack(block))
        moved = lax.ppermute(joined[-1], "ctx", back)
        returned.extend((moved, at) for at in range(len(group)))

    hop_0 = x_hop(0, odd)
    qg_m = both(queries, out_grad, after(core, hop_0))
    middle = pieces // 2
    local_part = lambda begin, order: local(
        begin, middle, order, qg_m, qg_t, kv_m, kv_t, q_gain_row, k_gain_row
    )
    prepared = [local_part(0, after(meta, hop_0, neighbour))]
    order = after(meta, x_hop(1, after(odd, prepared[0][7])))
    for piece in range(pieces):
        if piece == middle:
            prepared.append(local_part(middle, order))
        _, qn, gt, *_, total_own, out_own, doc_own = prepared[piece // middle]
        h1, h2, *result = halo(
            piece % middle, order, qn, gt, total_own, out_own, doc_own, kv1[piece], kv2[piece], k_gain_row
        )
        results.append(result)
        order = after(order, result[1])
        if piece + 3 < pieces:
            order = after(order, x_hop(piece + 2, after(odd, result[1])), far_hop(result[1]))
        swapped.append(lax.ppermute(h1, "ctx", x_swap))
        sums_h2.append(h2)
        if piece == 2:
            send_back((0, 1), after(odd, result[1]))
            order = after(order, joined[-1])
        elif piece > 2:
            send_back((piece - 1,), after(odd, result[1]))

    ends = lambda group: [(swapped[i], returned[i]) for i in group]
    late, soon = list(range(middle, pieces)), list(range(middle))

    def own_part(group, order, ends):
        qt, qn, _, k_own, kt_own, v_own, e_own, *_ = prepared[group[0] // middle]
        return own_keys(
            group, order, q_gain_row, (qt, qn, k_own, kt_own, v_own, e_own),
            [results[i] for i in group], ends,
        )

    order = after(order, joined[-1])
    dq_m_late, dq_t_late, *own_late = own_part(late, order, [])
    send_back((pieces - 1,), after(odd, dq_m_late))
    order = after(order, joined[-1], returned[0][0], returned[2][0])
    dq_m_soon, dq_t_soon, kv_m_soon, kv_t_soon = own_part(soon, order, ends(soon))
    swap = lambda array: lax.ppermute(array, "ctx", core_swap)
    query_grad = join_query([dq_m_soon, dq_m_late], [swap(dq_t_soon), swap(dq_t_late)])
    kv_m_late, kv_t_late = finish(order, own_late, ends(late))
    key_grad, value_grad = join_key(
        k_gain_row, keys, [kv_m_soon, kv_m_late], [swap(kv_t_soon), swap(kv_t_late)]
    )
    return (query_grad, key_grad, value_grad)


def solution(mesh):
    split = P(("groups", "ctx"), None)
    in_specs = (split, split, split, split, P(), P(), P(("groups", "ctx")))
    return jax.shard_map(
        on_device, mesh=mesh, in_specs=in_specs, out_specs=(split, split, split), check_vma=False
    )
```

```python
import functools

import jax
import jax.numpy as jnp
from jax import lax
from jax.experimental import pallas as pl
from jax.experimental.pallas import tpu as pltpu
from jax.sharding import PartitionSpec as P

HD = 128
WINDOW = 1024
BLK = 64
ID_ROWS = 16
VMEM_LIMIT = 12 * 1024 * 1024
HIDDEN = -1e30
SMALL = pl.CostEstimate(flops=2**20, bytes_accessed=2**16, transcendentals=0)

qk_scale = 168.0 ** (-0.5)
norm_epsilon = 1e-06


def inverse_rms(values_in, axis):
    return lax.rsqrt(jnp.mean(values_in * values_in, axis=axis, keepdims=True) + norm_epsilon)


def weights(scores, first, diagonal, token, e_ref, base):
    total = jnp.zeros((8, scores.shape[1]), jnp.float32)
    key = lax.broadcasted_iota(jnp.int32, (BLK, scores.shape[1]), 0)
    for at in range(0, scores.shape[0], BLK):
        block = scores[at : at + BLK] + jnp.where(first <= at, 0.0, HIDDEN)
        if diagonal == "window" and at < HD:
            block = jnp.where(key + at > token, block, HIDDEN)
        if diagonal == "causal" and at >= scores.shape[0] - HD:
            block = jnp.where(key + (at - scores.shape[0] + HD) <= token, block, HIDDEN)
        e = jnp.exp(block)
        total = total + jnp.sum(e.reshape(BLK // 8, 8, scores.shape[1]), axis=0)
        e_ref[base + at : base + at + BLK, :] = e.astype(e_ref.dtype)
    return jnp.sum(total, axis=0, keepdims=True)


def local_kernel(
    rows, meta, qg_m, qg_t, kv_m, kv_t, q_gain, k_gain,
    qt, qn, gt, k_own, kt_own, v_own, e_own, total_own, out_own, doc_own,
):
    f32, b16 = jnp.float32, jnp.bfloat16
    core = meta[0]
    wide = qt.shape[-1]
    blocks = rows // BLK
    runs = rows // HD
    gain = jnp.broadcast_to(q_gain[...], (HD, HD)).T * qk_scale
    gain = jnp.concatenate([gain] * (wide // HD), axis=1)
    for part, (qg, kv) in enumerate(((qg_m, kv_m), (qg_t, kv_t))):
        slot = core if part == 0 else 1 - core
        for head in range(wide // HD):
            columns = slice(head * HD, (head + 1) * HD)
            q, g = qg[0, :, columns].T, qg[1, :, columns].T
            for run in range(runs):
                tokens = slice(run * HD, (run + 1) * HD)
                qt[slot * runs + run, :, columns] = q[:, tokens]
                gt[slot * runs + run, :, columns] = g[:, tokens]
        off = pl.multiple_of(slot * rows, rows)
        k = kv[:rows].astype(f32)
        kn = (k * inverse_rms(k, -1) * k_gain[...]).astype(b16)
        k_own[pl.ds(off, rows), :] = kn
        kt_own[:, pl.ds(off, rows)] = kn.T
        v_own[pl.ds(off, rows), :] = kv[rows : 2 * rows]
    token = lax.rem(lax.broadcasted_iota(jnp.int32, (1, wide), 1), HD)
    ids = [[kv[2 * rows :, :1].astype(f32)[b : b + 1] for b in range(blocks)] for kv in (kv_m, kv_t)]
    base = 0
    for run in range(2 * runs):
        slot, inside = divmod(run * HD, rows)
        doc = jnp.zeros((1, wide), f32)
        for b in range(HD // BLK):
            at = inside // BLK + b
            here = jnp.where(core == slot, ids[0][at], ids[1][at])
            doc = jnp.where(token >= b * BLK, here, doc)
        doc_own[run] = doc
        earlier = jnp.zeros((1, wide), f32)
        for one in ids[0] + ids[1]:
            earlier = earlier + (one < doc).astype(f32)
        first = earlier.astype(jnp.int32) * BLK
        q = qt[run].astype(f32)
        qn_run = (q * inverse_rms(q, 0) * gain).astype(b16)
        qn[run] = qn_run
        count = (run + 1) * HD
        s = jnp.dot(k_own[:count, :], qn_run, preferred_element_type=f32)
        total_own[run] = weights(s, first, "causal", token, e_own, base)
        vt = v_own[:count, :].T
        out_own[run] = jnp.dot(vt, e_own[base : base + count, :], preferred_element_type=f32)
        base += count


def local(begin, heads, meta, qg_m, qg_t, kv_m, kv_t, q_gain, k_gain):
    f32, b16 = jnp.float32, jnp.bfloat16
    rows = qg_m.shape[1]
    group_cols = qg_m.shape[2] // (kv_m.shape[1] // HD)
    runs = 2 * rows // HD
    pairs = HD * runs * (runs + 1) // 2
    qg = pl.BlockSpec((2, rows, group_cols), lambda h, meta: (0, 0, begin + h))
    kv = pl.BlockSpec((kv_m.shape[0], HD), lambda h, meta: (0, begin + h))
    row = pl.BlockSpec((1, HD), lambda h, meta: (0, 0))
    out = lambda dtype, *shape: (
        pl.BlockSpec((None,) + shape, lambda h, meta: (h,) + (0,) * len(shape)),
        jax.ShapeDtypeStruct((heads,) + shape, dtype),
    )
    outs = [
        out(b16, runs, HD, group_cols), out(b16, runs, HD, group_cols),
        out(b16, runs, HD, group_cols), out(b16, 2 * rows, HD), out(b16, HD, 2 * rows),
        out(b16, 2 * rows, HD), out(b16, pairs, group_cols), out(f32, runs, 1, group_cols),
        out(f32, runs, HD, group_cols), out(f32, runs, 1, group_cols),
    ]
    return pl.pallas_call(
        functools.partial(local_kernel, rows),
        grid_spec=pltpu.PrefetchScalarGridSpec(
            num_scalar_prefetch=1,
            grid=(heads,),
            in_specs=[qg, qg, kv, kv, row, row],
            out_specs=[one[0] for one in outs],
        ),
        out_shape=[one[1] for one in outs],
        compiler_params=pltpu.CompilerParams(vmem_limit_bytes=VMEM_LIMIT),
        cost_estimate=SMALL,
        name=f"local_{begin}",
    )(meta, qg_m, qg_t, kv_m, kv_t, q_gain, k_gain)


def halo_kernel(
    piece, at, rows, meta, qn, gt, total_own, out_own, doc_own, kv1, kv2, k_gain,
    h1, h2, g_out, delta_out, dq_out,
    k_s, kt_s, v_s, vt_s, dk_s, dv_s, e_s,
):
    f32, b16 = jnp.float32, jnp.bfloat16
    core = meta[0]
    wide = qn.shape[-1]
    blocks = rows // BLK
    sources = ((kv2.at[at], 0), (kv1, 2 * rows))

    for source, base in sources:
        for part in range(2):
            off = pl.multiple_of(base + (core if part == 0 else 1 - core) * rows, rows)
            k = source[part, :rows].astype(f32)
            kn = (k * inverse_rms(k, -1) * k_gain[...]).astype(b16)
            k_s[pl.ds(off, rows), :] = kn
            kt_s[:, pl.ds(off, rows)] = kn.T
            v = source[part, rows : 2 * rows]
            v_s[pl.ds(off, rows), :] = v
            vt_s[:, pl.ds(off, rows)] = v.T

    token = lax.rem(lax.broadcasted_iota(jnp.int32, (1, wide), 1), HD)
    nt = (((1,), (1,)), ((), ()))
    ids = [
        source[part, 2 * rows :, :1].astype(f32)[b : b + 1]
        for source, base in sources
        for part in range(2)
        for b in range(blocks)
    ]
    runs = 2 * rows // HD

    def forward(run):
        low = run * HD
        doc = doc_own[piece, run]
        earlier = jnp.zeros((1, wide), f32)
        for one in ids:
            earlier = earlier + (one < doc).astype(f32)
        first = earlier.astype(jnp.int32) * BLK - low
        s = jnp.dot(k_s[low:, :], qn[piece, run], preferred_element_type=f32)
        e_run = e_s.at[run % 2]
        total = total_own[piece, run] + weights(s, first, "window", token, e_run, low)
        out = jnp.dot(vt_s[:, low:], e_run[low:, :], preferred_element_type=f32)
        return total, out_own[piece, run] + out

    def backward(run, total, out):
        low = run * HD
        qn_run = qn[piece, run]
        e = e_s[run % 2, low:, :]
        inverse = 1.0 / total
        g_l = (gt[piece, run].astype(f32) * inverse).astype(b16)
        delta = jnp.sum(g_l.astype(f32) * (out * inverse), axis=0, keepdims=True)
        g_out[run] = g_l
        delta_out[run] = delta
        dp = jnp.dot(v_s[low:, :], g_l, preferred_element_type=f32)
        ds = (e.astype(f32) * (dp - delta)).astype(b16)
        dv = lax.dot_general(e, g_l, nt, preferred_element_type=f32)
        dk = lax.dot_general(ds, qn_run, nt, preferred_element_type=f32)
        dv_s[low:, :] = dv if run == 0 else dv_s[low:, :] + dv
        dk_s[low:, :] = dk if run == 0 else dk_s[low:, :] + dk
        dq_out[run] = jnp.dot(kt_s[:, low:], ds, preferred_element_type=f32)

    state = forward(0)
    for run in range(runs):
        following = forward(run + 1) if run + 1 < runs else None
        backward(run, *state)
        state = following

    for target, base in ((h2, 0), (h1, 2 * rows)):
        for part in range(2):
            off = pl.multiple_of(base + (core if part == 0 else 1 - core) * rows, rows)
            target[part, :rows] = dk_s[pl.ds(off, rows), :].astype(b16)
            target[part, rows:] = dv_s[pl.ds(off, rows), :].astype(b16)


def halo(piece, meta, qn, gt, total_own, out_own, doc_own, kv1, kv2, k_gain):
    array, at = kv2
    rows = (array.shape[2] - ID_ROWS) // 2
    runs, wide = qn.shape[1], qn.shape[-1]
    f32, b16 = jnp.float32, jnp.bfloat16
    vmem = pl.BlockSpec(memory_space=pltpu.VMEM)
    return pl.pallas_call(
        functools.partial(halo_kernel, piece, at, rows),
        in_specs=[pl.BlockSpec(memory_space=pltpu.SMEM)] + [vmem] * 8,
        out_specs=[vmem] * 5,
        scratch_shapes=[
            pltpu.VMEM((WINDOW, HD), b16),
            pltpu.VMEM((HD, WINDOW), b16),
            pltpu.VMEM((WINDOW, HD), b16),
            pltpu.VMEM((HD, WINDOW), b16),
            pltpu.VMEM((WINDOW, HD), f32),
            pltpu.VMEM((WINDOW, HD), f32),
            pltpu.VMEM((2, WINDOW, wide), b16),
        ],
        out_shape=[
            jax.ShapeDtypeStruct((2, 2 * rows, HD), b16),
            jax.ShapeDtypeStruct((2, 2 * rows, HD), b16),
            jax.ShapeDtypeStruct((runs, HD, wide), b16),
            jax.ShapeDtypeStruct((runs, 1, wide), f32),
            jax.ShapeDtypeStruct((runs, HD, wide), f32),
        ],
        compiler_params=pltpu.CompilerParams(vmem_limit_bytes=VMEM_LIMIT),
        cost_estimate=SMALL,
        name=f"halo_{piece}",
    )(meta, qn, gt, total_own, out_own, doc_own, kv1, array, k_gain)


def key_sum(even, own, swapped, returned):
    f32 = jnp.float32
    return own + returned.astype(f32) + jnp.where(even, swapped.astype(f32), 0.0)


def own_kernel(
    pieces, places, rows, meta, q_gain, qt, qn, k_own, kt_own, v_own, e_own, *refs
):
    f32, b16 = jnp.float32, jnp.bfloat16
    core, even = meta[0], meta[1] == 0
    count = len(pieces)
    inputs, refs = refs[: 3 * count], refs[3 * count :]
    ends, refs = refs[: 2 * len(places)], refs[2 * len(places) :]
    (dq_m, dq_t), outs, (dq_s, dk_s, dv_s) = refs[:2], refs[2:-3], refs[-3:]
    runs, wide = qt.shape[1], qt.shape[-1]
    nt = (((1,), (1,)), ((), ()))
    gain = jnp.broadcast_to(q_gain[...], (HD, HD)).T * qk_scale
    gain = jnp.concatenate([gain] * (wide // HD), axis=1)
    for at, piece in enumerate(pieces):
        g_in, delta_in, dq_in = inputs[3 * at : 3 * at + 3]
        base = runs * (runs + 1) // 2 * HD
        for run in reversed(range(runs)):
            keys = (run + 1) * HD
            base -= keys
            g_l, qn_run = g_in[run], qn[piece, run]
            e = e_own[piece, base : base + keys, :]
            dp = jnp.dot(v_own[piece, :keys, :], g_l, preferred_element_type=f32)
            ds = (e.astype(f32) * (dp - delta_in[run])).astype(b16)
            dv = lax.dot_general(e, g_l, nt, preferred_element_type=f32)
            dk = lax.dot_general(ds, qn_run, nt, preferred_element_type=f32)
            dv_s[:keys, :] = dv if run == runs - 1 else dv_s[:keys, :] + dv
            dk_s[:keys, :] = dk if run == runs - 1 else dk_s[:keys, :] + dk
            dq = dq_in[run] + jnp.dot(kt_own[piece, :, :keys], ds, preferred_element_type=f32)
            q = qt[piece, run].astype(f32)
            r = inverse_rms(q, 0)
            scaled = dq * gain
            dq = r * scaled - q * (r * r * r * jnp.mean(q * scaled, axis=0, keepdims=True))
            slot, inside = divmod(run * HD, rows)
            for head in range(wide // HD):
                lanes = slice(head * HD, (head + 1) * HD)
                columns = slice(at * wide + head * HD, at * wide + (head + 1) * HD)
                dq_s[slot, inside : inside + HD, columns] = dq[:, lanes].T.astype(b16)
        for part in range(2):
            tokens = pl.ds(pl.multiple_of((core if part == 0 else 1 - core) * rows, rows), rows)
            if places:
                swapped, returned = ends[2 * at : 2 * at + 2]
                columns = slice(at * HD, (at + 1) * HD)
                for which, sums in enumerate((dk_s, dv_s)):
                    span = slice(which * rows, (which + 1) * rows)
                    total = key_sum(
                        even, sums[tokens, :], swapped[part, span], returned[places[at], part, span]
                    )
                    outs[part][span, columns] = total.astype(b16)
            else:
                outs[at][part, :rows] = dk_s[tokens, :]
                outs[at][part, rows:] = dv_s[tokens, :]
    dq_m[...] = dq_s[core]
    dq_t[...] = dq_s[1 - core]


def own_keys(pieces, meta, q_gain, prepared, results, ends):
    qt, qn, k_own, kt_own, v_own, e_own = prepared
    rows = k_own.shape[1] // 2
    columns = len(pieces) * qt.shape[-1]
    f32, b16 = jnp.float32, jnp.bfloat16
    vmem = pl.BlockSpec(memory_space=pltpu.VMEM)
    dq = jax.ShapeDtypeStruct((rows, columns), b16)
    own = jax.ShapeDtypeStruct((2, 2 * rows, HD), f32)
    final = jax.ShapeDtypeStruct((2 * rows, len(pieces) * HD), b16)
    flat = [one for result in results for one in result]
    flat += [one for swapped, back in ends for one in (swapped, back[0])]
    places = tuple(back[1] for swapped, back in ends)
    outs = [dq, dq] + ([final] * 2 if ends else [own] * len(pieces))
    return pl.pallas_call(
        functools.partial(own_kernel, tuple(range(len(pieces))), places, rows),
        in_specs=[pl.BlockSpec(memory_space=pltpu.SMEM)] + [vmem] * (7 + len(flat)),
        out_specs=[vmem] * len(outs),
        scratch_shapes=[
            pltpu.VMEM((2, rows, columns), b16),
            pltpu.VMEM((2 * rows, HD), f32),
            pltpu.VMEM((2 * rows, HD), f32),
        ],
        out_shape=outs,
        compiler_params=pltpu.CompilerParams(vmem_limit_bytes=VMEM_LIMIT),
        cost_estimate=pl.CostEstimate(flops=2**32, bytes_accessed=2**22, transcendentals=0),
        name=f"own_{pieces[0]}",
    )(meta, q_gain, *prepared, *flat)


def finish_kernel(places, meta, *refs):
    outs = refs[3 * len(places) :]
    for at, at_returned in enumerate(places):
        own, swapped, returned = refs[3 * at : 3 * at + 3]
        for part in range(2):
            total = key_sum(meta[1] == 0, own[part], swapped[part], returned[at_returned, part])
            outs[part][:, at * HD : (at + 1) * HD] = total.astype(outs[part].dtype)


def finish(meta, owns, ends):
    vmem = pl.BlockSpec(memory_space=pltpu.VMEM)
    shape = jax.ShapeDtypeStruct((owns[0].shape[1], len(owns) * HD), jnp.bfloat16)
    flat = []
    for own, (swapped, back) in zip(owns, ends):
        flat += [own, swapped, back[0]]
    places = tuple(back[1] for swapped, back in ends)
    return pl.pallas_call(
        functools.partial(finish_kernel, places),
        in_specs=[pl.BlockSpec(memory_space=pltpu.SMEM)] + [vmem] * len(flat),
        out_specs=[vmem, vmem],
        out_shape=[shape, shape],
        compiler_params=pltpu.CompilerParams(vmem_limit_bytes=VMEM_LIMIT),
        cost_estimate=SMALL,
        name="finish",
    )(meta, *flat)


def join_query_kernel(count, *refs):
    core = lax.rem(lax.axis_index("ctx"), 2)
    out, sem = refs[2 * count], refs[-1]
    copies = []
    for parts, who in ((refs[:count], core), (refs[count : 2 * count], 1 - core)):
        at = 0
        for part in parts:
            width = part.shape[1]
            columns = pl.ds(pl.multiple_of(who * (out.shape[1] // 2) + at, HD), width)
            copies.append(pltpu.make_async_copy(part, out.at[:, columns], sem.at[len(copies)]))
            at += width
    for copy in copies:
        copy.start()
    for copy in copies:
        copy.wait()


def join_query(mine, theirs):
    width = 2 * sum(part.shape[1] for part in mine)
    vmem = pl.BlockSpec(memory_space=pltpu.VMEM)
    return pl.pallas_call(
        functools.partial(join_query_kernel, len(mine)),
        in_specs=[vmem] * (2 * len(mine)),
        out_specs=pl.BlockSpec(memory_space=pltpu.HBM),
        out_shape=jax.ShapeDtypeStruct((mine[0].shape[0], width), mine[0].dtype),
        scratch_shapes=[pltpu.SemaphoreType.DMA((2 * len(mine),))],
        compiler_params=pltpu.CompilerParams(vmem_limit_bytes=VMEM_LIMIT),
        cost_estimate=SMALL,
        name="join_query",
    )(*mine, *theirs)


def join_key_kernel(count, rows, k_gain, keys, *refs):
    f32 = jnp.float32
    core = lax.rem(lax.axis_index("ctx"), 2)
    key_out, value_out = refs[2 * count :]
    half = key_out.shape[1] // 2
    for parts, who in ((refs[:count], core), (refs[count : 2 * count], 1 - core)):
        at = 0
        for part in parts:
            for head in range(part.shape[1] // HD):
                columns = pl.ds(pl.multiple_of(who * half + at, HD), HD)
                inside = slice(head * HD, (head + 1) * HD)
                k = keys[:, columns].astype(f32)
                r = inverse_rms(k, -1)
                scaled = part[:rows, inside].astype(f32) * k_gain[...]
                grad = r * scaled - k * (r * r * r * jnp.mean(k * scaled, axis=-1, keepdims=True))
                key_out[:, columns] = grad.astype(key_out.dtype)
                value_out[:, columns] = part[rows:, inside]
                at += HD


def join_key(k_gain, keys, mine, theirs):
    rows, width = keys.shape
    vmem = pl.BlockSpec(memory_space=pltpu.VMEM)
    out = jax.ShapeDtypeStruct((rows, width), keys.dtype)
    return pl.pallas_call(
        functools.partial(join_key_kernel, len(mine), rows),
        in_specs=[vmem] * (2 + 2 * len(mine)),
        out_specs=[vmem, vmem],
        out_shape=[out, out],
        compiler_params=pltpu.CompilerParams(vmem_limit_bytes=VMEM_LIMIT),
        cost_estimate=SMALL,
        name="join_key",
    )(k_gain, keys, *mine, *theirs)


def lay_kernel(kv_m, kv_t, *outs):
    place = [(out, at) for out in outs for at in range(out.shape[0])]
    for part, kv in enumerate((kv_m, kv_t)):
        for head, (out, at) in enumerate(place):
            out[at, part] = kv[:, head * HD : (head + 1) * HD]


def lay(kv_m, kv_t):
    shape = lambda count: jax.ShapeDtypeStruct((count, 2, kv_m.shape[0], HD), kv_m.dtype)
    vmem = pl.BlockSpec(memory_space=pltpu.VMEM)
    return pl.pallas_call(
        lay_kernel,
        in_specs=[vmem, vmem],
        out_specs=[vmem] * (kv_m.shape[1] // HD),
        out_shape=[shape(1)] * (kv_m.shape[1] // HD),
        compiler_params=pltpu.CompilerParams(vmem_limit_bytes=VMEM_LIMIT),
        cost_estimate=SMALL,
        name="lay",
    )(kv_m, kv_t)


def after(value, *others):
    return lax.optimization_barrier((value,) + others)[0]


def on_device(queries, keys, values, out_grad, q_gain, k_gain, doc_ids):
    f32, b16 = jnp.float32, jnp.bfloat16
    rows = queries.shape[0]
    half = keys.shape[1] // 2
    pieces = half // HD
    count = lax.axis_size("ctx")
    if WINDOW != 4 * rows or count % 4 != 0:
        raise ValueError("unsupported split")
    rank = lax.axis_index("ctx")
    core = lax.rem(rank, 2)
    parity = lax.rem(lax.div(rank, 2), 2)
    odd = parity == 1
    meta = jnp.stack([core, parity]).astype(jnp.int32)

    core_swap = [(i, i ^ 1) for i in range(count)]
    x_swap = [(i, i ^ 2) for i in range(count)]
    ahead = [(i, i + 4) for i in range(count - 4)]
    back = [(i + 4, i) for i in range(count - 4)]

    def half_of(array, who):
        width = array.shape[1] // 2
        return lax.dynamic_slice(array, (0, who * width), (rows, width))

    def both(one, two, who):
        return jnp.stack([half_of(one, who), half_of(two, who)])

    id_rows = jnp.pad((doc_ids + 1).astype(b16), (0, ID_ROWS - doc_ids.shape[0]))
    id_rows = jnp.broadcast_to(id_rows[:, None], (ID_ROWS, half))

    def pack(who):
        return jnp.concatenate([half_of(keys, who), half_of(values, who), id_rows])

    kv_t = lax.ppermute(pack(1 - core), "ctx", core_swap)
    kv_m = pack(core)

    kv0 = lay(kv_m, kv_t)
    kv1, kv2 = [], []
    for block in kv0[:2]:
        kv2.append((lax.ppermute(block, "ctx", ahead), 0))
    neighbour = lax.ppermute(kv0[-1], "ctx", x_swap)
    qg_m = both(queries, out_grad, core)
    qg_t = lax.ppermute(both(queries, out_grad, 1 - core), "ctx", core_swap)

    q_gain_row = q_gain.reshape(1, HD)
    k_gain_row = k_gain.reshape(1, HD)
    swapped, joined, returned, results, sums_h2 = [], [], [], [], []

    def x_hop(piece, turn):
        operand = jnp.where(turn, kv2[piece][0][0], kv0[piece][0])
        kv1.append(lax.ppermute(operand, "ctx", x_swap))
        return operand

    def far_hop(turn):
        theirs = after(neighbour, turn)
        block = jnp.concatenate([kv0[-1], theirs])
        moved = lax.ppermute(block, "ctx", ahead)
        kv2.append((moved, 0))
        kv1.append(jnp.where(odd, theirs[0], moved[1]))
        return block

    def send_back(group, turn):
        block = []
        for piece in group:
            arrived = jnp.where(turn, swapped[piece].astype(f32), 0.0)
            block.append((sums_h2[piece].astype(f32) + arrived).astype(b16))
        joined.append(jnp.stack(block))
        moved = lax.ppermute(joined[-1], "ctx", back)
        returned.extend((moved, at) for at in range(len(group)))

    hop_0 = x_hop(0, odd)
    for block in kv0[2:-1]:
        kv2.append((lax.ppermute(after(block, hop_0), "ctx", ahead), 0))
    middle = pieces // 2
    local_part = lambda begin, order: local(
        begin, middle, order, qg_m, qg_t, kv_m, kv_t, q_gain_row, k_gain_row
    )
    prepared = [local_part(0, after(meta, hop_0, neighbour))]
    order = after(meta, x_hop(1, after(odd, prepared[0][7])))
    for piece in range(pieces):
        if piece == middle:
            prepared.append(local_part(middle, order))
        _, qn, gt, *_, total_own, out_own, doc_own = prepared[piece // middle]
        h1, h2, *result = halo(
            piece % middle, order, qn, gt, total_own, out_own, doc_own, kv1[piece], kv2[piece], k_gain_row
        )
        results.append(result)
        order = after(order, result[1])
        if piece + 3 < pieces:
            order = after(order, x_hop(piece + 2, after(odd, result[1])), far_hop(result[1]))
        swapped.append(lax.ppermute(h1, "ctx", x_swap))
        sums_h2.append(h2)
        if piece == 2:
            send_back((0, 1), after(odd, result[1]))
            order = after(order, joined[-1])
        elif piece > 2:
            send_back((piece - 1,), after(odd, result[1]))

    ends = lambda group: [(swapped[i], returned[i]) for i in group]
    late, soon = list(range(middle, pieces)), list(range(middle))

    def own_part(group, order, ends):
        qt, qn, _, k_own, kt_own, v_own, e_own, *_ = prepared[group[0] // middle]
        return own_keys(
            group, order, q_gain_row, (qt, qn, k_own, kt_own, v_own, e_own),
            [results[i] for i in group], ends,
        )

    order = after(order, joined[-1])
    dq_m_late, dq_t_late, *own_late = own_part(late, order, [])
    send_back((pieces - 1,), after(odd, dq_m_late))
    order = after(order, joined[-1], returned[0][0], returned[2][0])
    dq_m_soon, dq_t_soon, kv_m_soon, kv_t_soon = own_part(soon, order, ends(soon))
    swap = lambda array: lax.ppermute(array, "ctx", core_swap)
    query_grad = join_query([dq_m_soon, dq_m_late], [swap(dq_t_soon), swap(dq_t_late)])
    kv_m_late, kv_t_late = finish(order, own_late, ends(late))
    key_grad, value_grad = join_key(
        k_gain_row, keys, [kv_m_soon, kv_m_late], [swap(kv_t_soon), swap(kv_t_late)]
    )
    return (query_grad, key_grad, value_grad)


def solution(mesh):
    split = P(("groups", "ctx"), None)
    in_specs = (split, split, split, split, P(), P(), P(("groups", "ctx")))
    return jax.shard_map(
        on_device, mesh=mesh, in_specs=in_specs, out_specs=(split, split, split), check_vma=False
    )
```

```python
import functools

import jax
import jax.numpy as jnp
from jax import lax
from jax.experimental import pallas as pl
from jax.experimental.pallas import tpu as pltpu
from jax.sharding import PartitionSpec as P

HD = 128
WINDOW = 1024
BLK = 64
ID_ROWS = 16
VMEM_LIMIT = 12 * 1024 * 1024
HIDDEN = -1e30
SMALL = pl.CostEstimate(flops=2**20, bytes_accessed=2**16, transcendentals=0)

qk_scale = 168.0 ** (-0.5)
norm_epsilon = 1e-06


def inverse_rms(values_in, axis):
    return lax.rsqrt(jnp.mean(values_in * values_in, axis=axis, keepdims=True) + norm_epsilon)


def weights(scores, first, diagonal, token, e_ref, base):
    total = jnp.zeros((8, scores.shape[1]), jnp.float32)
    key = lax.broadcasted_iota(jnp.int32, (BLK, scores.shape[1]), 0)
    for at in range(0, scores.shape[0], BLK):
        block = scores[at : at + BLK] + jnp.where(first <= at, 0.0, HIDDEN)
        if diagonal == "window" and at < HD:
            block = jnp.where(key + at > token, block, HIDDEN)
        if diagonal == "causal" and at >= scores.shape[0] - HD:
            block = jnp.where(key + (at - scores.shape[0] + HD) <= token, block, HIDDEN)
        e = jnp.exp(block)
        total = total + jnp.sum(e.reshape(BLK // 8, 8, scores.shape[1]), axis=0)
        e_ref[base + at : base + at + BLK, :] = e.astype(e_ref.dtype)
    return jnp.sum(total, axis=0, keepdims=True)


def local_kernel(
    rows, meta, qg_m, qg_t, kv_m, kv_t, q_gain, k_gain,
    qt, qn, gt, k_own, kt_own, v_own, e_own, total_own, out_own, doc_own,
):
    f32, b16 = jnp.float32, jnp.bfloat16
    core = meta[0]
    wide = qt.shape[-1]
    blocks = rows // BLK
    runs = rows // HD
    gain = jnp.broadcast_to(q_gain[...], (HD, HD)).T * qk_scale
    gain = jnp.concatenate([gain] * (wide // HD), axis=1)
    for part, (qg, kv) in enumerate(((qg_m, kv_m), (qg_t, kv_t))):
        slot = core if part == 0 else 1 - core
        for head in range(wide // HD):
            columns = slice(head * HD, (head + 1) * HD)
            q, g = qg[0, :, columns].T, qg[1, :, columns].T
            for run in range(runs):
                tokens = slice(run * HD, (run + 1) * HD)
                qt[slot * runs + run, :, columns] = q[:, tokens]
                gt[slot * runs + run, :, columns] = g[:, tokens]
        off = pl.multiple_of(slot * rows, rows)
        k = kv[:rows].astype(f32)
        kn = (k * inverse_rms(k, -1) * k_gain[...]).astype(b16)
        k_own[pl.ds(off, rows), :] = kn
        kt_own[:, pl.ds(off, rows)] = kn.T
        v_own[pl.ds(off, rows), :] = kv[rows : 2 * rows]
    token = lax.rem(lax.broadcasted_iota(jnp.int32, (1, wide), 1), HD)
    ids = [[kv[2 * rows :, :1].astype(f32)[b : b + 1] for b in range(blocks)] for kv in (kv_m, kv_t)]
    base = 0
    for run in range(2 * runs):
        slot, inside = divmod(run * HD, rows)
        doc = jnp.zeros((1, wide), f32)
        for b in range(HD // BLK):
            at = inside // BLK + b
            here = jnp.where(core == slot, ids[0][at], ids[1][at])
            doc = jnp.where(token >= b * BLK, here, doc)
        doc_own[run] = doc
        earlier = jnp.zeros((1, wide), f32)
        for one in ids[0] + ids[1]:
            earlier = earlier + (one < doc).astype(f32)
        first = earlier.astype(jnp.int32) * BLK
        q = qt[run].astype(f32)
        qn_run = (q * inverse_rms(q, 0) * gain).astype(b16)
        qn[run] = qn_run
        count = (run + 1) * HD
        s = jnp.dot(k_own[:count, :], qn_run, preferred_element_type=f32)
        total_own[run] = weights(s, first, "causal", token, e_own, base)
        vt = v_own[:count, :].T
        out_own[run] = jnp.dot(vt, e_own[base : base + count, :], preferred_element_type=f32)
        base += count


def local(begin, heads, meta, qg_m, qg_t, kv_m, kv_t, q_gain, k_gain):
    f32, b16 = jnp.float32, jnp.bfloat16
    rows = qg_m.shape[1]
    group_cols = qg_m.shape[2] // (kv_m.shape[1] // HD)
    runs = 2 * rows // HD
    pairs = HD * runs * (runs + 1) // 2
    qg = pl.BlockSpec((2, rows, group_cols), lambda h, meta: (0, 0, begin + h))
    kv = pl.BlockSpec((kv_m.shape[0], HD), lambda h, meta: (0, begin + h))
    row = pl.BlockSpec((1, HD), lambda h, meta: (0, 0))
    out = lambda dtype, *shape: (
        pl.BlockSpec((None,) + shape, lambda h, meta: (h,) + (0,) * len(shape)),
        jax.ShapeDtypeStruct((heads,) + shape, dtype),
    )
    outs = [
        out(b16, runs, HD, group_cols), out(b16, runs, HD, group_cols),
        out(b16, runs, HD, group_cols), out(b16, 2 * rows, HD), out(b16, HD, 2 * rows),
        out(b16, 2 * rows, HD), out(b16, pairs, group_cols), out(f32, runs, 1, group_cols),
        out(f32, runs, HD, group_cols), out(f32, runs, 1, group_cols),
    ]
    return pl.pallas_call(
        functools.partial(local_kernel, rows),
        grid_spec=pltpu.PrefetchScalarGridSpec(
            num_scalar_prefetch=1,
            grid=(heads,),
            in_specs=[qg, qg, kv, kv, row, row],
            out_specs=[one[0] for one in outs],
        ),
        out_shape=[one[1] for one in outs],
        compiler_params=pltpu.CompilerParams(vmem_limit_bytes=VMEM_LIMIT),
        cost_estimate=SMALL,
        name=f"local_{begin}",
    )(meta, qg_m, qg_t, kv_m, kv_t, q_gain, k_gain)


def halo_kernel(
    piece, at, rows, meta, qn, gt, total_own, out_own, doc_own, kv1, kv2, k_gain,
    h1, h2, g_out, delta_out, dq_out,
    k_s, kt_s, v_s, vt_s, dk_s, dv_s, e_s,
):
    f32, b16 = jnp.float32, jnp.bfloat16
    core = meta[0]
    wide = qn.shape[-1]
    blocks = rows // BLK
    sources = ((kv2.at[at], 0), (kv1, 2 * rows))

    for source, base in sources:
        for part in range(2):
            off = pl.multiple_of(base + (core if part == 0 else 1 - core) * rows, rows)
            k = source[part, :rows].astype(f32)
            kn = (k * inverse_rms(k, -1) * k_gain[...]).astype(b16)
            k_s[pl.ds(off, rows), :] = kn
            kt_s[:, pl.ds(off, rows)] = kn.T
            v = source[part, rows : 2 * rows]
            v_s[pl.ds(off, rows), :] = v
            vt_s[:, pl.ds(off, rows)] = v.T

    token = lax.rem(lax.broadcasted_iota(jnp.int32, (1, wide), 1), HD)
    nt = (((1,), (1,)), ((), ()))
    ids = [
        source[part, 2 * rows :, :1].astype(f32)[b : b + 1]
        for source, base in sources
        for part in range(2)
        for b in range(blocks)
    ]
    runs = 2 * rows // HD

    def forward(run):
        low = run * HD
        doc = doc_own[piece, run]
        earlier = jnp.zeros((1, wide), f32)
        for one in ids:
            earlier = earlier + (one < doc).astype(f32)
        first = earlier.astype(jnp.int32) * BLK - low
        s = jnp.dot(k_s[low:, :], qn[piece, run], preferred_element_type=f32)
        e_run = e_s.at[run % 2]
        total = total_own[piece, run] + weights(s, first, "window", token, e_run, low)
        out = jnp.dot(vt_s[:, low:], e_run[low:, :], preferred_element_type=f32)
        return total, out_own[piece, run] + out

    def backward(run, total, out):
        low = run * HD
        qn_run = qn[piece, run]
        e = e_s[run % 2, low:, :]
        inverse = 1.0 / total
        g_l = (gt[piece, run].astype(f32) * inverse).astype(b16)
        delta = jnp.sum(g_l.astype(f32) * (out * inverse), axis=0, keepdims=True)
        g_out[run] = g_l
        delta_out[run] = delta
        dp = jnp.dot(v_s[low:, :], g_l, preferred_element_type=f32)
        ds = (e.astype(f32) * (dp - delta)).astype(b16)
        dv = lax.dot_general(e, g_l, nt, preferred_element_type=f32)
        dk = lax.dot_general(ds, qn_run, nt, preferred_element_type=f32)
        dv_s[low:, :] = dv if run == 0 else dv_s[low:, :] + dv
        dk_s[low:, :] = dk if run == 0 else dk_s[low:, :] + dk
        dq_out[run] = jnp.dot(kt_s[:, low:], ds, preferred_element_type=f32)

    state = forward(0)
    for run in range(runs):
        following = forward(run + 1) if run + 1 < runs else None
        backward(run, *state)
        state = following

    for target, base in ((h2, 0), (h1, 2 * rows)):
        for part in range(2):
            off = pl.multiple_of(base + (core if part == 0 else 1 - core) * rows, rows)
            target[part, :rows] = dk_s[pl.ds(off, rows), :].astype(b16)
            target[part, rows:] = dv_s[pl.ds(off, rows), :].astype(b16)


def halo(piece, meta, qn, gt, total_own, out_own, doc_own, kv1, kv2, k_gain):
    array, at = kv2
    rows = (array.shape[2] - ID_ROWS) // 2
    runs, wide = qn.shape[1], qn.shape[-1]
    f32, b16 = jnp.float32, jnp.bfloat16
    vmem = pl.BlockSpec(memory_space=pltpu.VMEM)
    return pl.pallas_call(
        functools.partial(halo_kernel, piece, at, rows),
        in_specs=[pl.BlockSpec(memory_space=pltpu.SMEM)] + [vmem] * 8,
        out_specs=[vmem] * 5,
        scratch_shapes=[
            pltpu.VMEM((WINDOW, HD), b16),
            pltpu.VMEM((HD, WINDOW), b16),
            pltpu.VMEM((WINDOW, HD), b16),
            pltpu.VMEM((HD, WINDOW), b16),
            pltpu.VMEM((WINDOW, HD), f32),
            pltpu.VMEM((WINDOW, HD), f32),
            pltpu.VMEM((2, WINDOW, wide), b16),
        ],
        out_shape=[
            jax.ShapeDtypeStruct((2, 2 * rows, HD), b16),
            jax.ShapeDtypeStruct((2, 2 * rows, HD), b16),
            jax.ShapeDtypeStruct((runs, HD, wide), b16),
            jax.ShapeDtypeStruct((runs, 1, wide), f32),
            jax.ShapeDtypeStruct((runs, HD, wide), f32),
        ],
        compiler_params=pltpu.CompilerParams(vmem_limit_bytes=VMEM_LIMIT),
        cost_estimate=SMALL,
        name=f"halo_{piece}",
    )(meta, qn, gt, total_own, out_own, doc_own, kv1, array, k_gain)


def key_sum(even, own, swapped, returned):
    f32 = jnp.float32
    return own + returned.astype(f32) + jnp.where(even, swapped.astype(f32), 0.0)


def own_kernel(
    pieces, places, rows, meta, q_gain, qt, qn, k_own, kt_own, v_own, e_own, *refs
):
    f32, b16 = jnp.float32, jnp.bfloat16
    core, even = meta[0], meta[1] == 0
    count = len(pieces)
    inputs, refs = refs[: 3 * count], refs[3 * count :]
    ends, refs = refs[: 2 * len(places)], refs[2 * len(places) :]
    (dq_m, dq_t), outs, (dq_s, dk_s, dv_s) = refs[:2], refs[2:-3], refs[-3:]
    runs, wide = qt.shape[1], qt.shape[-1]
    nt = (((1,), (1,)), ((), ()))
    gain = jnp.broadcast_to(q_gain[...], (HD, HD)).T * qk_scale
    gain = jnp.concatenate([gain] * (wide // HD), axis=1)
    for at, piece in enumerate(pieces):
        g_in, delta_in, dq_in = inputs[3 * at : 3 * at + 3]
        base = runs * (runs + 1) // 2 * HD
        for run in reversed(range(runs)):
            keys = (run + 1) * HD
            base -= keys
            g_l, qn_run = g_in[run], qn[piece, run]
            e = e_own[piece, base : base + keys, :]
            dp = jnp.dot(v_own[piece, :keys, :], g_l, preferred_element_type=f32)
            ds = (e.astype(f32) * (dp - delta_in[run])).astype(b16)
            dv = lax.dot_general(e, g_l, nt, preferred_element_type=f32)
            dk = lax.dot_general(ds, qn_run, nt, preferred_element_type=f32)
            dv_s[:keys, :] = dv if run == runs - 1 else dv_s[:keys, :] + dv
            dk_s[:keys, :] = dk if run == runs - 1 else dk_s[:keys, :] + dk
            dq = dq_in[run] + jnp.dot(kt_own[piece, :, :keys], ds, preferred_element_type=f32)
            q = qt[piece, run].astype(f32)
            r = inverse_rms(q, 0)
            scaled = dq * gain
            dq = r * scaled - q * (r * r * r * jnp.mean(q * scaled, axis=0, keepdims=True))
            slot, inside = divmod(run * HD, rows)
            for head in range(wide // HD):
                lanes = slice(head * HD, (head + 1) * HD)
                columns = slice(at * wide + head * HD, at * wide + (head + 1) * HD)
                dq_s[slot, inside : inside + HD, columns] = dq[:, lanes].T.astype(b16)
        for part in range(2):
            tokens = pl.ds(pl.multiple_of((core if part == 0 else 1 - core) * rows, rows), rows)
            if places:
                swapped, returned = ends[2 * at : 2 * at + 2]
                columns = slice(at * HD, (at + 1) * HD)
                for which, sums in enumerate((dk_s, dv_s)):
                    span = slice(which * rows, (which + 1) * rows)
                    total = key_sum(
                        even, sums[tokens, :], swapped[part, span], returned[places[at], part, span]
                    )
                    outs[part][span, columns] = total.astype(b16)
            else:
                outs[at][part, :rows] = dk_s[tokens, :]
                outs[at][part, rows:] = dv_s[tokens, :]
    dq_m[...] = dq_s[core]
    dq_t[...] = dq_s[1 - core]


def own_keys(pieces, meta, q_gain, prepared, results, ends):
    qt, qn, k_own, kt_own, v_own, e_own = prepared
    rows = k_own.shape[1] // 2
    columns = len(pieces) * qt.shape[-1]
    f32, b16 = jnp.float32, jnp.bfloat16
    vmem = pl.BlockSpec(memory_space=pltpu.VMEM)
    dq = jax.ShapeDtypeStruct((rows, columns), b16)
    own = jax.ShapeDtypeStruct((2, 2 * rows, HD), f32)
    final = jax.ShapeDtypeStruct((2 * rows, len(pieces) * HD), b16)
    flat = [one for result in results for one in result]
    flat += [one for swapped, back in ends for one in (swapped, back[0])]
    places = tuple(back[1] for swapped, back in ends)
    outs = [dq, dq] + ([final] * 2 if ends else [own] * len(pieces))
    return pl.pallas_call(
        functools.partial(own_kernel, tuple(range(len(pieces))), places, rows),
        in_specs=[pl.BlockSpec(memory_space=pltpu.SMEM)] + [vmem] * (7 + len(flat)),
        out_specs=[vmem] * len(outs),
        scratch_shapes=[
            pltpu.VMEM((2, rows, columns), b16),
            pltpu.VMEM((2 * rows, HD), f32),
            pltpu.VMEM((2 * rows, HD), f32),
        ],
        out_shape=outs,
        compiler_params=pltpu.CompilerParams(vmem_limit_bytes=VMEM_LIMIT),
        cost_estimate=pl.CostEstimate(flops=2**32, bytes_accessed=2**22, transcendentals=0),
        name=f"own_{pieces[0]}",
    )(meta, q_gain, *prepared, *flat)


def finish_kernel(places, meta, *refs):
    outs = refs[3 * len(places) :]
    for at, at_returned in enumerate(places):
        own, swapped, returned = refs[3 * at : 3 * at + 3]
        for part in range(2):
            total = key_sum(meta[1] == 0, own[part], swapped[part], returned[at_returned, part])
            outs[part][:, at * HD : (at + 1) * HD] = total.astype(outs[part].dtype)


def finish(meta, owns, ends):
    vmem = pl.BlockSpec(memory_space=pltpu.VMEM)
    shape = jax.ShapeDtypeStruct((owns[0].shape[1], len(owns) * HD), jnp.bfloat16)
    flat = []
    for own, (swapped, back) in zip(owns, ends):
        flat += [own, swapped, back[0]]
    places = tuple(back[1] for swapped, back in ends)
    return pl.pallas_call(
        functools.partial(finish_kernel, places),
        in_specs=[pl.BlockSpec(memory_space=pltpu.SMEM)] + [vmem] * len(flat),
        out_specs=[vmem, vmem],
        out_shape=[shape, shape],
        compiler_params=pltpu.CompilerParams(vmem_limit_bytes=VMEM_LIMIT),
        cost_estimate=SMALL,
        name="finish",
    )(meta, *flat)


def join_query_kernel(count, *refs):
    core = lax.rem(lax.axis_index("ctx"), 2)
    out, sem = refs[2 * count], refs[-1]
    copies = []
    for parts, who in ((refs[:count], core), (refs[count : 2 * count], 1 - core)):
        at = 0
        for part in parts:
            width = part.shape[1]
            columns = pl.ds(pl.multiple_of(who * (out.shape[1] // 2) + at, HD), width)
            copies.append(pltpu.make_async_copy(part, out.at[:, columns], sem.at[len(copies)]))
            at += width
    for copy in copies:
        copy.start()
    for copy in copies:
        copy.wait()


def join_query(mine, theirs):
    width = 2 * sum(part.shape[1] for part in mine)
    vmem = pl.BlockSpec(memory_space=pltpu.VMEM)
    return pl.pallas_call(
        functools.partial(join_query_kernel, len(mine)),
        in_specs=[vmem] * (2 * len(mine)),
        out_specs=pl.BlockSpec(memory_space=pltpu.HBM),
        out_shape=jax.ShapeDtypeStruct((mine[0].shape[0], width), mine[0].dtype),
        scratch_shapes=[pltpu.SemaphoreType.DMA((2 * len(mine),))],
        compiler_params=pltpu.CompilerParams(vmem_limit_bytes=VMEM_LIMIT),
        cost_estimate=SMALL,
        name="join_query",
    )(*mine, *theirs)


def join_key_kernel(count, rows, k_gain, keys, *refs):
    f32 = jnp.float32
    core = lax.rem(lax.axis_index("ctx"), 2)
    key_out, value_out, grads, sem = refs[2 * count :]
    half = key_out.shape[1] // 2
    places, copies = [], []
    for parts, who in ((refs[:count], core), (refs[count : 2 * count], 1 - core)):
        at = 0
        for part in parts:
            columns = pl.ds(pl.multiple_of(who * half + at, HD), part.shape[1])
            copies.append(
                pltpu.make_async_copy(
                    part.at[pl.ds(rows, rows)], value_out.at[:, columns], sem.at[len(copies)]
                )
            )
            copies[-1].start()
            for head in range(part.shape[1] // HD):
                places.append((part, head, who * half + at))
                at += HD
    for index, (part, head, begin) in enumerate(places):
        columns = pl.ds(pl.multiple_of(begin, HD), HD)
        k = keys[:, columns].astype(f32)
        r = inverse_rms(k, -1)
        scaled = part[:rows, head * HD : (head + 1) * HD].astype(f32) * k_gain[...]
        grad = r * scaled - k * (r * r * r * jnp.mean(k * scaled, axis=-1, keepdims=True))
        grads[index] = grad.astype(grads.dtype)
        copies.append(
            pltpu.make_async_copy(grads.at[index], key_out.at[:, columns], sem.at[len(copies)])
        )
        copies[-1].start()
    for copy in copies:
        copy.wait()


def join_key(k_gain, keys, mine, theirs):
    rows, width = keys.shape
    vmem = pl.BlockSpec(memory_space=pltpu.VMEM)
    out = jax.ShapeDtypeStruct((rows, width), keys.dtype)
    return pl.pallas_call(
        functools.partial(join_key_kernel, len(mine), rows),
        in_specs=[vmem] * (2 + 2 * len(mine)),
        out_specs=[pl.BlockSpec(memory_space=pltpu.HBM)] * 2,
        out_shape=[out, out],
        scratch_shapes=[
            pltpu.VMEM((width // HD, rows, HD), keys.dtype),
            pltpu.SemaphoreType.DMA((width // HD + 2 * len(mine),)),
        ],
        compiler_params=pltpu.CompilerParams(vmem_limit_bytes=VMEM_LIMIT),
        cost_estimate=SMALL,
        name="join_key",
    )(k_gain, keys, *mine, *theirs)


def lay_kernel(kv_m, kv_t, *outs):
    place = [(out, at) for out in outs for at in range(out.shape[0])]
    for part, kv in enumerate((kv_m, kv_t)):
        for head, (out, at) in enumerate(place):
            out[at, part] = kv[:, head * HD : (head + 1) * HD]


def lay(kv_m, kv_t):
    shape = lambda count: jax.ShapeDtypeStruct((count, 2, kv_m.shape[0], HD), kv_m.dtype)
    vmem = pl.BlockSpec(memory_space=pltpu.VMEM)
    return pl.pallas_call(
        lay_kernel,
        in_specs=[vmem, vmem],
        out_specs=[vmem] * (kv_m.shape[1] // HD),
        out_shape=[shape(1)] * (kv_m.shape[1] // HD),
        compiler_params=pltpu.CompilerParams(vmem_limit_bytes=VMEM_LIMIT),
        cost_estimate=SMALL,
        name="lay",
    )(kv_m, kv_t)


def after(value, *others):
    return lax.optimization_barrier((value,) + others)[0]


def on_device(queries, keys, values, out_grad, q_gain, k_gain, doc_ids):
    f32, b16 = jnp.float32, jnp.bfloat16
    rows = queries.shape[0]
    half = keys.shape[1] // 2
    pieces = half // HD
    count = lax.axis_size("ctx")
    if WINDOW != 4 * rows or count % 4 != 0:
        raise ValueError("unsupported split")
    rank = lax.axis_index("ctx")
    core = lax.rem(rank, 2)
    parity = lax.rem(lax.div(rank, 2), 2)
    odd = parity == 1
    meta = jnp.stack([core, parity]).astype(jnp.int32)

    core_swap = [(i, i ^ 1) for i in range(count)]
    x_swap = [(i, i ^ 2) for i in range(count)]
    ahead = [(i, i + 4) for i in range(count - 4)]
    back = [(i + 4, i) for i in range(count - 4)]

    def half_of(array, who):
        width = array.shape[1] // 2
        return lax.dynamic_slice(array, (0, who * width), (rows, width))

    def both(one, two, who):
        return jnp.stack([half_of(one, who), half_of(two, who)])

    id_rows = jnp.pad((doc_ids + 1).astype(b16), (0, ID_ROWS - doc_ids.shape[0]))
    id_rows = jnp.broadcast_to(id_rows[:, None], (ID_ROWS, half))

    def pack(who):
        return jnp.concatenate([half_of(keys, who), half_of(values, who), id_rows])

    kv_t = lax.ppermute(pack(1 - core), "ctx", core_swap)
    kv_m = pack(core)

    kv0 = lay(kv_m, kv_t)
    kv1, kv2 = [], []
    for block in kv0[:-1]:
        kv2.append((lax.ppermute(block, "ctx", ahead), 0))
    neighbour = lax.ppermute(kv0[-1], "ctx", x_swap)
    qg_m = both(queries, out_grad, core)
    qg_t = lax.ppermute(both(queries, out_grad, 1 - core), "ctx", core_swap)

    q_gain_row = q_gain.reshape(1, HD)
    k_gain_row = k_gain.reshape(1, HD)
    swapped, joined, returned, results, sums_h2 = [], [], [], [], []

    def x_hop(piece, turn):
        operand = jnp.where(turn, kv2[piece][0][0], kv0[piece][0])
        kv1.append(lax.ppermute(operand, "ctx", x_swap))
        return operand

    def far_hop(turn):
        theirs = after(neighbour, turn)
        block = jnp.concatenate([kv0[-1], theirs])
        moved = lax.ppermute(block, "ctx", ahead)
        kv2.append((moved, 0))
        kv1.append(jnp.where(odd, theirs[0], moved[1]))
        return block

    def send_back(group, turn):
        block = []
        for piece in group:
            arrived = jnp.where(turn, swapped[piece].astype(f32), 0.0)
            block.append((sums_h2[piece].astype(f32) + arrived).astype(b16))
        joined.append(jnp.stack(block))
        moved = lax.ppermute(joined[-1], "ctx", back)
        returned.extend((moved, at) for at in range(len(group)))

    hop_0 = x_hop(0, odd)
    middle = pieces // 2
    local_part = lambda begin, order: local(
        begin, middle, order, qg_m, qg_t, kv_m, kv_t, q_gain_row, k_gain_row
    )
    prepared = [local_part(0, after(meta, hop_0, neighbour))]
    order = after(meta, x_hop(1, after(odd, prepared[0][7])))
    for piece in range(pieces):
        if piece == middle:
            prepared.append(local_part(middle, order))
        _, qn, gt, *_, total_own, out_own, doc_own = prepared[piece // middle]
        h1, h2, *result = halo(
            piece % middle, order, qn, gt, total_own, out_own, doc_own, kv1[piece], kv2[piece], k_gain_row
        )
        results.append(result)
        order = after(order, result[1])
        if piece + 3 < pieces:
            order = after(order, x_hop(piece + 2, after(odd, result[1])), far_hop(result[1]))
        swapped.append(lax.ppermute(h1, "ctx", x_swap))
        sums_h2.append(h2)
        if piece == 2:
            send_back((0, 1), after(odd, result[1]))
            order = after(order, joined[-1])
        elif piece > 2:
            send_back((piece - 1,), after(odd, result[1]))

    ends = lambda group: [(swapped[i], returned[i]) for i in group]
    late, soon = list(range(middle, pieces)), list(range(middle))

    def own_part(group, order, ends):
        qt, qn, _, k_own, kt_own, v_own, e_own, *_ = prepared[group[0] // middle]
        return own_keys(
            group, order, q_gain_row, (qt, qn, k_own, kt_own, v_own, e_own),
            [results[i] for i in group], ends,
        )

    order = after(order, joined[-1])
    dq_m_late, dq_t_late, *own_late = own_part(late, order, [])
    send_back((pieces - 1,), after(odd, dq_m_late))
    order = after(order, joined[-1], returned[0][0], returned[2][0])
    dq_m_soon, dq_t_soon, kv_m_soon, kv_t_soon = own_part(soon, order, ends(soon))
    swap = lambda array: lax.ppermute(array, "ctx", core_swap)
    query_grad = join_query([dq_m_soon, dq_m_late], [swap(dq_t_soon), swap(dq_t_late)])
    kv_m_late, kv_t_late = finish(order, own_late, ends(late))
    key_grad, value_grad = join_key(
        k_gain_row, keys, [kv_m_soon, kv_m_late], [swap(kv_t_soon), swap(kv_t_late)]
    )
    return (query_grad, key_grad, value_grad)


def solution(mesh):
    split = P(("groups", "ctx"), None)
    in_specs = (split, split, split, split, P(), P(), P(("groups", "ctx")))
    return jax.shard_map(
        on_device, mesh=mesh, in_specs=in_specs, out_specs=(split, split, split), check_vma=False
    )
```
